128 devices in a mesh: dp: 8 (over z, core), cent: 16 (over x, y).
Axes of the slice: x: 4, y: 4, z: 4, core: 2. Of those that a mesh axis runs over, the one named last changes fastest.
Arguments:
- embeddings: bfloat16 [32768, 1024], P(('dp', 'cent')), may hold values from -6 to 6
- codebook: float32 [16384, 1024], P(('cent', 'dp')), may hold values from -2 to 2
Outputs:
- new_codebook: float32 [16384, 1024], P(('cent', 'dp'))
- counts: float32 [16384], P(('cent', 'dp'))
- log_norm: float32 [32768], P(('dp', 'cent'))
The draws below stay inside these ranges and needn't reach their ends.
All inputs are finite; a program needn't handle non-finite values.
Results may differ from the reference program's by a relative error of at most 0.0022.
Values may be sent and summed in bfloat16 or wider, within the bound.
A program may use at most 128 MiB of HBM per device.

```python
import jax
import jax.numpy as jnp
from jax import lax

D = 1024
ROWS_DEV = 256
N = 32768
K = 16384
N_CENT = 16


def anchor_rows(key):
    first, second = jax.random.split(key)
    signs = jnp.where(jax.random.bernoulli(first, 0.5, (8, D)), 1.0, -1.0)
    sizes = jax.random.uniform(second, (8, D), jnp.float32, 0.8, 1.2)
    sizes = sizes.at[:, 0].set(1.0)
    return signs * sizes


def anchor_strengths():
    return 2.5 + 2.0 / 7.0 * jnp.arange(8, dtype=jnp.float32)


def draw_embeddings(key, part):
    anchors = anchor_rows(key)
    key = jax.random.fold_in(key, 11)
    values = jnp.clip(jax.random.normal(key, (N, D), jnp.float32), -6.0, 6.0)
    places = jnp.arange(8, dtype=jnp.int32) * (N // 8)
    values = values.at[places].set(anchor_strengths()[:, None] * anchors)
    return values.astype(jnp.bfloat16)


def draw_codebook(key, part):
    anchors = anchor_rows(key)
    key = jax.random.fold_in(key, 23)
    values = 0.05 * jnp.clip(jax.random.normal(key, (K, D), jnp.float32), -6.0, 6.0)
    places = jnp.arange(8, dtype=jnp.int32) * (K // 8)
    scaled = 1.5 * anchors
    halved = scaled.at[:, 0].set(0.5 * scaled[:, 0])
    values = values.at[places].set(scaled)
    values = values.at[places + 1].set(halved)
    return values


def setup_inputs(seed: int = 0) -> dict:
    streams_of = jax.random.split(jax.random.key(seed), 3)
    return {
        "embeddings": draw_embeddings(jax.random.fold_in(streams_of[2], 71), 0),
        "codebook": draw_codebook(jax.random.fold_in(streams_of[2], 71), 0),
    }


TEMPER = 0.8
PRIOR = 1.0


def score_block(rows, centers, squares):
    product = jnp.dot(rows, centers.T, preferred_element_type=jnp.float32)
    return (product - 0.5 * squares[None, :]) / TEMPER


def reference(embeddings, codebook):
    centers = codebook.astype(jnp.bfloat16)
    squares = jnp.sum(jnp.square(centers.astype(jnp.float32)), axis=1)
    blocks = embeddings.reshape(-1, ROWS_DEV * N_CENT, D)

    def step(carry, rows):
        scores = score_block(rows, centers, squares)
        highest = jnp.max(scores, axis=1)
        lognorm = highest + jnp.log(jnp.sum(jnp.exp(scores - highest[:, None]), axis=1))
        resp = jnp.exp(scores - lognorm[:, None]).astype(jnp.bfloat16)
        sums = carry[0] + lax.dot_general(resp, rows, (((0,), (0,)), ((), ())), preferred_element_type=jnp.float32)
        tally = carry[1] + jnp.sum(resp.astype(jnp.float32), axis=0)
        return (sums, tally), lognorm

    start = (jnp.zeros((K, D), jnp.float32), jnp.zeros((K,), jnp.float32))
    (sums, tally), lognorm = lax.scan(step, start, blocks)
    new_codebook = (sums + PRIOR * codebook) / (tally + PRIOR)[:, None]
    return new_codebook, tally, lognorm.reshape(-1)
```

```python
import functools
import math

import jax
import jax.numpy as jnp
from jax import lax
from jax.experimental import pallas as pl
from jax.experimental.pallas import tpu as pltpu
from jax.sharding import PartitionSpec as P

TEMPER = 0.8
PRIOR = 1.0
ALPHA = math.log2(math.e) / TEMPER
LN2 = math.log(2.0)
MESH = pl.DeviceIdType.MESH

ROWS, CENTS, WIDTH = 256, 128, 1024
BLOCK = 2 * ROWS
ROW_THIRDS = ((0, 96), (96, 80), (176, 80))
CENT_THIRDS = ((0, 48), (48, 48), (96, 32))
PLACE = {0: 0, 1: 1, 2: 2, 4: 3, 3: 4, 5: 5, 6: 6, 7: 7}
NT = (((1,), (1,)), ((), ()))
NN = (((1,), (0,)), ((), ()))


def waves():
    bit = lambda d: 1 << (d % 3)
    return (
        [(d, d, 0) for d in range(3)],
        [(d, (d - 1) % 3, 0) for d in range(3)],
        [(d, (d - 2) % 3, 0) for d in range(3)],
        [(d, (d - 1) % 3, bit(d - 1)) for d in range(3)],
        [(d, (d - 2) % 3, bit(d - 2)) for d in range(3)],
        [(d, (d - 2) % 3, bit(d - 1)) for d in range(3)],
        [(d, (d - 2) % 3, bit(d - 1) | bit(d - 2)) for d in range(3)],
    )


def combine(terms):
    top = functools.reduce(jnp.maximum, terms)
    total = functools.reduce(jnp.add, [jnp.exp2(t - top) for t in terms])
    return top + jnp.log2(total)


def kernel(
    emb, book, new_out, count_out, norm_out,
    rows, cents, scores, half_sq, peak, sums, tally, lse_all,
    lse_mine, lse_in, part_mine, part_in, fin_in, count_mine, count_in,
    outbox, inbox1, inbox2, inbox3,
    own_sem, row_send, row_recv, sib_send, sib_recv, cent_send, cent_recv,
    stat_send, stat_recv, part_send, part_recv, fin_send, fin_recv,
    count_send, count_recv, sum_send, sum_recv,
):
    dp, cent = lax.axis_index("dp"), lax.axis_index("cent")
    place = (cent // 4, cent % 4, dp // 2)
    core = dp % 2

    def device(p, c):
        return (p[2] * 2 + c, p[0] * 4 + p[1])

    def row_peer(mask, other=0):
        p = [v + 1 - 2 * (v % 2) if mask >> d & 1 else v for d, v in enumerate(place)]
        return device(p, 1 - core if other else core)

    def cent_peer(mask):
        return device([3 - v if mask >> d & 1 else v for d, v in enumerate(place)], core)

    def slot_peer(a):
        return row_peer(a >> 1, a & 1)

    def remote(src, dst, send, recv, to):
        return pltpu.make_async_remote_copy(
            src_ref=src, dst_ref=dst, send_sem=send, recv_sem=recv,
            device_id=to, device_id_type=MESH,
        )

    barrier = pltpu.get_barrier_semaphore()
    peers = [slot_peer(a) for a in range(1, 16)] + [cent_peer(n) for n in range(1, 8)]
    for peer in peers:
        pl.semaphore_signal(barrier, inc=1, device_id=peer, device_id_type=MESH)
    own = pltpu.make_async_copy(emb, rows.at[pl.ds(0, ROWS)], own_sem)
    own.start()
    cents[0:CENTS, :] = book[...].astype(jnp.bfloat16)
    pl.semaphore_wait(barrier, len(peers))

    def row_copy(d, j, m):
        off, size = ROW_THIRDS[j]
        n = m | 1 << d
        dst = rows.at[pl.ds(n * BLOCK + off, size)]
        src = emb.at[pl.ds(off, size)] if m == 0 else rows.at[pl.ds(m * BLOCK + off, size)]
        return remote(src, dst, row_send.at[n, j], row_recv.at[n, j], row_peer(1 << d))

    def cent_copy(d, j, m):
        off, size = CENT_THIRDS[j]
        n = m | 1 << d
        src = cents.at[pl.ds(PLACE[m] * CENTS + off, size)]
        dst = cents.at[pl.ds(PLACE[n] * CENTS + off, size)]
        return remote(src, dst, cent_send.at[n, j], cent_recv.at[n, j], cent_peer(1 << d))

    def sib_copy(n, j):
        off, size = ROW_THIRDS[j]
        src = emb.at[pl.ds(off, size)] if n == 0 else rows.at[pl.ds(n * BLOCK + off, size)]
        dst = rows.at[pl.ds(n * BLOCK + ROWS + off, size)]
        return remote(src, dst, sib_send.at[n, j], sib_recv.at[n, j], row_peer(0, 1))

    wave = waves()

    def row_start(w):
        for msg in wave[w]:
            row_copy(*msg).start()

    def cent_start(w):
        for msg in wave[w]:
            cent_copy(*msg).start()

    def row_arrive(w):
        for d, j, m in wave[w]:
            row_copy(d, j, m).wait_recv()
            sib_copy(m | 1 << d, j).start()

    def cent_arrive(w):
        for msg in wave[w]:
            cent_copy(*msg).wait_recv()

    def sib_arrive(n):
        for j in range(3):
            sib_copy(n, j).wait_recv()

    def squares(half):
        @pl.loop(0, 4)
        def _(i):
            at = pl.ds(pl.multiple_of(half * 512 + i * CENTS, CENTS), CENTS)
            c = cents[at, :].astype(jnp.float32)
            total = jnp.sum(c * c, axis=1, keepdims=True) * (0.5 * ALPHA)
            half_sq[at, :] = jnp.broadcast_to(total, (CENTS, 128))

    def score(n, half):
        if half == 0:
            peak[n] = jnp.full((8, BLOCK), -jnp.inf, jnp.float32)

        @pl.loop(0, 2)
        def _(i):
            at = pl.ds(pl.multiple_of(half * 512 + i * 256, 256), 256)
            product = lax.dot_general(
                cents[at, :], rows[n * BLOCK : (n + 1) * BLOCK, :], NT,
                preferred_element_type=jnp.float32,
            )
            h = half_sq[at, :]
            t = product * ALPHA - jnp.concatenate([h] * (BLOCK // 128), axis=1)
            scores[at, n * BLOCK : (n + 1) * BLOCK] = t
            peak[n] = jnp.maximum(peak[n], jnp.max(t.reshape(32, 8, BLOCK), axis=0))

    def soften(n):
        top = jnp.max(peak[n], axis=0, keepdims=True)

        def body(i, total):
            at = pl.ds(pl.multiple_of(i * 256, 256), 256)
            e = jnp.exp2(scores[at, n * BLOCK : (n + 1) * BLOCK] - top)
            return total + jnp.sum(e.reshape(32, 8, BLOCK), axis=0)

        total = lax.fori_loop(0, 4, body, jnp.zeros((8, BLOCK), jnp.float32))
        lse = top + jnp.log2(jnp.sum(total, axis=0, keepdims=True))
        lse_mine[2 * n] = lse[:, :ROWS]
        lse_mine[2 * n + 1] = lse[:, ROWS:]

    def stat_copy(a):
        return remote(lse_mine.at[a], lse_in.at[a], stat_send.at[a], stat_recv, slot_peer(a))

    def part_copy(a):
        return remote(part_mine, part_in.at[a], part_send.at[a], part_recv, slot_peer(a))

    def fin_copy(a):
        return remote(
            lse_mine.at[pl.ds(12, 4)], fin_in.at[a], fin_send.at[a], fin_recv, slot_peer(a)
        )

    def count_copy(n):
        return remote(count_mine.at[n], count_in.at[n], count_send.at[n], count_recv, cent_peer(n))

    def wait_all(ref, sem):
        remote(ref, ref, own_sem, sem, row_peer(0, 1)).wait_recv()

    cent_start(0)
    row_start(0)
    cent_start(1)
    row_start(1)
    cent_start(2)
    row_start(2)
    for j in range(3):
        sib_copy(0, j).start()
    cent_arrive(0)
    cent_start(3)
    cent_start(4)
    row_arrive(0)
    row_start(3)
    row_start(4)
    cent_arrive(1)
    cent_start(5)
    cent_arrive(2)
    own.wait()
    sib_arrive(0)
    squares(0)
    score(0, 0)
    row_arrive(1)
    row_start(5)
    cent_arrive(3)
    cent_start(6)
    row_arrive(2)
    for n in (1, 2, 4):
        sib_arrive(n)
        score(n, 0)
    cent_arrive(4)
    cent_arrive(5)
    cent_arrive(6)
    squares(1)

    def finish(n):
        score(n, 1)
        soften(n)
        if n < 6:
            for a in (2 * n, 2 * n + 1):
                if a:
                    stat_copy(a).start()

    finish(0)
    row_arrive(3)
    row_start(6)
    finish(1)
    finish(2)
    row_arrive(4)
    finish(4)
    row_arrive(5)
    for n in (3, 5):
        sib_arrive(n)
        score(n, 0)
        finish(n)
    sib_arrive(6)
    score(6, 0)
    finish(6)
    row_arrive(6)
    sib_arrive(7)
    score(7, 0)
    score(7, 1)
    wait_all(lse_in.at[pl.ds(1, 11)], stat_recv)
    part = combine([lse_mine[0]] + [lse_in[a] for a in range(1, 12)])
    part_mine[...] = part
    for a in range(1, 16):
        part_copy(a).start()
    soften(7)
    for a in range(1, 16):
        fin_copy(a).start()
    wait_all(part_in.at[pl.ds(1, 15)], part_recv)
    wait_all(fin_in.at[pl.ds(1, 15)], fin_recv)
    for s in range(16):
        terms = [part_mine[...] if s == 0 else part_in[s]]
        for q in range(12, 16):
            terms.append(lse_mine[q] if s == q else fin_in[s ^ q, q - 12])
        lse = combine(terms)
        lse_all[:, s * ROWS : (s + 1) * ROWS] = lse
        if s == 0:
            norm_out[...] = lse * LN2

    def weigh(n):
        at = PLACE[n] * CENTS
        sums[n] = jnp.zeros((CENTS, WIDTH), jnp.float32)
        tally[...] = jnp.zeros((CENTS, 128), jnp.float32)

        @pl.loop(0, 8)
        def _(r):
            cols = pl.ds(pl.multiple_of(r * BLOCK, BLOCK), BLOCK)
            resp = jnp.exp2(scores[at : at + CENTS, cols] - lse_all[:, cols]).astype(jnp.bfloat16)
            wide = resp.astype(jnp.float32)
            tally[...] += functools.reduce(
                jnp.add, [wide[:, q * 128 : (q + 1) * 128] for q in range(BLOCK // 128)]
            )
            sums[n] += lax.dot_general(resp, rows[cols, :], NN, preferred_element_type=jnp.float32)

        count_mine[n] = jnp.sum(tally[...].T, axis=0, keepdims=True)
        if n:
            count_copy(n).start()

    def step_of(n, j):
        return next(s for s in range(3) if n >> (j + s) % 3 & 1)

    def sum_copy(n, j):
        off, size = CENT_THIRDS[j]
        s = step_of(n, j)
        d = (j + s) % 3
        to = n ^ 1 << d
        box = (inbox1, inbox2, inbox3)[s]
        dst = box.at[0 if s == 2 else to, pl.ds(off, size)]
        return remote(
            outbox.at[n, pl.ds(off, size)], dst, sum_send.at[n, j], sum_recv.at[n, j],
            cent_peer(1 << d),
        )

    def gathered(n, j):
        off, size = CENT_THIRDS[j]
        value = sums[n, off : off + size, :]
        for s in range(step_of(n, j) if n else 3):
            came = n | 1 << (j + s) % 3
            sum_copy(came, j).wait_recv()
            box = (inbox1, inbox2, inbox3)[s]
            value = value + box[0 if s == 2 else n, off : off + size, :].astype(jnp.float32)
        return value

    def send_sums(n, step):
        for j in range(3):
            if step_of(n, j) == step:
                off, size = CENT_THIRDS[j]
                outbox[n, off : off + size, :] = gathered(n, j).astype(jnp.bfloat16)
                sum_copy(n, j).start()

    for n in (7, 3, 6, 5):
        weigh(n)
        send_sums(n, 0)
    for n in (3, 6, 5):
        send_sums(n, 1)
    for n in (1, 2, 4):
        weigh(n)
        send_sums(n, 0)
    for n in (1, 2, 4):
        send_sums(n, 1)
    weigh(0)
    for n in (1, 2, 4):
        send_sums(n, 2)

    for w in range(7):
        for msg in wave[w]:
            row_copy(*msg).wait_send()
            cent_copy(*msg).wait_send()
    for n in range(8):
        for j in range(3):
            sib_copy(n, j).wait_send()
    for a in range(1, 16):
        if a < 12:
            stat_copy(a).wait_send()
        part_copy(a).wait_send()
        fin_copy(a).wait_send()
    wait_all(count_in.at[pl.ds(1, 7)], count_recv)
    count = functools.reduce(jnp.add, [count_mine[0]] + [count_in[n] for n in range(1, 8)])
    count_out[...] = count
    below = jnp.broadcast_to(count, (CENTS, 128)).T + PRIOR
    for j in range(3):
        off, size = CENT_THIRDS[j]
        top = gathered(0, j) + PRIOR * book[off : off + size, :]
        for q in range(WIDTH // 128):
            cols = slice(q * 128, (q + 1) * 128)
            new_out[off : off + size, cols] = top[:, cols] / below[off : off + size, :]
    for n in range(1, 8):
        count_copy(n).wait_send()
        for j in range(3):
            sum_copy(n, j).wait_send()


def local(embeddings, codebook):
    f32, bf16 = jnp.float32, jnp.bfloat16
    vmem, dma = pltpu.VMEM, pltpu.SemaphoreType.DMA
    new, count, norm = pl.pallas_call(
        kernel,
        out_shape=(
            jax.ShapeDtypeStruct((CENTS, WIDTH), f32),
            jax.ShapeDtypeStruct((1, CENTS), f32),
            jax.ShapeDtypeStruct((1, ROWS), f32),
        ),
        in_specs=[pl.BlockSpec(memory_space=pl.ANY), pl.BlockSpec(memory_space=pltpu.VMEM)],
        out_specs=[pl.BlockSpec(memory_space=pltpu.VMEM)] * 3,
        scratch_shapes=[
            vmem((8 * BLOCK, WIDTH), bf16),
            vmem((8 * CENTS, WIDTH), bf16),
            vmem((8 * CENTS, 8 * BLOCK), f32),
            vmem((8 * CENTS, 128), f32),
            vmem((8, 8, BLOCK), f32),
            vmem((8, CENTS, WIDTH), f32),
            vmem((CENTS, 128), f32),
            vmem((1, 8 * BLOCK), f32),
            vmem((16, 1, ROWS), f32),
            vmem((16, 1, ROWS), f32),
            vmem((1, ROWS), f32),
            vmem((16, 1, ROWS), f32),
            vmem((16, 4, 1, ROWS), f32),
            vmem((8, 1, CENTS), f32),
            vmem((8, 1, CENTS), f32),
            vmem((8, CENTS, WIDTH), bf16),
            vmem((8, CENTS, WIDTH), bf16),
            vmem((8, CENTS, WIDTH), bf16),
            vmem((1, CENTS, WIDTH), bf16),
            dma(()),
            dma((8, 3)), dma((8, 3)),
            dma((8, 3)), dma((8, 3)),
            dma((8, 3)), dma((8, 3)),
            dma((16,)), dma(()),
            dma((16,)), dma(()),
            dma((16,)), dma(()),
            dma((8,)), dma(()),
            dma((8, 3)), dma((8, 3)),
        ],
        compiler_params=pltpu.CompilerParams(
            collective_id=0, has_side_effects=True, vmem_limit_bytes=58 * 2**20
        ),
        cost_estimate=pl.CostEstimate(
            flops=4 * 4096 * 1024 * 1024, bytes_accessed=2**21, transcendentals=2**23
        ),
    )(embeddings, codebook)
    return new, count.reshape(CENTS), norm.reshape(ROWS)


def solution(mesh):
    return jax.shard_map(
        local,
        mesh=mesh,
        in_specs=(P(("dp", "cent"), None), P(("cent", "dp"), None)),
        out_specs=(P(("cent", "dp"), None), P(("cent", "dp")), P(("dp", "cent"))),
        check_vma=False,
    )
```

```python
import functools
import math

import jax
import jax.numpy as jnp
from jax import lax
from jax.experimental import pallas as pl
from jax.experimental.pallas import tpu as pltpu
from jax.sharding import PartitionSpec as P

TEMPER = 0.8
PRIOR = 1.0
ALPHA = math.log2(math.e) / TEMPER
LN2 = math.log(2.0)
MESH = pl.DeviceIdType.MESH

ROWS, CENTS, WIDTH = 256, 128, 1024
BLOCK = 2 * ROWS
ROW_THIRDS = ((0, 96), (96, 80), (176, 80))
CENT_THIRDS = ((0, 48), (48, 48), (96, 32))
ORDER = (0, 1, 2, 4, 3, 5, 6, 7)
PLACE = {mask: i for i, mask in enumerate(ORDER)}
NT = (((1,), (1,)), ((), ()))
NN = (((1,), (0,)), ((), ()))


def waves():
    bit = lambda d: 1 << (d % 3)
    return (
        [(d, d, 0) for d in range(3)],
        [(d, (d - 1) % 3, 0) for d in range(3)],
        [(d, (d - 2) % 3, 0) for d in range(3)],
        [(d, (d - 1) % 3, bit(d - 1)) for d in range(3)],
        [(d, (d - 2) % 3, bit(d - 2)) for d in range(3)],
        [(d, (d - 2) % 3, bit(d - 1)) for d in range(3)],
        [(d, (d - 2) % 3, bit(d - 1) | bit(d - 2)) for d in range(3)],
    )


def combine(terms):
    top = functools.reduce(jnp.maximum, terms)
    total = functools.reduce(jnp.add, [jnp.exp2(t - top) for t in terms])
    return top + jnp.log2(total)


def kernel(
    emb, book, new_out, count_out, norm_out,
    rows, cents, scores, half_sq, peak, sums, tally, lse_all,
    lse_mine, lse_in, part_mine, part_in, fin_in, count_mine, count_in,
    outbox, inbox1, inbox2, inbox3,
    own_sem, row_send, row_recv, sib_send, sib_recv, cent_send, cent_recv,
    stat_send, stat_recv, part_send, part_recv, fin_send, fin_recv,
    count_send, count_recv, sum_send, sum_recv,
):
    dp, cent = lax.axis_index("dp"), lax.axis_index("cent")
    place = (cent // 4, cent % 4, dp // 2)
    core = dp % 2

    def device(p, c):
        return (p[2] * 2 + c, p[0] * 4 + p[1])

    def row_peer(mask, other=0):
        p = [v + 1 - 2 * (v % 2) if mask >> d & 1 else v for d, v in enumerate(place)]
        return device(p, 1 - core if other else core)

    def cent_peer(mask):
        return device([3 - v if mask >> d & 1 else v for d, v in enumerate(place)], core)

    def slot_peer(a):
        return row_peer(ORDER[a // 2], a % 2)

    def remote(src, dst, send, recv, to):
        return pltpu.make_async_remote_copy(
            src_ref=src, dst_ref=dst, send_sem=send, recv_sem=recv,
            device_id=to, device_id_type=MESH,
        )

    barrier = pltpu.get_barrier_semaphore()
    peers = [row_peer(0, 1)] + [row_peer(b) for b in (1, 2, 4)] + [cent_peer(b) for b in (1, 2, 4)]
    for peer in peers:
        pl.semaphore_signal(barrier, inc=1, device_id=peer, device_id_type=MESH)
    own = pltpu.make_async_copy(emb, rows.at[pl.ds(0, ROWS)], own_sem)
    own.start()
    cents[0:CENTS, :] = book[...].astype(jnp.bfloat16)
    pl.semaphore_wait(barrier, len(peers))

    def row_at(n, k, j):
        off, size = ROW_THIRDS[j]
        return pl.ds(PLACE[n] * BLOCK + k * ROWS + off, size)

    def cent_at(n, j):
        off, size = CENT_THIRDS[j]
        return pl.ds(PLACE[n] * CENTS + off, size)

    def row_copy(d, j, m):
        n = m | 1 << d
        src = emb.at[pl.ds(*ROW_THIRDS[j])] if m == 0 else rows.at[row_at(m, 0, j)]
        dst = rows.at[row_at(n, 0, j)]
        return remote(src, dst, row_send.at[n, j], row_recv.at[n, j], row_peer(1 << d))

    def cent_copy(d, j, m):
        n = m | 1 << d
        src, dst = cents.at[cent_at(m, j)], cents.at[cent_at(n, j)]
        return remote(src, dst, cent_send.at[n, j], cent_recv.at[n, j], cent_peer(1 << d))

    def sib_copy(n, j):
        src = emb.at[pl.ds(*ROW_THIRDS[j])] if n == 0 else rows.at[row_at(n, 0, j)]
        dst = rows.at[row_at(n, 1, j)]
        return remote(src, dst, sib_send.at[n, j], sib_recv.at[n, j], row_peer(0, 1))

    wave = waves()

    def row_start(w):
        for msg in wave[w]:
            row_copy(*msg).start()

    def cent_start(w):
        for msg in wave[w]:
            cent_copy(*msg).start()

    def row_arrive(w):
        for d, j, m in wave[w]:
            row_copy(d, j, m).wait_recv()
            sib_copy(m | 1 << d, j).start()

    def cent_arrive(w):
        for msg in wave[w]:
            cent_copy(*msg).wait_recv()

    def sib_arrive(n):
        for j in range(3):
            sib_copy(n, j).wait_recv()

    def squares(half):
        @pl.loop(0, 4)
        def _(i):
            at = pl.ds(pl.multiple_of(half * 512 + i * CENTS, CENTS), CENTS)
            c = cents[at, :].astype(jnp.float32)
            total = jnp.sum(c * c, axis=1, keepdims=True) * (0.5 * ALPHA)
            half_sq[at, :] = jnp.broadcast_to(total, (CENTS, 128))

    def score(p, half):
        cols = pl.ds(pl.multiple_of(p * BLOCK, BLOCK), BLOCK)
        top = jnp.where(half == 0, -jnp.inf, peak[p])
        for i in range(2):
            at = pl.ds(pl.multiple_of(half * 512 + i * 256, 256), 256)
            product = lax.dot_general(
                cents[at, :], rows[cols, :], NT, preferred_element_type=jnp.float32
            )
            h = half_sq[at, :]
            t = product * ALPHA - jnp.concatenate([h] * (BLOCK // 128), axis=1)
            scores[at, cols] = t
            top = jnp.maximum(top, jnp.max(t.reshape(32, 8, BLOCK), axis=0))
        peak[p] = top

    def soften(p):
        cols = pl.ds(pl.multiple_of(p * BLOCK, BLOCK), BLOCK)
        top = jnp.max(peak[p], axis=0, keepdims=True)
        total = jnp.zeros((8, BLOCK), jnp.float32)
        for i in range(4):
            e = jnp.exp2(scores[i * 256 : (i + 1) * 256, cols] - top)
            total = total + jnp.sum(e.reshape(32, 8, BLOCK), axis=0)
        lse = top + jnp.log2(jnp.sum(total, axis=0, keepdims=True))
        lse_mine[2 * p] = lse[:, :ROWS]
        lse_mine[2 * p + 1] = lse[:, ROWS:]

    def mirror(s, a):
        return 2 * PLACE[ORDER[s // 2] ^ ORDER[a // 2]] + (s % 2 ^ a % 2)

    def stat_copy(a):
        return remote(lse_mine.at[a], lse_in.at[a], stat_send.at[a], stat_recv, slot_peer(a))

    def part_copy(a):
        return remote(part_mine, part_in.at[a], part_send.at[a], part_recv, slot_peer(a))

    def fin_copy(a):
        return remote(
            lse_mine.at[pl.ds(12, 4)], fin_in.at[a], fin_send.at[a], fin_recv, slot_peer(a)
        )

    def count_copy(n):
        return remote(
            count_mine.at[n], count_in.at[n], count_send.at[n], count_recv, cent_peer(ORDER[n])
        )

    def wait_all(ref, sem):
        remote(ref, ref, own_sem, sem, row_peer(0, 1)).wait_recv()

    cent_start(0)
    row_start(0)
    cent_start(1)
    row_start(1)
    cent_start(2)
    row_start(2)
    for j in range(3):
        sib_copy(0, j).start()
    cent_arrive(0)
    cent_start(3)
    cent_start(4)
    row_arrive(0)
    row_start(3)
    row_start(4)
    cent_arrive(1)
    cent_start(5)
    cent_arrive(2)
    own.wait()
    squares(0)

    def before(t):
        if t == 0:
            sib_arrive(0)
        if t == 1:
            row_arrive(1)
            row_start(5)
            cent_arrive(3)
            cent_start(6)
            row_arrive(2)
        if t in (1, 2, 3):
            sib_arrive(ORDER[t])
        if t == 4:
            for w in (4, 5, 6):
                cent_arrive(w)
            squares(1)
        if t == 5:
            row_arrive(3)
            row_start(6)
        if t == 7:
            row_arrive(4)
        if t == 8:
            row_arrive(5)
        if t == 12:
            row_arrive(6)
        if t in (8, 10, 12, 14):
            sib_arrive(ORDER[t // 2])

    @pl.loop(0, 16)
    def _(t):
        for when in (0, 1, 2, 3, 4, 5, 7, 8, 10, 12, 14):
            pl.when(t == when)(functools.partial(before, when))
        p = jnp.where(t < 8, t % 4, t // 2)
        half = jnp.where(t < 8, t // 4, t % 2)
        score(p, half)

        @pl.when(t == 15)
        def _():
            wait_all(lse_in.at[pl.ds(1, 11)], stat_recv)
            part_mine[...] = combine([lse_mine[0]] + [lse_in[a] for a in range(1, 12)])
            for a in range(1, 16):
                part_copy(a).start()

        @pl.when(half == 1)
        def _():
            soften(p)
            for q in range(6):

                @pl.when(p == q)
                def _():
                    for a in (2 * q, 2 * q + 1):
                        if a:
                            stat_copy(a).start()

    for a in range(1, 16):
        fin_copy(a).start()
    wait_all(part_in.at[pl.ds(1, 15)], part_recv)
    wait_all(fin_in.at[pl.ds(1, 15)], fin_recv)
    for s in range(16):
        terms = [part_mine[...] if s == 0 else part_in[s]]
        for q in range(12, 16):
            a = mirror(s, q)
            terms.append(lse_mine[q] if a == 0 else fin_in[a, q - 12])
        lse = combine(terms)
        lse_all[:, s * ROWS : (s + 1) * ROWS] = lse
        if s == 0:
            norm_out[...] = (lse * LN2).reshape(ROWS)

    def weigh(p):
        at = pl.ds(pl.multiple_of(p * CENTS, CENTS), CENTS)
        count = jnp.zeros((CENTS, 128), jnp.float32)
        total = jnp.zeros((CENTS, WIDTH), jnp.float32)
        for r in range(8):
            cols = slice(r * BLOCK, (r + 1) * BLOCK)
            resp = jnp.exp2(scores[at, cols] - lse_all[:, cols]).astype(jnp.bfloat16)
            wide = resp.astype(jnp.float32)
            for q in range(BLOCK // 128):
                count = count + wide[:, q * 128 : (q + 1) * 128]
            total = total + lax.dot_general(
                resp, rows[cols, :], NN, preferred_element_type=jnp.float32
            )
        sums[p] = total
        outbox[p] = total.astype(jnp.bfloat16)
        count_mine[p] = jnp.sum(count.T, axis=0, keepdims=True)

    def step_of(n, j):
        return next(s for s in range(3) if n >> (j + s) % 3 & 1)

    def sum_copy(n, j):
        at = pl.ds(*CENT_THIRDS[j])
        s = step_of(n, j)
        d = (j + s) % 3
        box = (inbox1, inbox2, inbox3)[s]
        dst = box.at[0 if s == 2 else PLACE[n ^ 1 << d], at]
        return remote(
            outbox.at[PLACE[n], at], dst, sum_send.at[n, j], sum_recv.at[n, j], cent_peer(1 << d)
        )

    def gathered(n, j):
        off, size = CENT_THIRDS[j]
        value = sums[PLACE[n], off : off + size, :]
        for s in range(step_of(n, j) if n else 3):
            came = n | 1 << (j + s) % 3
            sum_copy(came, j).wait_recv()
            box = (inbox1, inbox2, inbox3)[s]
            at = 0 if s == 2 else PLACE[n]
            value = value + box[at, off : off + size, :].astype(jnp.float32)
        return value

    def send_sums(n, step):
        for j in range(3):
            if step_of(n, j) == step:
                if step:
                    off, size = CENT_THIRDS[j]
                    outbox[PLACE[n], off : off + size, :] = gathered(n, j).astype(jnp.bfloat16)
                sum_copy(n, j).start()

    def after(p):
        n = ORDER[p]
        if n:
            send_sums(n, 0)
            count_copy(p).start()
        if p == 4:
            for m in (6, 5, 3):
                send_sums(m, 1)
        if p == 1:
            for m in (4, 2, 1):
                send_sums(m, 1)

    @pl.loop(0, 8)
    def _(i):
        weigh(7 - i)
        for p in range(8):
            pl.when(i == 7 - p)(functools.partial(after, p))

    for n in (4, 2, 1):
        send_sums(n, 2)

    for w in range(7):
        for msg in wave[w]:
            row_copy(*msg).wait_send()
            cent_copy(*msg).wait_send()
    for n in range(8):
        for j in range(3):
            sib_copy(n, j).wait_send()
    for a in range(1, 16):
        if a < 12:
            stat_copy(a).wait_send()
        part_copy(a).wait_send()
        fin_copy(a).wait_send()
    wait_all(count_in.at[pl.ds(1, 7)], count_recv)
    count = functools.reduce(jnp.add, [count_mine[0]] + [count_in[n] for n in range(1, 8)])
    count_out[...] = count.reshape(CENTS)
    below = jnp.broadcast_to(count, (CENTS, 128)).T + PRIOR
    for j in range(3):
        off, size = CENT_THIRDS[j]
        top = gathered(0, j) + PRIOR * book[off : off + size, :]
        for q in range(WIDTH // 128):
            cols = slice(q * 128, (q + 1) * 128)
            new_out[off : off + size, cols] = top[:, cols] / below[off : off + size, :]
    for n in range(1, 8):
        count_copy(n).wait_send()
        for j in range(3):
            sum_copy(n, j).wait_send()


def hand_over(*results):
    def body(*refs):
        ins, outs, sems = refs[:3], refs[3:6], refs[6]
        copies = [pltpu.make_async_copy(a, b, sems.at[i]) for i, (a, b) in enumerate(zip(ins, outs))]
        for copy in copies:
            copy.start()
        for copy in copies:
            copy.wait()

    return pl.pallas_call(
        body,
        out_shape=[jax.ShapeDtypeStruct(r.shape, r.dtype) for r in results],
        in_specs=[pl.BlockSpec(memory_space=pl.ANY)] * 3,
        out_specs=[pl.BlockSpec(memory_space=pl.ANY)] * 3,
        scratch_shapes=[pltpu.SemaphoreType.DMA((3,))],
    )(*results)


def local(embeddings, codebook):
    f32, bf16 = jnp.float32, jnp.bfloat16
    vmem, dma = pltpu.VMEM, pltpu.SemaphoreType.DMA
    new, count, norm = pl.pallas_call(
        kernel,
        out_shape=(
            jax.ShapeDtypeStruct((CENTS, WIDTH), f32),
            jax.ShapeDtypeStruct((CENTS,), f32),
            jax.ShapeDtypeStruct((ROWS,), f32),
        ),
        in_specs=[pl.BlockSpec(memory_space=pl.ANY), pl.BlockSpec(memory_space=pltpu.VMEM)],
        out_specs=[pl.BlockSpec(memory_space=pltpu.VMEM)] * 3,
        scratch_shapes=[
            vmem((8 * BLOCK, WIDTH), bf16),
            vmem((8 * CENTS, WIDTH), bf16),
            vmem((8 * CENTS, 8 * BLOCK), f32),
            vmem((8 * CENTS, 128), f32),
            vmem((8, 8, BLOCK), f32),
            vmem((8, CENTS, WIDTH), f32),
            vmem((CENTS, 128), f32),
            vmem((1, 8 * BLOCK), f32),
            vmem((16, 1, ROWS), f32),
            vmem((16, 1, ROWS), f32),
            vmem((1, ROWS), f32),
            vmem((16, 1, ROWS), f32),
            vmem((16, 4, 1, ROWS), f32),
            vmem((8, 1, CENTS), f32),
            vmem((8, 1, CENTS), f32),
            vmem((8, CENTS, WIDTH), bf16),
            vmem((8, CENTS, WIDTH), bf16),
            vmem((8, CENTS, WIDTH), bf16),
            vmem((1, CENTS, WIDTH), bf16),
            dma(()),
            dma((8, 3)), dma((8, 3)),
            dma((8, 3)), dma((8, 3)),
            dma((8, 3)), dma((8, 3)),
            dma((16,)), dma(()),
            dma((16,)), dma(()),
            dma((16,)), dma(()),
            dma((8,)), dma(()),
            dma((8, 3)), dma((8, 3)),
        ],
        compiler_params=pltpu.CompilerParams(
            collective_id=0, has_side_effects=True, vmem_limit_bytes=58 * 2**20
        ),
        cost_estimate=pl.CostEstimate(
            flops=4 * 4096 * 1024 * 1024, bytes_accessed=2**21, transcendentals=2**23
        ),
    )(embeddings, codebook)
    return hand_over(new, count, norm)


def solution(mesh):
    return jax.shard_map(
        local,
        mesh=mesh,
        in_specs=(P(("dp", "cent"), None), P(("cent", "dp"), None)),
        out_specs=(P(("cent", "dp"), None), P(("cent", "dp")), P(("dp", "cent"))),
        check_vma=False,
    )
```

```python
import functools
import math

import jax
import jax.numpy as jnp
from jax import lax
from jax.experimental import pallas as pl
from jax.experimental.pallas import tpu as pltpu
from jax.sharding import PartitionSpec as P

TEMPER = 0.8
PRIOR = 1.0
ALPHA = math.log2(math.e) / TEMPER
LN2 = math.log(2.0)
MESH = pl.DeviceIdType.MESH

ROWS, CENTS, WIDTH = 256, 128, 1024
BLOCK = 2 * ROWS
ROW_THIRDS = ((0, 96), (96, 80), (176, 80))
CENT_THIRDS = ((0, 48), (48, 48), (96, 32))
ORDER = (0, 1, 2, 4, 3, 5, 6, 7)
PLACE = {mask: i for i, mask in enumerate(ORDER)}
NT = (((1,), (1,)), ((), ()))
NN = (((1,), (0,)), ((), ()))


def waves():
    bit = lambda d: 1 << (d % 3)
    return (
        [(d, d, 0) for d in range(3)],
        [(d, (d - 1) % 3, 0) for d in range(3)],
        [(d, (d - 2) % 3, 0) for d in range(3)],
        [(d, (d - 1) % 3, bit(d - 1)) for d in range(3)],
        [(d, (d - 2) % 3, bit(d - 2)) for d in range(3)],
        [(d, (d - 2) % 3, bit(d - 1)) for d in range(3)],
        [(d, (d - 2) % 3, bit(d - 1) | bit(d - 2)) for d in range(3)],
    )


def combine(terms):
    top = functools.reduce(jnp.maximum, terms)
    total = functools.reduce(jnp.add, [jnp.exp2(t - top) for t in terms])
    return top + jnp.log2(total)


def kernel(
    emb, book, new_out, count_out, norm_out,
    rows, cents, scores, half_sq, peak, sums, tally, lse_all,
    lse_mine, lse_in, part_mine, part_in, fin_in, count_mine, count_in,
    outbox, inbox1, inbox2, inbox3,
    own_sem, row_send, row_recv, sib_send, sib_recv, cent_send, cent_recv,
    stat_send, stat_recv, part_send, part_recv, fin_send, fin_recv,
    count_send, count_recv, sum_send, sum_recv,
):
    dp, cent = lax.axis_index("dp"), lax.axis_index("cent")
    place = (cent // 4, cent % 4, dp // 2)
    core = dp % 2

    def device(p, c):
        return (p[2] * 2 + c, p[0] * 4 + p[1])

    def row_peer(mask, other=0):
        p = [v + 1 - 2 * (v % 2) if mask >> d & 1 else v for d, v in enumerate(place)]
        return device(p, 1 - core if other else core)

    def cent_peer(mask):
        return device([3 - v if mask >> d & 1 else v for d, v in enumerate(place)], core)

    def slot_peer(a):
        return row_peer(ORDER[a // 2], a % 2)

    def remote(src, dst, send, recv, to):
        return pltpu.make_async_remote_copy(
            src_ref=src, dst_ref=dst, send_sem=send, recv_sem=recv,
            device_id=to, device_id_type=MESH,
        )

    barrier = pltpu.get_barrier_semaphore()
    peers = [row_peer(0, 1)] + [row_peer(b) for b in (1, 2, 4)] + [cent_peer(b) for b in (1, 2, 4)]
    for peer in peers:
        pl.semaphore_signal(barrier, inc=1, device_id=peer, device_id_type=MESH)
    own = pltpu.make_async_copy(emb, rows.at[pl.ds(0, ROWS)], own_sem)
    own.start()
    cents[0:CENTS, :] = book[...].astype(jnp.bfloat16)
    pl.semaphore_wait(barrier, len(peers))

    def row_at(n, k, j):
        off, size = ROW_THIRDS[j]
        return pl.ds(PLACE[n] * BLOCK + k * ROWS + off, size)

    def cent_at(n, j):
        off, size = CENT_THIRDS[j]
        return pl.ds(PLACE[n] * CENTS + off, size)

    def row_copy(d, j, m):
        n = m | 1 << d
        src = emb.at[pl.ds(*ROW_THIRDS[j])] if m == 0 else rows.at[row_at(m, 0, j)]
        dst = rows.at[row_at(n, 0, j)]
        return remote(src, dst, row_send.at[n, j], row_recv.at[n, j], row_peer(1 << d))

    def cent_copy(d, j, m):
        n = m | 1 << d
        src, dst = cents.at[cent_at(m, j)], cents.at[cent_at(n, j)]
        return remote(src, dst, cent_send.at[n, j], cent_recv.at[n, j], cent_peer(1 << d))

    def sib_copy(n, j):
        src = emb.at[pl.ds(*ROW_THIRDS[j])] if n == 0 else rows.at[row_at(n, 0, j)]
        dst = rows.at[row_at(n, 1, j)]
        return remote(src, dst, sib_send.at[n, j], sib_recv.at[n, j], row_peer(0, 1))

    wave = waves()

    def row_start(w):
        for msg in wave[w]:
            row_copy(*msg).start()

    def cent_start(w):
        for msg in wave[w]:
            cent_copy(*msg).start()

    def row_arrive(w):
        for d, j, m in wave[w]:
            row_copy(d, j, m).wait_recv()
            sib_copy(m | 1 << d, j).start()

    def cent_arrive(w):
        for msg in wave[w]:
            cent_copy(*msg).wait_recv()

    def sib_arrive(n):
        for j in range(3):
            sib_copy(n, j).wait_recv()

    def squares(half):
        @pl.loop(0, 4)
        def _(i):
            at = pl.ds(pl.multiple_of(half * 512 + i * CENTS, CENTS), CENTS)
            c = cents[at, :].astype(jnp.float32)
            total = jnp.sum(c * c, axis=1, keepdims=True) * (0.5 * ALPHA)
            half_sq[at, :] = jnp.broadcast_to(total, (CENTS, 128))

    def score(p, half):
        cols = pl.ds(pl.multiple_of(p * BLOCK, BLOCK), BLOCK)
        top = jnp.where(half == 0, -jnp.inf, peak[p])
        for i in range(2):
            at = pl.ds(pl.multiple_of(half * 512 + i * 256, 256), 256)
            product = lax.dot_general(
                cents[at, :], rows[cols, :], NT, preferred_element_type=jnp.float32
            )
            h = half_sq[at, :]
            t = product * ALPHA - jnp.concatenate([h] * (BLOCK // 128), axis=1)
            scores[at, cols] = t
            top = jnp.maximum(top, jnp.max(t.reshape(32, 8, BLOCK), axis=0))
        peak[p] = top

    def soften(p):
        cols = pl.ds(pl.multiple_of(p * BLOCK, BLOCK), BLOCK)
        top = jnp.max(peak[p], axis=0, keepdims=True)
        total = jnp.zeros((8, BLOCK), jnp.float32)
        for i in range(4):
            e = jnp.exp2(scores[i * 256 : (i + 1) * 256, cols] - top)
            total = total + jnp.sum(e.reshape(32, 8, BLOCK), axis=0)
        lse = top + jnp.log2(jnp.sum(total, axis=0, keepdims=True))
        lse_mine[2 * p] = lse[:, :ROWS]
        lse_mine[2 * p + 1] = lse[:, ROWS:]

    def mirror(s, a):
        return 2 * PLACE[ORDER[s // 2] ^ ORDER[a // 2]] + (s % 2 ^ a % 2)

    def stat_copy(a):
        return remote(lse_mine.at[a], lse_in.at[a], stat_send.at[a], stat_recv, slot_peer(a))

    def part_copy(a):
        return remote(part_mine, part_in.at[a], part_send.at[a], part_recv, slot_peer(a))

    def fin_copy(a):
        return remote(
            lse_mine.at[pl.ds(12, 4)], fin_in.at[a], fin_send.at[a], fin_recv, slot_peer(a)
        )

    def count_copy(n):
        return remote(
            count_mine.at[n], count_in.at[n], count_send.at[n], count_recv, cent_peer(ORDER[n])
        )

    def wait_all(ref, sem):
        remote(ref, ref, own_sem, sem, row_peer(0, 1)).wait_recv()

    cent_start(0)
    row_start(0)
    cent_start(1)
    row_start(1)
    cent_start(2)
    row_start(2)
    for j in range(3):
        sib_copy(0, j).start()
    cent_arrive(0)
    cent_start(3)
    cent_start(4)
    row_arrive(0)
    row_start(3)
    row_start(4)
    cent_arrive(1)
    cent_start(5)
    cent_arrive(2)
    own.wait()
    squares(0)

    def before(t):
        if t == 0:
            sib_arrive(0)
        if t == 1:
            row_arrive(1)
            row_start(5)
            cent_arrive(3)
            cent_start(6)
            row_arrive(2)
        if t in (1, 2, 3):
            sib_arrive(ORDER[t])
        if t == 4:
            for w in (4, 5, 6):
                cent_arrive(w)
            squares(1)
        if t == 5:
            row_arrive(3)
            row_start(6)
        if t == 7:
            row_arrive(4)
        if t == 8:
            row_arrive(5)
        if t == 12:
            row_arrive(6)
        if t in (8, 10, 12, 14):
            sib_arrive(ORDER[t // 2])

    @pl.loop(0, 16)
    def _(t):
        for when in (0, 1, 2, 3, 4, 5, 7, 8, 10, 12, 14):
            pl.when(t == when)(functools.partial(before, when))
        p = jnp.where(t < 8, t % 4, t // 2)
        half = jnp.where(t < 8, t // 4, t % 2)
        score(p, half)

        @pl.when(t == 15)
        def _():
            wait_all(lse_in.at[pl.ds(1, 11)], stat_recv)
            part_mine[...] = combine([lse_mine[0]] + [lse_in[a] for a in range(1, 12)])
            for a in range(1, 16):
                part_copy(a).start()

        @pl.when(half == 1)
        def _():
            soften(p)
            for q in range(6):

                @pl.when(p == q)
                def _():
                    for a in (2 * q, 2 * q + 1):
                        if a:
                            stat_copy(a).start()

    for a in range(1, 16):
        fin_copy(a).start()
    wait_all(part_in.at[pl.ds(1, 15)], part_recv)
    wait_all(fin_in.at[pl.ds(1, 15)], fin_recv)
    for s in range(16):
        terms = [part_mine[...] if s == 0 else part_in[s]]
        for q in range(12, 16):
            a = mirror(s, q)
            terms.append(lse_mine[q] if a == 0 else fin_in[a, q - 12])
        lse = combine(terms)
        lse_all[:, s * ROWS : (s + 1) * ROWS] = lse
        if s == 0:
            norm_out[...] = (lse * LN2).reshape(ROWS)

    def weigh(p):
        at = pl.ds(pl.multiple_of(p * CENTS, CENTS), CENTS)
        count = jnp.zeros((CENTS, 128), jnp.float32)
        total = jnp.zeros((CENTS, WIDTH), jnp.float32)
        for r in range(8):
            cols = slice(r * BLOCK, (r + 1) * BLOCK)
            resp = jnp.exp2(scores[at, cols] - lse_all[:, cols]).astype(jnp.bfloat16)
            wide = resp.astype(jnp.float32)
            for q in range(BLOCK // 128):
                count = count + wide[:, q * 128 : (q + 1) * 128]
            total = total + lax.dot_general(
                resp, rows[cols, :], NN, preferred_element_type=jnp.float32
            )
        sums[p] = total
        outbox[p] = total.astype(jnp.bfloat16)
        count_mine[p] = jnp.sum(count.T, axis=0, keepdims=True)

    def step_of(n, j):
        return next(s for s in range(3) if n >> (j + s) % 3 & 1)

    def sum_copy(n, j):
        at = pl.ds(*CENT_THIRDS[j])
        s = step_of(n, j)
        d = (j + s) % 3
        box = (inbox1, inbox2, inbox3)[s]
        dst = box.at[0 if s == 2 else PLACE[n ^ 1 << d], at]
        return remote(
            outbox.at[PLACE[n], at], dst, sum_send.at[n, j], sum_recv.at[n, j], cent_peer(1 << d)
        )

    def gathered(n, j):
        off, size = CENT_THIRDS[j]
        value = sums[PLACE[n], off : off + size, :]
        for s in range(step_of(n, j) if n else 3):
            came = n | 1 << (j + s) % 3
            sum_copy(came, j).wait_recv()
            box = (inbox1, inbox2, inbox3)[s]
            at = 0 if s == 2 else PLACE[n]
            value = value + box[at, off : off + size, :].astype(jnp.float32)
        return value

    def send_sums(n, step):
        for j in range(3):
            if step_of(n, j) == step:
                if step:
                    off, size = CENT_THIRDS[j]
                    outbox[PLACE[n], off : off + size, :] = gathered(n, j).astype(jnp.bfloat16)
                sum_copy(n, j).start()

    def after(p):
        n = ORDER[p]
        if n:
            send_sums(n, 0)
            count_copy(p).start()
        if p == 4:
            for m in (6, 5, 3):
                send_sums(m, 1)
        if p == 1:
            for m in (4, 2, 1):
                send_sums(m, 1)

    @pl.loop(0, 8)
    def _(i):
        weigh(7 - i)
        for p in range(8):
            pl.when(i == 7 - p)(functools.partial(after, p))

    for n in (4, 2, 1):
        send_sums(n, 2)

    for w in range(7):
        for msg in wave[w]:
            row_copy(*msg).wait_send()
            cent_copy(*msg).wait_send()
    for n in range(8):
        for j in range(3):
            sib_copy(n, j).wait_send()
    for a in range(1, 16):
        if a < 12:
            stat_copy(a).wait_send()
        part_copy(a).wait_send()
        fin_copy(a).wait_send()
    wait_all(count_in.at[pl.ds(1, 7)], count_recv)
    count = functools.reduce(jnp.add, [count_mine[0]] + [count_in[n] for n in range(1, 8)])
    count_out[...] = count.reshape(CENTS)
    below = jnp.broadcast_to(count, (CENTS, 128)).T + PRIOR
    for j in range(3):
        off, size = CENT_THIRDS[j]
        top = gathered(0, j) + PRIOR * book[off : off + size, :]
        for q in range(WIDTH // 128):
            cols = slice(q * 128, (q + 1) * 128)
            new_out[off : off + size, cols] = top[:, cols] / below[off : off + size, :]
    for n in range(1, 8):
        count_copy(n).wait_send()
        for j in range(3):
            sum_copy(n, j).wait_send()


def hand_over(*results):
    def body(*refs):
        for i in range(3):
            refs[3 + i][...] = refs[i][...]

    return pl.pallas_call(
        body,
        out_shape=[jax.ShapeDtypeStruct(r.shape, r.dtype) for r in results],
        in_specs=[pl.BlockSpec(memory_space=pltpu.VMEM)] * 3,
        out_specs=[pl.BlockSpec(memory_space=pltpu.VMEM)] * 3,
    )(*results)


def local(embeddings, codebook):
    f32, bf16 = jnp.float32, jnp.bfloat16
    vmem, dma = pltpu.VMEM, pltpu.SemaphoreType.DMA
    new, count, norm = pl.pallas_call(
        kernel,
        out_shape=(
            jax.ShapeDtypeStruct((CENTS, WIDTH), f32),
            jax.ShapeDtypeStruct((CENTS,), f32),
            jax.ShapeDtypeStruct((ROWS,), f32),
        ),
        in_specs=[pl.BlockSpec(memory_space=pl.ANY), pl.BlockSpec(memory_space=pltpu.VMEM)],
        out_specs=[pl.BlockSpec(memory_space=pltpu.VMEM)] * 3,
        scratch_shapes=[
            vmem((8 * BLOCK, WIDTH), bf16),
            vmem((8 * CENTS, WIDTH), bf16),
            vmem((8 * CENTS, 8 * BLOCK), f32),
            vmem((8 * CENTS, 128), f32),
            vmem((8, 8, BLOCK), f32),
            vmem((8, CENTS, WIDTH), f32),
            vmem((CENTS, 128), f32),
            vmem((1, 8 * BLOCK), f32),
            vmem((16, 1, ROWS), f32),
            vmem((16, 1, ROWS), f32),
            vmem((1, ROWS), f32),
            vmem((16, 1, ROWS), f32),
            vmem((16, 4, 1, ROWS), f32),
            vmem((8, 1, CENTS), f32),
            vmem((8, 1, CENTS), f32),
            vmem((8, CENTS, WIDTH), bf16),
            vmem((8, CENTS, WIDTH), bf16),
            vmem((8, CENTS, WIDTH), bf16),
            vmem((1, CENTS, WIDTH), bf16),
            dma(()),
            dma((8, 3)), dma((8, 3)),
            dma((8, 3)), dma((8, 3)),
            dma((8, 3)), dma((8, 3)),
            dma((16,)), dma(()),
            dma((16,)), dma(()),
            dma((16,)), dma(()),
            dma((8,)), dma(()),
            dma((8, 3)), dma((8, 3)),
        ],
        compiler_params=pltpu.CompilerParams(
            collective_id=0, has_side_effects=True, vmem_limit_bytes=58 * 2**20
        ),
        cost_estimate=pl.CostEstimate(
            flops=4 * 4096 * 1024 * 1024, bytes_accessed=2**21, transcendentals=2**23
        ),
    )(embeddings, codebook)
    return hand_over(new, count, norm)


def solution(mesh):
    return jax.shard_map(
        local,
        mesh=mesh,
        in_specs=(P(("dp", "cent"), None), P(("cent", "dp"), None)),
        out_specs=(P(("cent", "dp"), None), P(("cent", "dp")), P(("dp", "cent"))),
        check_vma=False,
    )
```

```python
import functools
import math

import jax
import jax.numpy as jnp
from jax import lax
from jax.experimental import pallas as pl
from jax.experimental.pallas import tpu as pltpu
from jax.sharding import PartitionSpec as P

TEMPER = 0.8
PRIOR = 1.0
ALPHA = math.log2(math.e) / TEMPER
LN2 = math.log(2.0)
MESH = pl.DeviceIdType.MESH

ROWS, CENTS, WIDTH = 256, 128, 1024
PART, UNIT = 128, 256
PIECES = (
    (0, 16, (2, 1, 0)),
    (16, 32, (1, 2, 0)),
    (48, 16, (2, 0, 1)),
    (64, 32, (0, 2, 1)),
    (96, 16, (1, 0, 2)),
    (112, 16, (0, 1, 2)),
)
N_PIECES = len(PIECES)
ORDER = (0, 1, 2, 4, 3, 5, 6, 7)
PLACE = {mask: i for i, mask in enumerate(ORDER)}
NT = (((1,), (1,)), ((), ()))
NN = (((1,), (0,)), ((), ()))


def waves():
    wave = [[] for _ in range(7)]
    for j, (_, _, (a, b, c)) in enumerate(PIECES):
        sent = ((a, 0), (b, 0), (c, 0), (b, 1 << a), (c, 1 << a), (c, 1 << b), (c, 1 << a | 1 << b))
        for w, (d, m) in enumerate(sent):
            wave[w].append((d, j, m))
    return wave


def combine(terms):
    top = functools.reduce(jnp.maximum, terms)
    total = functools.reduce(jnp.add, [jnp.exp2(t - top) for t in terms])
    return top + jnp.log2(total)


def kernel(
    emb, book, new_out, count_out, norm_out,
    rows, cents, scores, half_sq, peak, sums, tally, lse_all,
    lse_mine, lse_in, part_mine, part_in, fin_in, count_mine, count_in,
    outbox, inbox1, inbox2, inbox3,
    book_in, own_sem, row_send, row_recv, sib_send, sib_recv, cent_send, cent_recv,
    stat_send, stat_recv, part_send, part_recv, fin_send, fin_recv,
    count_send, count_recv, sum_send, sum_recv,
):
    dp, cent = lax.axis_index("dp"), lax.axis_index("cent")
    place = (cent // 4, cent % 4, dp // 2)
    core = dp % 2

    def device(p, c):
        return (p[2] * 2 + c, p[0] * 4 + p[1])

    def row_peer(mask, other=0):
        p = [v + 1 - 2 * (v % 2) if mask >> d & 1 else v for d, v in enumerate(place)]
        return device(p, 1 - core if other else core)

    def cent_peer(mask):
        return device([3 - v if mask >> d & 1 else v for d, v in enumerate(place)], core)

    def slot_peer(a):
        return row_peer(ORDER[a // 2], a % 2)

    def remote(src, dst, send, recv, to):
        return pltpu.make_async_remote_copy(
            src_ref=src, dst_ref=dst, send_sem=send, recv_sem=recv,
            device_id=to, device_id_type=MESH,
        )

    barrier = pltpu.get_barrier_semaphore()
    peers = [row_peer(0, 1)] + [row_peer(b) for b in (1, 2, 4)] + [cent_peer(b) for b in (1, 2, 4)]
    for peer in peers:
        pl.semaphore_signal(barrier, inc=1, device_id=peer, device_id_type=MESH)
    own = [
        pltpu.make_async_copy(
            emb.at[pl.ds(r * PART, PART)], rows.at[pl.ds(r * 8 * UNIT, PART)], own_sem.at[r]
        )
        for r in range(2)
    ]
    own.append(pltpu.make_async_copy(book, book_in, own_sem.at[2]))
    own[2].start()
    own[0].start()
    own[1].start()
    pl.semaphore_wait(barrier, len(peers))

    def row_at(r, n, k, j):
        return pl.ds((r * 8 + PLACE[n]) * UNIT + k * PART + PIECES[j][0], PIECES[j][1])

    def cent_at(n, j):
        return pl.ds(PLACE[n] * CENTS + PIECES[j][0], PIECES[j][1])

    def row_source(r, m, j):
        if m == 0:
            return emb.at[pl.ds(r * PART + PIECES[j][0], PIECES[j][1])]
        return rows.at[row_at(r, m, 0, j)]

    def row_copy(r, d, j, m):
        n = m | 1 << d
        return remote(
            row_source(r, m, j), rows.at[row_at(r, n, 0, j)],
            row_send.at[r, n, j], row_recv.at[r, n, j], row_peer(1 << d),
        )

    def cent_copy(d, j, m):
        n = m | 1 << d
        src, dst = cents.at[cent_at(m, j)], cents.at[cent_at(n, j)]
        return remote(src, dst, cent_send.at[n, j], cent_recv.at[n, j], cent_peer(1 << d))

    def sib_copy(r, n, j):
        return remote(
            row_source(r, n, j), rows.at[row_at(r, n, 1, j)],
            sib_send.at[r, n, j], sib_recv.at[r, n, j], row_peer(0, 1),
        )

    wave = waves()

    def row_start(r, w):
        for msg in wave[w]:
            row_copy(r, *msg).start()

    def cent_start(w):
        for msg in wave[w]:
            cent_copy(*msg).start()

    def row_arrive(r, w):
        for d, j, m in wave[w]:
            row_copy(r, d, j, m).wait_recv()
            sib_copy(r, m | 1 << d, j).start()

    def cent_arrive(w):
        for msg in wave[w]:
            cent_copy(*msg).wait_recv()

    def sib_arrive(r, p):
        for j in range(N_PIECES):
            sib_copy(r, ORDER[p], j).wait_recv()

    def squares(half):
        @pl.loop(0, 4)
        def _(i):
            at = pl.ds(pl.multiple_of(half * 512 + i * CENTS, CENTS), CENTS)
            c = cents[at, :].astype(jnp.float32)
            total = jnp.sum(c * c, axis=1, keepdims=True) * (0.5 * ALPHA)
            half_sq[at, :] = jnp.broadcast_to(total, (CENTS, 128))

    def columns(u):
        return pl.ds(pl.multiple_of(u * UNIT, UNIT), UNIT)

    def score(u, blocks, fresh, last=None):
        cols = columns(u)
        top = jnp.full((8, UNIT), -jnp.inf, jnp.float32) if fresh else peak[u]
        if last is not None:
            summed = columns(last)
            high = jnp.max(peak[last], axis=0, keepdims=True)
            total = jnp.zeros((8, UNIT), jnp.float32)
        for i in blocks:
            at = slice(i * 256, (i + 1) * 256)
            product = lax.dot_general(
                cents[at, :], rows[cols, :], NT, preferred_element_type=jnp.float32
            )
            if last is not None:
                step = 1024 // len(blocks)
                first = (i - blocks[0]) * step
                e = jnp.exp2(scores[first : first + step, summed] - high)
                total = total + jnp.sum(e.reshape(step // 8, 8, UNIT), axis=0)
            h = half_sq[at, :]
            t = product * ALPHA - jnp.concatenate([h] * (UNIT // 128), axis=1)
            scores[at, cols] = t
            top = jnp.maximum(top, jnp.max(t.reshape(32, 8, UNIT), axis=0))
        peak[u] = top
        if last is not None:
            settle(last, high, total)

    def settle(u, high, total):
        lse = high + jnp.log2(jnp.sum(total, axis=0, keepdims=True))
        r, p = u // 8, u % 8
        lse_mine[r, 2 * p] = lse[:, :PART]
        lse_mine[r, 2 * p + 1] = lse[:, PART:]

    def soften(u):
        high = jnp.max(peak[u], axis=0, keepdims=True)
        total = jnp.zeros((8, UNIT), jnp.float32)
        for i in range(4):
            e = jnp.exp2(scores[i * 256 : (i + 1) * 256, columns(u)] - high)
            total = total + jnp.sum(e.reshape(32, 8, UNIT), axis=0)
        settle(u, high, total)

    def mirror(s, a):
        return 2 * PLACE[ORDER[s // 2] ^ ORDER[a // 2]] + (s % 2 ^ a % 2)

    def stat_copy(r, a):
        return remote(
            lse_mine.at[r, a], lse_in.at[r, a], stat_send.at[r, a], stat_recv.at[r], slot_peer(a)
        )

    def part_copy(r, a):
        return remote(
            part_mine.at[r], part_in.at[r, a], part_send.at[r, a], part_recv.at[r], slot_peer(a)
        )

    def fin_copy(r, a):
        return remote(
            lse_mine.at[r, pl.ds(12, 4)], fin_in.at[r, a],
            fin_send.at[r, a], fin_recv.at[r], slot_peer(a),
        )

    def count_copy(n):
        return remote(
            count_mine.at[n], count_in.at[n], count_send.at[n], count_recv, cent_peer(ORDER[n])
        )

    def wait_all(ref, sem):
        remote(ref, ref, own_sem.at[0], sem, row_peer(0, 1)).wait_recv()

    def settled(u):
        r, p = u // 8, u % 8
        if p < 6:
            for a in (2 * p, 2 * p + 1):
                if a:
                    stat_copy(r, a).start()
        if p == 6:
            wait_all(lse_in.at[r, pl.ds(1, 11)], stat_recv.at[r])
            part_mine[r] = combine([lse_mine[r, 0]] + [lse_in[r, a] for a in range(1, 12)])
            for a in range(1, 16):
                part_copy(r, a).start()
        if p == 7:
            for a in range(1, 16):
                fin_copy(r, a).start()

    def agree(r):
        wait_all(part_in.at[r, pl.ds(1, 15)], part_recv.at[r])
        wait_all(fin_in.at[r, pl.ds(1, 15)], fin_recv.at[r])
        for s in range(16):
            terms = [part_mine[r] if s == 0 else part_in[r, s]]
            for q in range(12, 16):
                a = mirror(s, q)
                terms.append(lse_mine[r, q] if a == 0 else fin_in[r, a, q - 12])
            lse = combine(terms)
            at = (r * 16 + s) * PART
            lse_all[:, at : at + PART] = lse
            if s == 0:
                norm_out[r * PART : (r + 1) * PART] = (lse * LN2).reshape(PART)

    for w in range(3):
        row_start(0, w)
    own[2].wait()
    cents[0:CENTS, :] = book_in[...].astype(jnp.bfloat16)
    for w in range(3):
        cent_start(w)
    for r in range(2):
        for j in range(N_PIECES):
            sib_copy(r, 0, j).start()
    own[0].wait()
    own[1].wait()
    cent_arrive(0)
    cent_start(3)
    cent_start(4)
    row_arrive(0, 0)
    row_start(0, 3)
    row_start(0, 4)
    cent_arrive(1)
    cent_start(5)
    row_arrive(0, 1)
    row_start(0, 5)
    cent_arrive(2)
    squares(0)
    row_arrive(0, 2)
    cent_arrive(3)
    cent_start(6)
    row_arrive(0, 3)
    row_start(0, 6)
    row_start(1, 0)
    for p in range(4):
        sib_arrive(0, p)

    @pl.loop(0, 4)
    def _(u):
        score(u, (0, 1), True)

    row_arrive(0, 4)
    cent_arrive(4)
    row_arrive(0, 5)
    row_start(1, 1)
    row_start(1, 2)
    cent_arrive(5)
    row_arrive(0, 6)
    cent_arrive(6)
    squares(1)
    score(0, (2, 3), False)

    @pl.loop(1, 4)
    def _(u):
        @pl.when(u == 2)
        def _():
            row_arrive(1, 0)
            row_start(1, 3)
            row_start(1, 4)

        score(u, (2, 3), False, u - 1)
        for v in range(3):
            pl.when(u == v + 1)(functools.partial(settled, v))

    def before(u):
        if u == 5:
            row_arrive(1, 1)
            row_start(1, 5)
        if u == 8:
            row_arrive(1, 2)
        if u == 10:
            row_arrive(1, 3)
            row_start(1, 6)
        if u == 14:
            row_arrive(1, 6)
        sib_arrive(u // 8, u % 8)

    def unit_loop(lo, hi):
        @pl.loop(lo, hi)
        def _(u):
            for v in range(lo, hi):
                pl.when(u == v)(functools.partial(before, v))
            score(u, (0, 1, 2, 3), True, u - 1)
            for v in range(lo, hi):
                pl.when(u == v)(functools.partial(settled, v - 1))

    def weigh(p, r):
        at = pl.ds(pl.multiple_of(p * CENTS, CENTS), CENTS)
        count = tally[p] if r else jnp.zeros((CENTS, 128), jnp.float32)
        total = sums[p] if r else jnp.zeros((CENTS, WIDTH), jnp.float32)
        for i in range(4):
            cols = slice((r * 4 + i) * 2 * UNIT, (r * 4 + i + 1) * 2 * UNIT)
            resp = jnp.exp2(scores[at, cols] - lse_all[:, cols]).astype(jnp.bfloat16)
            wide = resp.astype(jnp.float32)
            for q in range(2 * UNIT // 128):
                count = count + wide[:, q * 128 : (q + 1) * 128]
            total = total + lax.dot_general(
                resp, rows[cols, :], NN, preferred_element_type=jnp.float32
            )
        sums[p] = total
        if r:
            outbox[p] = total.astype(jnp.bfloat16)
            count_mine[p] = jnp.sum(count.T, axis=0, keepdims=True)
        else:
            tally[p] = count

    def step_of(n, j):
        return next(s for s in range(3) if n >> PIECES[j][2][s] & 1)

    def sum_copy(n, j):
        at = pl.ds(*PIECES[j][:2])
        s = step_of(n, j)
        d = PIECES[j][2][s]
        box = (inbox1, inbox2, inbox3)[s]
        dst = box.at[0 if s == 2 else PLACE[n ^ 1 << d], at]
        return remote(
            outbox.at[PLACE[n], at], dst, sum_send.at[n, j], sum_recv.at[n, j], cent_peer(1 << d)
        )

    def gathered(n, j):
        off, size, order = PIECES[j]
        value = sums[PLACE[n], off : off + size, :]
        for s in range(step_of(n, j) if n else 3):
            came = n | 1 << order[s]
            sum_copy(came, j).wait_recv()
            box = (inbox1, inbox2, inbox3)[s]
            at = 0 if s == 2 else PLACE[n]
            value = value + box[at, off : off + size, :].astype(jnp.float32)
        return value

    def send_sums(n, step):
        for j in range(N_PIECES):
            if step_of(n, j) == step:
                if step:
                    off, size, _ = PIECES[j]
                    outbox[PLACE[n], off : off + size, :] = gathered(n, j).astype(jnp.bfloat16)
                sum_copy(n, j).start()

    def after(p):
        n = ORDER[p]
        if n:
            send_sums(n, 0)
            count_copy(p).start()
        if p == 4:
            for m in (6, 5, 3):
                send_sums(m, 1)
        if p == 1:
            for m in (4, 2, 1):
                send_sums(m, 1)

    unit_loop(4, 12)
    agree(0)

    @pl.loop(0, 3)
    def _(i):
        weigh(7 - i, 0)
        pl.when(i == 0)(functools.partial(row_arrive, 1, 4))

    row_arrive(1, 5)
    unit_loop(12, 16)
    soften(15)
    settled(15)

    @pl.loop(3, 8)
    def _(i):
        weigh(7 - i, 0)

    agree(1)

    @pl.loop(0, 8)
    def _(i):
        weigh(7 - i, 1)
        for p in range(8):
            pl.when(i == 7 - p)(functools.partial(after, p))

    for n in (4, 2, 1):
        send_sums(n, 2)

    for w in range(7):
        for msg in wave[w]:
            row_copy(0, *msg).wait_send()
            row_copy(1, *msg).wait_send()
            cent_copy(*msg).wait_send()
    for r in range(2):
        for n in range(8):
            for j in range(N_PIECES):
                sib_copy(r, n, j).wait_send()
        for a in range(1, 16):
            if a < 12:
                stat_copy(r, a).wait_send()
            part_copy(r, a).wait_send()
            fin_copy(r, a).wait_send()
    wait_all(count_in.at[pl.ds(1, 7)], count_recv)
    count = functools.reduce(jnp.add, [count_mine[0]] + [count_in[n] for n in range(1, 8)])
    count_out[...] = count.reshape(CENTS)
    below = jnp.broadcast_to(count, (CENTS, 128)).T + PRIOR
    for j in range(N_PIECES):
        off, size, _ = PIECES[j]
        top = gathered(0, j) + PRIOR * book_in[off : off + size, :]
        for q in range(WIDTH // 128):
            cols = slice(q * 128, (q + 1) * 128)
            new_out[off : off + size, cols] = top[:, cols] / below[off : off + size, :]
    for n in range(1, 8):
        count_copy(n).wait_send()
        for j in range(N_PIECES):
            sum_copy(n, j).wait_send()


def hand_over(*results):
    def body(*refs):
        for i in range(3):
            refs[3 + i][...] = refs[i][...]

    return pl.pallas_call(
        body,
        out_shape=[jax.ShapeDtypeStruct(r.shape, r.dtype) for r in results],
        in_specs=[pl.BlockSpec(memory_space=pltpu.VMEM)] * 3,
        out_specs=[pl.BlockSpec(memory_space=pltpu.VMEM)] * 3,
    )(*results)


def local(embeddings, codebook):
    f32, bf16 = jnp.float32, jnp.bfloat16
    vmem, dma = pltpu.VMEM, pltpu.SemaphoreType.DMA
    new, count, norm = pl.pallas_call(
        kernel,
        out_shape=(
            jax.ShapeDtypeStruct((CENTS, WIDTH), f32),
            jax.ShapeDtypeStruct((CENTS,), f32),
            jax.ShapeDtypeStruct((ROWS,), f32),
        ),
        in_specs=[pl.BlockSpec(memory_space=pl.ANY)] * 2,
        out_specs=[pl.BlockSpec(memory_space=pltpu.VMEM)] * 3,
        scratch_shapes=[
            vmem((16 * UNIT, WIDTH), bf16),
            vmem((8 * CENTS, WIDTH), bf16),
            vmem((8 * CENTS, 16 * UNIT), f32),
            vmem((8 * CENTS, 128), f32),
            vmem((16, 8, UNIT), f32),
            vmem((8, CENTS, WIDTH), f32),
            vmem((8, CENTS, 128), f32),
            vmem((1, 16 * UNIT), f32),
            vmem((2, 16, 1, PART), f32),
            vmem((2, 16, 1, PART), f32),
            vmem((2, 1, PART), f32),
            vmem((2, 16, 1, PART), f32),
            vmem((2, 16, 4, 1, PART), f32),
            vmem((8, 1, CENTS), f32),
            vmem((8, 1, CENTS), f32),
            vmem((8, CENTS, WIDTH), bf16),
            vmem((8, CENTS, WIDTH), bf16),
            vmem((8, CENTS, WIDTH), bf16),
            vmem((1, CENTS, WIDTH), bf16),
            vmem((CENTS, WIDTH), f32),
            dma((3,)),
            dma((2, 8, N_PIECES)), dma((2, 8, N_PIECES)),
            dma((2, 8, N_PIECES)), dma((2, 8, N_PIECES)),
            dma((8, N_PIECES)), dma((8, N_PIECES)),
            dma((2, 16)), dma((2,)),
            dma((2, 16)), dma((2,)),
            dma((2, 16)), dma((2,)),
            dma((8,)), dma(()),
            dma((8, N_PIECES)), dma((8, N_PIECES)),
        ],
        compiler_params=pltpu.CompilerParams(
            collective_id=0, has_side_effects=True, vmem_limit_bytes=58 * 2**20
        ),
        cost_estimate=pl.CostEstimate(
            flops=4 * 4096 * 1024 * 1024, bytes_accessed=2**21, transcendentals=2**23
        ),
    )(embeddings, codebook)
    return hand_over(new, count, norm)


def solution(mesh):
    return jax.shard_map(
        local,
        mesh=mesh,
        in_specs=(P(("dp", "cent"), None), P(("cent", "dp"), None)),
        out_specs=(P(("cent", "dp"), None), P(("cent", "dp")), P(("dp", "cent"))),
        check_vma=False,
    )
```

```python
import functools
import math

import jax
import jax.numpy as jnp
from jax import lax
from jax.experimental import pallas as pl
from jax.experimental.pallas import tpu as pltpu
from jax.sharding import PartitionSpec as P

TEMPER = 0.8
PRIOR = 1.0
ALPHA = math.log2(math.e) / TEMPER
LN2 = math.log(2.0)
MESH = pl.DeviceIdType.MESH

ROWS, CENTS, WIDTH = 256, 128, 1024
PART, UNIT = 128, 256
PIECES = (
    (0, 16, (2, 1, 0)),
    (16, 32, (1, 2, 0)),
    (48, 16, (2, 0, 1)),
    (64, 32, (0, 2, 1)),
    (96, 16, (1, 0, 2)),
    (112, 16, (0, 1, 2)),
)
N_PIECES = len(PIECES)
ORDER = (0, 1, 2, 4, 3, 5, 6, 7)
PLACE = {mask: i for i, mask in enumerate(ORDER)}
EARLY = 8
NT = (((1,), (1,)), ((), ()))
NN = (((1,), (0,)), ((), ()))


def waves():
    wave = [[] for _ in range(7)]
    for j, (_, _, (a, b, c)) in enumerate(PIECES):
        sent = ((a, 0), (b, 0), (c, 0), (b, 1 << a), (c, 1 << a), (c, 1 << b), (c, 1 << a | 1 << b))
        for w, (d, m) in enumerate(sent):
            wave[w].append((d, j, m))
    return wave


def combine(terms):
    top = functools.reduce(jnp.maximum, terms)
    total = functools.reduce(jnp.add, [jnp.exp2(t - top) for t in terms])
    return top + jnp.log2(total)


def kernel(
    emb, book, new_out, count_out, norm_out,
    rows, cents, scores, half_sq, peak, sums, tally, lse_all,
    lse_mine, lse_in, part_mine, part_in, fin_in, count_mine, count_in,
    outbox, inbox1, inbox2, inbox3,
    book_in, own_sem, row_send, row_recv, sib_send, sib_recv, cent_send, cent_recv,
    stat_send, stat_recv, part_send, part_recv, fin_send, fin_recv,
    count_send, count_recv, sum_send, sum_recv,
):
    dp, cent = lax.axis_index("dp"), lax.axis_index("cent")
    place = (cent // 4, cent % 4, dp // 2)
    core = dp % 2

    def device(p, c):
        return (p[2] * 2 + c, p[0] * 4 + p[1])

    def row_peer(mask, other=0):
        p = [v + 1 - 2 * (v % 2) if mask >> d & 1 else v for d, v in enumerate(place)]
        return device(p, 1 - core if other else core)

    def cent_peer(mask):
        return device([3 - v if mask >> d & 1 else v for d, v in enumerate(place)], core)

    def slot_peer(a):
        return row_peer(ORDER[a // 2], a % 2)

    def remote(src, dst, send, recv, to):
        return pltpu.make_async_remote_copy(
            src_ref=src, dst_ref=dst, send_sem=send, recv_sem=recv,
            device_id=to, device_id_type=MESH,
        )

    barrier = pltpu.get_barrier_semaphore()
    peers = [row_peer(0, 1)] + [row_peer(b) for b in (1, 2, 4)] + [cent_peer(b) for b in (1, 2, 4)]
    for peer in peers:
        pl.semaphore_signal(barrier, inc=1, device_id=peer, device_id_type=MESH)
    own = [
        pltpu.make_async_copy(
            emb.at[pl.ds(r * PART, PART)], rows.at[pl.ds(r * 8 * UNIT, PART)], own_sem.at[r]
        )
        for r in range(2)
    ]
    own.append(pltpu.make_async_copy(book, book_in, own_sem.at[2]))
    own[2].start()
    own[0].start()
    own[1].start()
    pl.semaphore_wait(barrier, len(peers))

    def row_at(r, n, k, j):
        return pl.ds((r * 8 + PLACE[n]) * UNIT + k * PART + PIECES[j][0], PIECES[j][1])

    def cent_at(n, j):
        return pl.ds(PLACE[n] * CENTS + PIECES[j][0], PIECES[j][1])

    def row_source(r, m, j):
        if m == 0:
            return emb.at[pl.ds(r * PART + PIECES[j][0], PIECES[j][1])]
        return rows.at[row_at(r, m, 0, j)]

    def row_copy(r, w, d, j, m):
        n = m | 1 << d
        return remote(
            row_source(r, m, j), rows.at[row_at(r, n, 0, j)],
            row_send, row_recv.at[r, w], row_peer(1 << d),
        )

    def cent_copy(w, d, j, m):
        n = m | 1 << d
        src, dst = cents.at[cent_at(m, j)], cents.at[cent_at(n, j)]
        return remote(src, dst, cent_send, cent_recv.at[w], cent_peer(1 << d))

    def sib_copy(r, n, j):
        return remote(
            row_source(r, n, j), rows.at[row_at(r, n, 1, j)],
            sib_send, sib_recv.at[r, PLACE[n]], row_peer(0, 1),
        )

    wave = waves()

    def took(sem, *refs):
        for ref in refs:
            pltpu.make_async_copy(ref, ref, sem).wait()

    def row_start(r, w):
        for msg in wave[w]:
            row_copy(r, w, *msg).start()

    def cent_start(w):
        for msg in wave[w]:
            cent_copy(w, *msg).start()

    def row_arrive(r, w):
        took(row_recv.at[r, w], rows.at[pl.ds(0, PART)])
        for d, j, m in wave[w]:
            sib_copy(r, m | 1 << d, j).start()

    def cent_arrive(w):
        took(cent_recv.at[w], cents.at[pl.ds(0, CENTS)])

    def sib_arrive(r, p):
        took(sib_recv.at[r, p], rows.at[pl.ds(0, PART)])

    def squares(half):
        @pl.loop(0, 4)
        def _(i):
            at = pl.ds(pl.multiple_of(half * 512 + i * CENTS, CENTS), CENTS)
            c = cents[at, :].astype(jnp.float32)
            total = jnp.sum(c * c, axis=1, keepdims=True) * (0.5 * ALPHA)
            half_sq[at, :] = jnp.broadcast_to(total, (CENTS, 128))

    def columns(u):
        return pl.ds(pl.multiple_of(u * UNIT, UNIT), UNIT)

    def score(u, blocks, fresh, last=None):
        cols = columns(u)
        top = jnp.full((8, UNIT), -jnp.inf, jnp.float32) if fresh else peak[u]
        if last is not None:
            summed = columns(last)
            high = jnp.max(peak[last], axis=0, keepdims=True)
            total = jnp.zeros((8, UNIT), jnp.float32)
        for i in blocks:
            at = slice(i * 256, (i + 1) * 256)
            product = lax.dot_general(
                cents[at, :], rows[cols, :], NT, preferred_element_type=jnp.float32
            )
            if last is not None:
                step = 1024 // len(blocks)
                first = (i - blocks[0]) * step
                e = jnp.exp2(scores[first : first + step, summed] - high)
                total = total + jnp.sum(e.reshape(step // 8, 8, UNIT), axis=0)
            h = half_sq[at, :]
            t = product * ALPHA - jnp.concatenate([h] * (UNIT // 128), axis=1)
            scores[at, cols] = t
            top = jnp.maximum(top, jnp.max(t.reshape(32, 8, UNIT), axis=0))
        peak[u] = top
        if last is not None:
            settle(last, high, total)

    def settle(u, high, total):
        lse = high + jnp.log2(jnp.sum(total, axis=0, keepdims=True))
        r, p = u // 8, u % 8
        lse_mine[r, 2 * p] = lse[:, :PART]
        lse_mine[r, 2 * p + 1] = lse[:, PART:]

    def soften(u):
        high = jnp.max(peak[u], axis=0, keepdims=True)
        total = jnp.zeros((8, UNIT), jnp.float32)
        for i in range(4):
            e = jnp.exp2(scores[i * 256 : (i + 1) * 256, columns(u)] - high)
            total = total + jnp.sum(e.reshape(32, 8, UNIT), axis=0)
        settle(u, high, total)

    def mirror(s, a):
        return 2 * PLACE[ORDER[s // 2] ^ ORDER[a // 2]] + (s % 2 ^ a % 2)

    def stat_copy(r, a):
        return remote(
            lse_mine.at[r, a], lse_in.at[r, a], stat_send, stat_recv.at[r], slot_peer(a)
        )

    def part_copy(r, a):
        return remote(
            part_mine.at[r], part_in.at[r, a], part_send, part_recv.at[r], slot_peer(a)
        )

    def fin_copy(r, a):
        return remote(
            lse_mine.at[r, pl.ds(EARLY, 16 - EARLY)], fin_in.at[r, a],
            fin_send, fin_recv.at[r], slot_peer(a),
        )

    def count_copy(n):
        return remote(
            count_mine.at[n], count_in.at[n], count_send, count_recv, cent_peer(ORDER[n])
        )

    def settled(u):
        r, p = u // 8, u % 8
        if 2 * p < EARLY:
            for a in (2 * p, 2 * p + 1):
                if a:
                    stat_copy(r, a).start()
        if p == 7:
            for a in range(1, 16):
                fin_copy(r, a).start()
            took(stat_recv.at[r], lse_in.at[r, pl.ds(1, EARLY - 1)])
            part_mine[r] = combine([lse_mine[r, 0]] + [lse_in[r, a] for a in range(1, EARLY)])
            for a in range(1, 16):
                part_copy(r, a).start()

    def agree(r):
        took(part_recv.at[r], part_in.at[r, pl.ds(1, 15)])
        took(fin_recv.at[r], fin_in.at[r, pl.ds(1, 15)])
        for s in range(16):
            terms = [part_mine[r] if s == 0 else part_in[r, s]]
            for q in range(EARLY, 16):
                a = mirror(s, q)
                terms.append(lse_mine[r, q] if a == 0 else fin_in[r, a, q - EARLY])
            lse = combine(terms)
            at = (r * 16 + s) * PART
            lse_all[:, at : at + PART] = lse
            if s == 0:
                norm_out[r * PART : (r + 1) * PART] = (lse * LN2).reshape(PART)

    for w in range(3):
        row_start(0, w)
    own[2].wait()
    cents[0:CENTS, :] = book_in[...].astype(jnp.bfloat16)
    for w in range(3):
        cent_start(w)
    for r in range(2):
        for j in range(N_PIECES):
            sib_copy(r, 0, j).start()
    own[0].wait()
    own[1].wait()
    cent_arrive(0)
    cent_start(3)
    cent_start(4)
    row_arrive(0, 0)
    row_start(0, 3)
    row_start(0, 4)
    cent_arrive(1)
    cent_start(5)
    row_arrive(0, 1)
    row_start(0, 5)
    cent_arrive(2)
    squares(0)
    row_arrive(0, 2)
    cent_arrive(3)
    cent_start(6)
    row_arrive(0, 3)
    row_start(0, 6)
    row_start(1, 0)
    for p in range(4):
        sib_arrive(0, p)

    @pl.loop(0, 4)
    def _(u):
        score(u, (0, 1), True)

    row_arrive(0, 4)
    cent_arrive(4)
    row_arrive(0, 5)
    row_start(1, 1)
    row_start(1, 2)
    cent_arrive(5)
    row_arrive(0, 6)
    cent_arrive(6)
    squares(1)
    score(0, (2, 3), False)

    @pl.loop(1, 4)
    def _(u):
        @pl.when(u == 2)
        def _():
            row_arrive(1, 0)
            row_start(1, 3)
            row_start(1, 4)

        score(u, (2, 3), False, u - 1)
        for v in range(3):
            pl.when(u == v + 1)(functools.partial(settled, v))

    def before(u):
        if u == 5:
            row_arrive(1, 1)
            row_start(1, 5)
        if u == 8:
            row_arrive(1, 2)
        if u == 10:
            row_arrive(1, 3)
            row_start(1, 6)
        if u == 14:
            row_arrive(1, 6)
        sib_arrive(u // 8, u % 8)

    def unit_loop(lo, hi):
        @pl.loop(lo, hi)
        def _(u):
            for v in range(lo, hi):
                pl.when(u == v)(functools.partial(before, v))
            score(u, (0, 1, 2, 3), True, u - 1)
            for v in range(lo, hi):
                pl.when(u == v)(functools.partial(settled, v - 1))

    def weigh(p, r):
        at = pl.ds(pl.multiple_of(p * CENTS, CENTS), CENTS)
        count = tally[p] if r else jnp.zeros((CENTS, 128), jnp.float32)
        total = sums[p] if r else jnp.zeros((CENTS, WIDTH), jnp.float32)
        for i in range(4):
            cols = slice((r * 4 + i) * 2 * UNIT, (r * 4 + i + 1) * 2 * UNIT)
            resp = jnp.exp2(scores[at, cols] - lse_all[:, cols]).astype(jnp.bfloat16)
            wide = resp.astype(jnp.float32)
            for q in range(2 * UNIT // 128):
                count = count + wide[:, q * 128 : (q + 1) * 128]
            total = total + lax.dot_general(
                resp, rows[cols, :], NN, preferred_element_type=jnp.float32
            )
        sums[p] = total
        if r:
            outbox[p] = total.astype(jnp.bfloat16)
            count_mine[p] = jnp.sum(count.T, axis=0, keepdims=True)
        else:
            tally[p] = count

    def step_of(n, j):
        return next(s for s in range(3) if n >> PIECES[j][2][s] & 1)

    def sum_copy(n, j):
        at = pl.ds(*PIECES[j][:2])
        s = step_of(n, j)
        d = PIECES[j][2][s]
        group = 3 if n in (1, 2, 4) else 0 if n == 7 else 1 + s
        box = (inbox1, inbox2, inbox3)[s]
        dst = box.at[0 if s == 2 else PLACE[n ^ 1 << d], at]
        return remote(
            outbox.at[PLACE[n], at], dst, sum_send, sum_recv.at[group], cent_peer(1 << d)
        )

    def gathered(n, j):
        off, size, _ = PIECES[j]
        value = sums[PLACE[n], off : off + size, :]
        for s in range(step_of(n, j) if n else 3):
            box = (inbox1, inbox2, inbox3)[s]
            at = 0 if s == 2 else PLACE[n]
            value = value + box[at, off : off + size, :].astype(jnp.float32)
        return value

    def send_sums(n, step):
        for j in range(N_PIECES):
            if step_of(n, j) == step:
                if step:
                    off, size, _ = PIECES[j]
                    outbox[PLACE[n], off : off + size, :] = gathered(n, j).astype(jnp.bfloat16)
                sum_copy(n, j).start()

    def after(p):
        n = ORDER[p]
        if n:
            send_sums(n, 0)
            count_copy(p).start()
        if p == 4:
            took(sum_recv.at[0], inbox1.at[0])
            for m in (6, 5, 3):
                send_sums(m, 1)
        if p == 1:
            took(sum_recv.at[1], inbox1.at[pl.ds(0, 2)])
            for m in (4, 2, 1):
                send_sums(m, 1)

    unit_loop(4, 12)
    agree(0)

    @pl.loop(0, 3)
    def _(i):
        weigh(7 - i, 0)
        pl.when(i == 0)(functools.partial(row_arrive, 1, 4))

    row_arrive(1, 5)
    unit_loop(12, 16)
    soften(15)
    settled(15)

    @pl.loop(3, 8)
    def _(i):
        weigh(7 - i, 0)

    agree(1)

    @pl.loop(0, 8)
    def _(i):
        weigh(7 - i, 1)
        for p in range(8):
            pl.when(i == 7 - p)(functools.partial(after, p))

    took(sum_recv.at[2], inbox2.at[0])
    for n in (4, 2, 1):
        send_sums(n, 2)

    took(row_send, rows.at[pl.ds(0, 14 * PART)])
    took(sib_send, rows.at[pl.ds(0, 16 * PART)])
    took(cent_send, cents.at[pl.ds(0, 7 * CENTS)])
    for r in range(2):
        took(stat_send, lse_in.at[r, pl.ds(1, EARLY - 1)])
        took(part_send, part_in.at[r, pl.ds(1, 15)])
        took(fin_send, fin_in.at[r, pl.ds(1, 15)])
    took(count_send, count_in.at[pl.ds(1, 7)])
    took(count_recv, count_in.at[pl.ds(1, 7)])
    count = functools.reduce(jnp.add, [count_mine[0]] + [count_in[n] for n in range(1, 8)])
    count_out[...] = count.reshape(CENTS)
    below = jnp.broadcast_to(count, (CENTS, 128)).T + PRIOR
    took(sum_recv.at[3], inbox1.at[pl.ds(0, 3)])
    for j in range(N_PIECES):
        off, size, _ = PIECES[j]
        top = gathered(0, j) + PRIOR * book_in[off : off + size, :]
        for q in range(WIDTH // 128):
            cols = slice(q * 128, (q + 1) * 128)
            new_out[off : off + size, cols] = top[:, cols] / below[off : off + size, :]
    took(sum_send, outbox.at[pl.ds(1, 7)])


def hand_over(*results):
    def body(*refs):
        for i in range(3):
            refs[3 + i][...] = refs[i][...]

    return pl.pallas_call(
        body,
        out_shape=[jax.ShapeDtypeStruct(r.shape, r.dtype) for r in results],
        in_specs=[pl.BlockSpec(memory_space=pltpu.VMEM)] * 3,
        out_specs=[pl.BlockSpec(memory_space=pltpu.VMEM)] * 3,
    )(*results)


def local(embeddings, codebook):
    f32, bf16 = jnp.float32, jnp.bfloat16
    vmem, dma = pltpu.VMEM, pltpu.SemaphoreType.DMA
    new, count, norm = pl.pallas_call(
        kernel,
        out_shape=(
            jax.ShapeDtypeStruct((CENTS, WIDTH), f32),
            jax.ShapeDtypeStruct((CENTS,), f32),
            jax.ShapeDtypeStruct((ROWS,), f32),
        ),
        in_specs=[pl.BlockSpec(memory_space=pl.ANY)] * 2,
        out_specs=[pl.BlockSpec(memory_space=pltpu.VMEM)] * 3,
        scratch_shapes=[
            vmem((16 * UNIT, WIDTH), bf16),
            vmem((8 * CENTS, WIDTH), bf16),
            vmem((8 * CENTS, 16 * UNIT), f32),
            vmem((8 * CENTS, 128), f32),
            vmem((16, 8, UNIT), f32),
            vmem((8, CENTS, WIDTH), f32),
            vmem((8, CENTS, 128), f32),
            vmem((1, 16 * UNIT), f32),
            vmem((2, 16, 1, PART), f32),
            vmem((2, 16, 1, PART), f32),
            vmem((2, 1, PART), f32),
            vmem((2, 16, 1, PART), f32),
            vmem((2, 16, 16 - EARLY, 1, PART), f32),
            vmem((8, 1, CENTS), f32),
            vmem((8, 1, CENTS), f32),
            vmem((8, CENTS, WIDTH), bf16),
            vmem((8, CENTS, WIDTH), bf16),
            vmem((8, CENTS, WIDTH), bf16),
            vmem((1, CENTS, WIDTH), bf16),
            vmem((CENTS, WIDTH), f32),
            dma((3,)),
            dma(()), dma((2, 7)),
            dma(()), dma((2, 8)),
            dma(()), dma((7,)),
            dma(()), dma((2,)),
            dma(()), dma((2,)),
            dma(()), dma((2,)),
            dma(()), dma(()),
            dma(()), dma((4,)),
        ],
        compiler_params=pltpu.CompilerParams(
            collective_id=0, has_side_effects=True, vmem_limit_bytes=58 * 2**20
        ),
        cost_estimate=pl.CostEstimate(
            flops=4 * 4096 * 1024 * 1024, bytes_accessed=2**21, transcendentals=2**23
        ),
    )(embeddings, codebook)
    return hand_over(new, count, norm)


def solution(mesh):
    return jax.shard_map(
        local,
        mesh=mesh,
        in_specs=(P(("dp", "cent"), None), P(("cent", "dp"), None)),
        out_specs=(P(("cent", "dp"), None), P(("cent", "dp")), P(("dp", "cent"))),
        check_vma=False,
    )
```

```python
import functools
import math

import jax
import jax.numpy as jnp
from jax import lax
from jax.experimental import pallas as pl
from jax.experimental.pallas import tpu as pltpu
from jax.sharding import PartitionSpec as P

TEMPER = 0.8
PRIOR = 1.0
ALPHA = math.log2(math.e) / TEMPER
LN2 = math.log(2.0)
MESH = pl.DeviceIdType.MESH

ROWS, CENTS, WIDTH = 256, 128, 1024
PART, UNIT = 128, 256
PIECES = (
    (0, 16, (2, 1, 0)),
    (16, 32, (1, 2, 0)),
    (48, 16, (2, 0, 1)),
    (64, 32, (0, 2, 1)),
    (96, 16, (1, 0, 2)),
    (112, 16, (0, 1, 2)),
)
N_PIECES = len(PIECES)
ORDER = (0, 1, 2, 4, 3, 5, 6, 7)
PLACE = {mask: i for i, mask in enumerate(ORDER)}
EARLY = 8
NT = (((1,), (1,)), ((), ()))
NN = (((1,), (0,)), ((), ()))


def waves():
    wave = [[] for _ in range(7)]
    for j, (_, _, (a, b, c)) in enumerate(PIECES):
        sent = ((a, 0), (b, 0), (c, 0), (b, 1 << a), (c, 1 << a), (c, 1 << b), (c, 1 << a | 1 << b))
        for w, (d, m) in enumerate(sent):
            wave[w].append((d, j, m))
    return wave


def wave_of(j, mask):
    a, b, c = (1 << d for d in PIECES[j][2])
    return (a, b, c, a | b, a | c, b | c, 7).index(mask)


def mask_of(j, w):
    return next(mask for mask in range(1, 8) if wave_of(j, mask) == w)


def mosaic(rows):
    lane = lax.broadcasted_iota(jnp.int32, (1, PART), 1)
    whole = rows[-1]
    for (off, _, _), (end, _, _), row in list(zip(PIECES, PIECES[1:], rows))[::-1]:
        if row is not whole:
            whole = jnp.where((lane >= off) & (lane < end), row, whole)
    return whole


def combine(terms):
    top = functools.reduce(jnp.maximum, terms)
    total = functools.reduce(jnp.add, [jnp.exp2(t - top) for t in terms])
    return top + jnp.log2(total)


def kernel(
    emb, book, new_out, count_out, norm_out,
    rows, cents, scores, half_sq, peak, sums, tally, lse_all,
    lse_unit, lse_mine, lse_in, part_mine, part_in, fin_in, count_mine, count_in,
    outbox, inbox1, inbox2, inbox3,
    book_in, own_sem, row_send, row_recv, sib_send, sib_recv, cent_send, cent_recv,
    stat_send, stat_recv, part_send, part_recv, fin_send, fin_recv,
    count_send, count_recv, sum_send, sum_recv,
):
    dp, cent = lax.axis_index("dp"), lax.axis_index("cent")
    place = (cent // 4, cent % 4, dp // 2)
    core = dp % 2

    def device(p, c):
        return (p[2] * 2 + c, p[0] * 4 + p[1])

    def row_peer(mask, other=0):
        p = [v + 1 - 2 * (v % 2) if mask >> d & 1 else v for d, v in enumerate(place)]
        return device(p, 1 - core if other else core)

    def cent_peer(mask):
        return device([3 - v if mask >> d & 1 else v for d, v in enumerate(place)], core)

    def slot_peer(a):
        return row_peer(ORDER[a // 2], a % 2)

    def remote(src, dst, send, recv, to):
        return pltpu.make_async_remote_copy(
            src_ref=src, dst_ref=dst, send_sem=send, recv_sem=recv,
            device_id=to, device_id_type=MESH,
        )

    barrier = pltpu.get_barrier_semaphore()
    peers = [row_peer(0, 1)] + [row_peer(b) for b in (1, 2, 4)] + [cent_peer(b) for b in (1, 2, 4)]
    for peer in peers:
        pl.semaphore_signal(barrier, inc=1, device_id=peer, device_id_type=MESH)
    own = [
        pltpu.make_async_copy(
            emb.at[pl.ds(r * PART, PART)], rows.at[pl.ds(r * 8 * UNIT, PART)], own_sem.at[r]
        )
        for r in range(2)
    ]
    own.append(pltpu.make_async_copy(book, book_in, own_sem.at[2]))
    own[2].start()
    own[0].start()
    own[1].start()
    pl.semaphore_wait(barrier, len(peers))

    def row_at(r, n, j):
        return pl.ds((r * 8 + 1 + wave_of(j, n)) * UNIT + PIECES[j][0], PIECES[j][1])

    def cent_at(n, j):
        return pl.ds(PLACE[n] * CENTS + PIECES[j][0], PIECES[j][1])

    def row_copy(r, w, d, j, m):
        off, size, _ = PIECES[j]
        src = rows.at[row_at(r, m, j)] if m else emb.at[pl.ds(r * PART + off, size)]
        dst = rows.at[row_at(r, m | 1 << d, j)]
        return remote(src, dst, row_send, row_recv.at[r, w], row_peer(1 << d))

    def cent_copy(w, d, j, m):
        n = m | 1 << d
        src, dst = cents.at[cent_at(m, j)], cents.at[cent_at(n, j)]
        return remote(src, dst, cent_send, cent_recv.at[w], cent_peer(1 << d))

    def sib_copy(r, i):
        at = (r * 8 + i) * UNIT
        src = rows.at[pl.ds(at, PART)] if i else emb.at[pl.ds(r * PART, PART)]
        dst = rows.at[pl.ds(at + PART, PART)]
        return remote(src, dst, sib_send, sib_recv.at[r, i], row_peer(0, 1))

    wave = waves()

    def took(sem, *refs):
        for ref in refs:
            pltpu.make_async_copy(ref, ref, sem).wait()

    def row_start(r, w):
        for msg in wave[w]:
            row_copy(r, w, *msg).start()

    def cent_start(w):
        for msg in wave[w]:
            cent_copy(w, *msg).start()

    def row_arrive(r, w):
        took(row_recv.at[r, w], rows.at[pl.ds(0, PART)])
        sib_copy(r, 1 + w).start()

    def cent_arrive(w):
        took(cent_recv.at[w], cents.at[pl.ds(0, CENTS)])

    def sib_arrive(u):
        took(sib_recv.at[u // 8, u % 8], rows.at[pl.ds(0, PART)])

    def squares(half):
        @pl.loop(0, 4)
        def _(i):
            at = pl.ds(pl.multiple_of(half * 512 + i * CENTS, CENTS), CENTS)
            c = cents[at, :].astype(jnp.float32)
            total = jnp.sum(c * c, axis=1, keepdims=True) * (0.5 * ALPHA)
            half_sq[at, :] = jnp.broadcast_to(total, (CENTS, 128))

    def columns(u):
        return pl.ds(pl.multiple_of(u * UNIT, UNIT), UNIT)

    def score(u, blocks, fresh, last=None):
        cols = columns(u)
        top = jnp.full((8, UNIT), -jnp.inf, jnp.float32) if fresh else peak[u]
        if last is not None:
            summed = columns(last)
            high = jnp.max(peak[last], axis=0, keepdims=True)
            total = jnp.zeros((8, UNIT), jnp.float32)
        for i in blocks:
            at = slice(i * 256, (i + 1) * 256)
            product = lax.dot_general(
                cents[at, :], rows[cols, :], NT, preferred_element_type=jnp.float32
            )
            if last is not None:
                step = 1024 // len(blocks)
                first = (i - blocks[0]) * step
                e = jnp.exp2(scores[first : first + step, summed] - high)
                total = total + jnp.sum(e.reshape(step // 8, 8, UNIT), axis=0)
            h = half_sq[at, :]
            t = product * ALPHA - jnp.concatenate([h] * (UNIT // 128), axis=1)
            scores[at, cols] = t
            top = jnp.maximum(top, jnp.max(t.reshape(32, 8, UNIT), axis=0))
        peak[u] = top
        if last is not None:
            settle(last, high, total)

    def settle(u, high, total):
        lse = high + jnp.log2(jnp.sum(total, axis=0, keepdims=True))
        lse_unit[u, 0] = lse[:, :PART]
        lse_unit[u, 1] = lse[:, PART:]

    def soften(u):
        high = jnp.max(peak[u], axis=0, keepdims=True)
        total = jnp.zeros((8, UNIT), jnp.float32)
        for i in range(4):
            e = jnp.exp2(scores[i * 256 : (i + 1) * 256, columns(u)] - high)
            total = total + jnp.sum(e.reshape(32, 8, UNIT), axis=0)
        settle(u, high, total)

    def mirror(s, a):
        return 2 * PLACE[ORDER[s // 2] ^ ORDER[a // 2]] + (s % 2 ^ a % 2)

    def stat_copy(r, a):
        return remote(
            lse_mine.at[r, a], lse_in.at[r, a], stat_send, stat_recv.at[r], slot_peer(a)
        )

    def part_copy(r, a):
        return remote(
            part_mine.at[r], part_in.at[r, a], part_send, part_recv.at[r], slot_peer(a)
        )

    def fin_copy(r, a):
        return remote(
            lse_mine.at[r, pl.ds(EARLY, 16 - EARLY)], fin_in.at[r, a],
            fin_send, fin_recv.at[r], slot_peer(a),
        )

    def count_copy(n):
        return remote(
            count_mine.at[n], count_in.at[n], count_send, count_recv, cent_peer(ORDER[n])
        )

    def settled(u):
        r, i = u // 8, u % 8
        if i in (3, 7):
            for a in range(0, EARLY) if i == 3 else range(EARLY, 16):
                n, k = ORDER[a // 2], a % 2
                units = [r * 8 + (1 + wave_of(j, n) if n else 0) for j in range(N_PIECES)]
                known = {v: lse_unit[v, k] for v in set(units)}
                lse_mine[r, a] = mosaic([known[v] for v in units])
        if i == 3:
            for a in range(1, EARLY):
                stat_copy(r, a).start()
        if i == 7:
            for a in range(1, 16):
                fin_copy(r, a).start()
            took(stat_recv.at[r], lse_in.at[r, pl.ds(1, EARLY - 1)])
            part_mine[r] = combine([lse_mine[r, 0]] + [lse_in[r, a] for a in range(1, EARLY)])
            for a in range(1, 16):
                part_copy(r, a).start()

    def agree(r):
        took(part_recv.at[r], part_in.at[r, pl.ds(1, 15)])
        took(fin_recv.at[r], fin_in.at[r, pl.ds(1, 15)])
        agreed = []
        for s in range(16):
            terms = [part_mine[r] if s == 0 else part_in[r, s]]
            for q in range(EARLY, 16):
                a = mirror(s, q)
                terms.append(lse_mine[r, q] if a == 0 else fin_in[r, a, q - EARLY])
            agreed.append(combine(terms))
        norm_out[r * PART : (r + 1) * PART] = (agreed[0] * LN2).reshape(PART)
        for i in range(8):
            masks = [mask_of(j, i - 1) if i else 0 for j in range(N_PIECES)]
            for k in range(2):
                at = (r * 8 + i) * UNIT + k * PART
                lse_all[:, at : at + PART] = mosaic([agreed[2 * PLACE[n] + k] for n in masks])

    def weigh(p, r):
        at = pl.ds(pl.multiple_of(p * CENTS, CENTS), CENTS)
        count = tally[p] if r else jnp.zeros((CENTS, 128), jnp.float32)
        total = sums[p] if r else jnp.zeros((CENTS, WIDTH), jnp.float32)
        for i in range(4):
            cols = slice((r * 4 + i) * 2 * UNIT, (r * 4 + i + 1) * 2 * UNIT)
            resp = jnp.exp2(scores[at, cols] - lse_all[:, cols]).astype(jnp.bfloat16)
            wide = resp.astype(jnp.float32)
            for q in range(2 * UNIT // 128):
                count = count + wide[:, q * 128 : (q + 1) * 128]
            total = total + lax.dot_general(
                resp, rows[cols, :], NN, preferred_element_type=jnp.float32
            )
        sums[p] = total
        if r:
            outbox[p] = total.astype(jnp.bfloat16)
            count_mine[p] = jnp.sum(count.T, axis=0, keepdims=True)
        else:
            tally[p] = count

    for w in range(3):
        row_start(0, w)
    own[2].wait()
    cents[0:CENTS, :] = book_in[...].astype(jnp.bfloat16)
    for w in range(3):
        cent_start(w)
    sib_copy(0, 0).start()
    sib_copy(1, 0).start()
    own[0].wait()
    own[1].wait()
    cent_arrive(0)
    cent_start(3)
    cent_start(4)
    row_arrive(0, 0)
    row_start(0, 3)
    row_start(0, 4)
    cent_arrive(1)
    cent_start(5)
    row_arrive(0, 1)
    row_start(0, 5)
    cent_arrive(2)
    squares(0)
    row_arrive(0, 2)

    first = (0, 8, 1, 2, 3, 4, 5, 6)

    def first_unit(i):
        return jnp.where(i == 0, 0, jnp.where(i == 1, 8, i - 1))

    def before_first(i):
        if i == 5:
            cent_arrive(3)
            cent_start(6)
            row_arrive(0, 3)
            row_start(0, 6)
            row_start(1, 0)
        if i == 6:
            row_arrive(0, 4)
            cent_arrive(4)
        if i == 7:
            row_arrive(0, 5)
            row_start(1, 1)
            row_start(1, 2)
            cent_arrive(5)
        sib_arrive(first[i])

    @pl.loop(0, 8)
    def _(i):
        for v in range(8):
            pl.when(i == v)(functools.partial(before_first, v))
        score(first_unit(i), (0, 1), True)

    row_arrive(0, 6)
    cent_arrive(6)
    squares(1)
    score(0, (2, 3), False)

    @pl.loop(1, 8)
    def _(i):
        @pl.when(i == 3)
        def _():
            row_arrive(1, 0)
            row_start(1, 3)
            row_start(1, 4)

        score(first_unit(i), (2, 3), False, first_unit(i - 1))
        pl.when(i == 5)(functools.partial(settled, 3))

    def before_full(i):
        if i == 2:
            row_arrive(1, 1)
            row_start(1, 5)
        if i == 3:
            row_arrive(1, 2)
        if i == 4:
            row_arrive(1, 3)
            row_start(1, 6)
            agree(0)
        if i > 4:
            row_arrive(1, i - 1)

    @pl.loop(0, 8)
    def _(i):
        for v in range(2, 8):
            pl.when(i == v)(functools.partial(before_full, v))
        pl.when(i > 4)(lambda: weigh(12 - i, 0))
        for v in range(8):
            pl.when(i == v)(functools.partial(sib_arrive, v + 8 if v else 7))
        last = jnp.where(i == 0, 6, jnp.where(i == 1, 7, 7 + i))
        score(jnp.where(i == 0, 7, 8 + i), (0, 1, 2, 3), True, last)
        pl.when(i == 1)(functools.partial(settled, 7))
        pl.when(i == 4)(functools.partial(settled, 11))

    soften(15)
    settled(15)

    def step_of(n, j):
        return next(s for s in range(3) if n >> PIECES[j][2][s] & 1)

    def sum_copy(n, j):
        at = pl.ds(*PIECES[j][:2])
        s = step_of(n, j)
        d = PIECES[j][2][s]
        group = 3 if n in (1, 2, 4) else 0 if n == 7 else 1 + s
        box = (inbox1, inbox2, inbox3)[s]
        dst = box.at[0 if s == 2 else PLACE[n ^ 1 << d], at]
        return remote(
            outbox.at[PLACE[n], at], dst, sum_send, sum_recv.at[group], cent_peer(1 << d)
        )

    def gathered(n, j):
        off, size, _ = PIECES[j]
        value = sums[PLACE[n], off : off + size, :]
        for s in range(step_of(n, j) if n else 3):
            box = (inbox1, inbox2, inbox3)[s]
            at = 0 if s == 2 else PLACE[n]
            value = value + box[at, off : off + size, :].astype(jnp.float32)
        return value

    def send_sums(n, step):
        for j in range(N_PIECES):
            if step_of(n, j) == step:
                if step:
                    off, size, _ = PIECES[j]
                    outbox[PLACE[n], off : off + size, :] = gathered(n, j).astype(jnp.bfloat16)
                sum_copy(n, j).start()

    def after(p):
        n = ORDER[p]
        if n:
            send_sums(n, 0)
            count_copy(p).start()
        if p == 4:
            took(sum_recv.at[0], inbox1.at[0])
            for m in (6, 5, 3):
                send_sums(m, 1)
        if p == 1:
            took(sum_recv.at[1], inbox1.at[pl.ds(0, 2)])
            for m in (4, 2, 1):
                send_sums(m, 1)

    @pl.loop(3, 8)
    def _(i):
        weigh(7 - i, 0)

    agree(1)

    @pl.loop(0, 8)
    def _(i):
        weigh(7 - i, 1)
        for p in range(8):
            pl.when(i == 7 - p)(functools.partial(after, p))

    took(sum_recv.at[2], inbox2.at[0])
    for n in (4, 2, 1):
        send_sums(n, 2)

    took(row_send, rows.at[pl.ds(0, 14 * PART)])
    took(sib_send, rows.at[pl.ds(0, 16 * PART)])
    took(cent_send, cents.at[pl.ds(0, 7 * CENTS)])
    for r in range(2):
        took(stat_send, lse_in.at[r, pl.ds(1, EARLY - 1)])
        took(part_send, part_in.at[r, pl.ds(1, 15)])
        took(fin_send, fin_in.at[r, pl.ds(1, 15)])
    took(count_send, count_in.at[pl.ds(1, 7)])
    took(count_recv, count_in.at[pl.ds(1, 7)])
    count = functools.reduce(jnp.add, [count_mine[0]] + [count_in[n] for n in range(1, 8)])
    count_out[...] = count.reshape(CENTS)
    below = jnp.broadcast_to(count, (CENTS, 128)).T + PRIOR
    took(sum_recv.at[3], inbox1.at[pl.ds(0, 3)])
    for j in range(N_PIECES):
        off, size, _ = PIECES[j]
        top = gathered(0, j) + PRIOR * book_in[off : off + size, :]
        for q in range(WIDTH // 128):
            cols = slice(q * 128, (q + 1) * 128)
            new_out[off : off + size, cols] = top[:, cols] / below[off : off + size, :]
    took(sum_send, outbox.at[pl.ds(1, 7)])


def hand_over(*results):
    def body(*refs):
        for i in range(3):
            refs[3 + i][...] = refs[i][...]

    return pl.pallas_call(
        body,
        out_shape=[jax.ShapeDtypeStruct(r.shape, r.dtype) for r in results],
        in_specs=[pl.BlockSpec(memory_space=pltpu.VMEM)] * 3,
        out_specs=[pl.BlockSpec(memory_space=pltpu.VMEM)] * 3,
    )(*results)


def local(embeddings, codebook):
    f32, bf16 = jnp.float32, jnp.bfloat16
    vmem, dma = pltpu.VMEM, pltpu.SemaphoreType.DMA
    new, count, norm = pl.pallas_call(
        kernel,
        out_shape=(
            jax.ShapeDtypeStruct((CENTS, WIDTH), f32),
            jax.ShapeDtypeStruct((CENTS,), f32),
            jax.ShapeDtypeStruct((ROWS,), f32),
        ),
        in_specs=[pl.BlockSpec(memory_space=pl.ANY)] * 2,
        out_specs=[pl.BlockSpec(memory_space=pltpu.VMEM)] * 3,
        scratch_shapes=[
            vmem((16 * UNIT, WIDTH), bf16),
            vmem((8 * CENTS, WIDTH), bf16),
            vmem((8 * CENTS, 16 * UNIT), f32),
            vmem((8 * CENTS, 128), f32),
            vmem((16, 8, UNIT), f32),
            vmem((8, CENTS, WIDTH), f32),
            vmem((8, CENTS, 128), f32),
            vmem((1, 16 * UNIT), f32),
            vmem((16, 2, 1, PART), f32),
            vmem((2, 16, 1, PART), f32),
            vmem((2, 16, 1, PART), f32),
            vmem((2, 1, PART), f32),
            vmem((2, 16, 1, PART), f32),
            vmem((2, 16, 16 - EARLY, 1, PART), f32),
            vmem((8, 1, CENTS), f32),
            vmem((8, 1, CENTS), f32),
            vmem((8, CENTS, WIDTH), bf16),
            vmem((8, CENTS, WIDTH), bf16),
            vmem((8, CENTS, WIDTH), bf16),
            vmem((1, CENTS, WIDTH), bf16),
            vmem((CENTS, WIDTH), f32),
            dma((3,)),
            dma(()), dma((2, 7)),
            dma(()), dma((2, 8)),
            dma(()), dma((7,)),
            dma(()), dma((2,)),
            dma(()), dma((2,)),
            dma(()), dma((2,)),
            dma(()), dma(()),
            dma(()), dma((4,)),
        ],
        compiler_params=pltpu.CompilerParams(
            collective_id=0, has_side_effects=True, vmem_limit_bytes=58 * 2**20
        ),
        cost_estimate=pl.CostEstimate(
            flops=4 * 4096 * 1024 * 1024, bytes_accessed=2**21, transcendentals=2**23
        ),
    )(embeddings, codebook)
    return hand_over(new, count, norm)


def solution(mesh):
    return jax.shard_map(
        local,
        mesh=mesh,
        in_specs=(P(("dp", "cent"), None), P(("cent", "dp"), None)),
        out_specs=(P(("cent", "dp"), None), P(("cent", "dp")), P(("dp", "cent"))),
        check_vma=False,
    )
```

```python
import functools
import math

import jax
import jax.numpy as jnp
from jax import lax
from jax.experimental import pallas as pl
from jax.experimental.pallas import tpu as pltpu
from jax.sharding import PartitionSpec as P

TEMPER = 0.8
PRIOR = 1.0
ALPHA = math.log2(math.e) / TEMPER
LN2 = math.log(2.0)
MESH = pl.DeviceIdType.MESH

ROWS, CENTS, WIDTH = 256, 128, 1024
PART, UNIT = 128, 256
PIECES = (
    (0, 16, (2, 1, 0)),
    (16, 32, (1, 2, 0)),
    (48, 16, (2, 0, 1)),
    (64, 32, (0, 2, 1)),
    (96, 16, (1, 0, 2)),
    (112, 16, (0, 1, 2)),
)
N_PIECES = len(PIECES)
ORDER = (0, 1, 2, 4, 3, 5, 6, 7)
PLACE = {mask: i for i, mask in enumerate(ORDER)}
EARLY = 8
NT = (((1,), (1,)), ((), ()))
NN = (((1,), (0,)), ((), ()))


def waves():
    wave = [[] for _ in range(7)]
    for j, (_, _, (a, b, c)) in enumerate(PIECES):
        sent = ((a, 0), (b, 0), (c, 0), (b, 1 << a), (c, 1 << a), (c, 1 << b), (c, 1 << a | 1 << b))
        for w, (d, m) in enumerate(sent):
            wave[w].append((d, j, m))
    return wave


def wave_of(j, mask):
    a, b, c = (1 << d for d in PIECES[j][2])
    return (a, b, c, a | b, a | c, b | c, 7).index(mask)


def mask_of(j, w):
    return next(mask for mask in range(1, 8) if wave_of(j, mask) == w)


def mosaic(rows):
    lane = lax.broadcasted_iota(jnp.int32, (1, PART), 1)
    whole = rows[-1]
    for (off, _, _), (end, _, _), row in list(zip(PIECES, PIECES[1:], rows))[::-1]:
        if row is not whole:
            whole = jnp.where((lane >= off) & (lane < end), row, whole)
    return whole


def combine(terms):
    top = functools.reduce(jnp.maximum, terms)
    total = functools.reduce(jnp.add, [jnp.exp2(t - top) for t in terms])
    return top + jnp.log2(total)


def kernel(
    emb, book, new_out, count_out, norm_out,
    rows, cents, scores, half_sq, peak, sums, tally, lse_all,
    lse_unit, lse_mine, lse_in, part_mine, part_in, fin_in, count_mine, count_in,
    outbox, inbox1, inbox2, inbox3,
    book_in, own_sem, row_send, row_recv, sib_send, sib_recv, cent_send, cent_recv,
    stat_send, stat_recv, part_send, part_recv, fin_send, fin_recv,
    count_send, count_recv, sum_send, sum_recv,
):
    dp, cent = lax.axis_index("dp"), lax.axis_index("cent")
    place = (cent // 4, cent % 4, dp // 2)
    core = dp % 2

    def device(p, c):
        return (p[2] * 2 + c, p[0] * 4 + p[1])

    def row_peer(mask, other=0):
        p = [v + 1 - 2 * (v % 2) if mask >> d & 1 else v for d, v in enumerate(place)]
        return device(p, 1 - core if other else core)

    def cent_peer(mask):
        return device([3 - v if mask >> d & 1 else v for d, v in enumerate(place)], core)

    def slot_peer(a):
        return row_peer(ORDER[a // 2], a % 2)

    def remote(src, dst, send, recv, to):
        return pltpu.make_async_remote_copy(
            src_ref=src, dst_ref=dst, send_sem=send, recv_sem=recv,
            device_id=to, device_id_type=MESH,
        )

    barrier = pltpu.get_barrier_semaphore()
    peers = [row_peer(0, 1)] + [row_peer(b) for b in (1, 2, 4)] + [cent_peer(b) for b in (1, 2, 4)]
    for peer in peers:
        pl.semaphore_signal(barrier, inc=1, device_id=peer, device_id_type=MESH)
    own = [
        pltpu.make_async_copy(
            emb.at[pl.ds(r * PART, PART)], rows.at[pl.ds(r * 8 * UNIT, PART)], own_sem.at[r]
        )
        for r in range(2)
    ]
    own.append(pltpu.make_async_copy(book, book_in, own_sem.at[2]))
    own[2].start()
    own[0].start()
    own[1].start()
    pl.semaphore_wait(barrier, len(peers))

    def row_at(r, n, j):
        return pl.ds((r * 8 + 1 + wave_of(j, n)) * UNIT + PIECES[j][0], PIECES[j][1])

    def cent_at(n, j):
        return pl.ds(PLACE[n] * CENTS + PIECES[j][0], PIECES[j][1])

    def row_copy(r, w, d, j, m):
        off, size, _ = PIECES[j]
        src = rows.at[row_at(r, m, j)] if m else emb.at[pl.ds(r * PART + off, size)]
        dst = rows.at[row_at(r, m | 1 << d, j)]
        return remote(src, dst, row_send, row_recv.at[r, w], row_peer(1 << d))

    def cent_copy(w, d, j, m):
        n = m | 1 << d
        src, dst = cents.at[cent_at(m, j)], cents.at[cent_at(n, j)]
        return remote(src, dst, cent_send, cent_recv.at[w], cent_peer(1 << d))

    def sib_copy(r, i):
        at = (r * 8 + i) * UNIT
        src = rows.at[pl.ds(at, PART)] if i else emb.at[pl.ds(r * PART, PART)]
        dst = rows.at[pl.ds(at + PART, PART)]
        return remote(src, dst, sib_send, sib_recv.at[r, i], row_peer(0, 1))

    wave = waves()

    def took(sem, *refs):
        for ref in refs:
            pltpu.make_async_copy(ref, ref, sem).wait()

    def row_start(r, w):
        for msg in wave[w]:
            row_copy(r, w, *msg).start()

    def cent_start(w):
        for msg in wave[w]:
            cent_copy(w, *msg).start()

    def row_arrive(r, w):
        took(row_recv.at[r, w], rows.at[pl.ds(0, PART)])
        sib_copy(r, 1 + w).start()

    def cent_arrive(w):
        took(cent_recv.at[w], cents.at[pl.ds(0, CENTS)])

    def sib_arrive(u):
        took(sib_recv.at[u // 8, u % 8], rows.at[pl.ds(0, PART)])

    def squares(half):
        @pl.loop(0, 4)
        def _(i):
            at = pl.ds(pl.multiple_of(half * 512 + i * CENTS, CENTS), CENTS)
            c = cents[at, :].astype(jnp.float32)
            total = jnp.sum(c * c, axis=1, keepdims=True) * (0.5 * ALPHA)
            half_sq[at, :] = jnp.broadcast_to(total, (CENTS, 128))

    def columns(u):
        return pl.ds(pl.multiple_of(u * UNIT, UNIT), UNIT)

    def score(u, blocks, fresh, last=None):
        cols = columns(u)
        top = jnp.full((8, UNIT), -jnp.inf, jnp.float32) if fresh else peak[u]
        if last is not None:
            summed = columns(last)
            high = jnp.max(peak[last], axis=0, keepdims=True)
            total = jnp.zeros((8, UNIT), jnp.float32)
        for i in blocks:
            at = slice(i * 256, (i + 1) * 256)
            product = lax.dot_general(
                cents[at, :], rows[cols, :], NT, preferred_element_type=jnp.float32
            )
            if last is not None:
                step = 1024 // len(blocks)
                first = (i - blocks[0]) * step
                e = jnp.exp2(scores[first : first + step, summed] - high)
                total = total + jnp.sum(e.reshape(step // 8, 8, UNIT), axis=0)
            h = half_sq[at, :]
            t = product * ALPHA - jnp.concatenate([h] * (UNIT // 128), axis=1)
            scores[at, cols] = t
            top = jnp.maximum(top, jnp.max(t.reshape(32, 8, UNIT), axis=0))
        peak[u] = top
        if last is not None:
            settle(last, high, total)

    def settle(u, high, total):
        lse = high + jnp.log2(jnp.sum(total, axis=0, keepdims=True))
        lse_unit[u, 0] = lse[:, :PART]
        lse_unit[u, 1] = lse[:, PART:]

    def soften(u):
        high = jnp.max(peak[u], axis=0, keepdims=True)
        total = jnp.zeros((8, UNIT), jnp.float32)
        for i in range(4):
            e = jnp.exp2(scores[i * 256 : (i + 1) * 256, columns(u)] - high)
            total = total + jnp.sum(e.reshape(32, 8, UNIT), axis=0)
        settle(u, high, total)

    def mirror(s, a):
        return 2 * PLACE[ORDER[s // 2] ^ ORDER[a // 2]] + (s % 2 ^ a % 2)

    def stat_copy(r, a):
        return remote(
            lse_mine.at[r, a], lse_in.at[r, a], stat_send, stat_recv.at[r], slot_peer(a)
        )

    def part_copy(r, a):
        return remote(
            part_mine.at[r], part_in.at[r, a], part_send, part_recv.at[r], slot_peer(a)
        )

    def fin_copy(r, a):
        return remote(
            lse_mine.at[r, pl.ds(EARLY, 16 - EARLY)], fin_in.at[r, a],
            fin_send, fin_recv.at[r], slot_peer(a),
        )

    def count_copy(n):
        return remote(
            count_mine.at[n], count_in.at[n], count_send, count_recv, cent_peer(ORDER[n])
        )

    def settled(u):
        r, i = u // 8, u % 8
        if i in (3, 7):
            for a in range(0, EARLY) if i == 3 else range(EARLY, 16):
                n, k = ORDER[a // 2], a % 2
                units = [r * 8 + (1 + wave_of(j, n) if n else 0) for j in range(N_PIECES)]
                known = {v: lse_unit[v, k] for v in set(units)}
                lse_mine[r, a] = mosaic([known[v] for v in units])
        if i == 3:
            for a in range(1, EARLY):
                stat_copy(r, a).start()
        if i == 7:
            for a in range(1, 16):
                fin_copy(r, a).start()
            took(stat_recv.at[r], lse_in.at[r, pl.ds(1, EARLY - 1)])
            part_mine[r] = combine([lse_mine[r, 0]] + [lse_in[r, a] for a in range(1, EARLY)])
            for a in range(1, 16):
                part_copy(r, a).start()

    def agree(r):
        took(part_recv.at[r], part_in.at[r, pl.ds(1, 15)])
        took(fin_recv.at[r], fin_in.at[r, pl.ds(1, 15)])
        agreed = []
        for s in range(16):
            terms = [part_mine[r] if s == 0 else part_in[r, s]]
            for q in range(EARLY, 16):
                a = mirror(s, q)
                terms.append(lse_mine[r, q] if a == 0 else fin_in[r, a, q - EARLY])
            agreed.append(combine(terms))
        norm_out[r * PART : (r + 1) * PART] = (agreed[0] * LN2).reshape(PART)
        for i in range(8):
            masks = [mask_of(j, i - 1) if i else 0 for j in range(N_PIECES)]
            for k in range(2):
                at = (r * 8 + i) * UNIT + k * PART
                lse_all[:, at : at + PART] = mosaic([agreed[2 * PLACE[n] + k] for n in masks])

    def weigh(p, r):
        at = pl.ds(pl.multiple_of(p * CENTS, CENTS), CENTS)
        count = tally[p] if r else jnp.zeros((CENTS, 128), jnp.float32)
        total = sums[p] if r else jnp.zeros((CENTS, WIDTH), jnp.float32)
        for i in range(4):
            cols = slice((r * 4 + i) * 2 * UNIT, (r * 4 + i + 1) * 2 * UNIT)
            resp = jnp.exp2(scores[at, cols] - lse_all[:, cols]).astype(jnp.bfloat16)
            wide = resp.astype(jnp.float32)
            for q in range(2 * UNIT // 128):
                count = count + wide[:, q * 128 : (q + 1) * 128]
            total = total + lax.dot_general(
                resp, rows[cols, :], NN, preferred_element_type=jnp.float32
            )
        sums[p] = total
        if r:
            outbox[p] = total.astype(jnp.bfloat16)
            count_mine[p] = jnp.sum(count.T, axis=0, keepdims=True)
        else:
            tally[p] = count

    for w in range(3):
        row_start(0, w)
    own[2].wait()
    cents[0:CENTS, :] = book_in[...].astype(jnp.bfloat16)
    for w in range(3):
        cent_start(w)
    sib_copy(0, 0).start()
    sib_copy(1, 0).start()
    own[0].wait()
    own[1].wait()
    cent_arrive(0)
    cent_start(3)
    cent_start(4)
    row_arrive(0, 0)
    row_start(0, 3)
    row_start(0, 4)
    cent_arrive(1)
    cent_start(5)
    row_arrive(0, 1)
    row_start(0, 5)
    cent_arrive(2)
    squares(0)
    row_arrive(0, 2)

    first = (0, 8, 1, 2, 3, 4, 5, 6)

    def first_unit(i):
        return jnp.where(i == 0, 0, jnp.where(i == 1, 8, i - 1))

    def before_first(i):
        if i == 4:
            cent_arrive(3)
            cent_start(6)
            row_arrive(0, 3)
            row_start(0, 6)
            row_start(1, 0)
        if i == 5:
            row_arrive(0, 4)
            cent_arrive(4)
        if i == 6:
            row_arrive(0, 5)
            row_start(1, 1)
            row_start(1, 2)
            cent_arrive(5)
        if i == 7:
            row_arrive(0, 6)
        sib_arrive(first[i])

    @pl.loop(0, 8)
    def _(i):
        for v in range(8):
            pl.when(i == v)(functools.partial(before_first, v))
        score(first_unit(i), (0, 1), True)

    cent_arrive(6)
    squares(1)
    score(0, (2, 3), False)

    @pl.loop(1, 8)
    def _(i):
        @pl.when(i == 3)
        def _():
            row_arrive(1, 0)
            row_start(1, 3)
            row_start(1, 4)

        score(first_unit(i), (2, 3), False, first_unit(i - 1))
        pl.when(i == 5)(functools.partial(settled, 3))

    def before_full(i):
        if i == 1:
            row_arrive(1, 1)
            row_start(1, 5)
        if i == 2:
            row_arrive(1, 2)
        if i == 3:
            row_arrive(1, 3)
            row_start(1, 6)
        if i == 5:
            agree(0)
        if i in (5, 6):
            weigh(12 - i, 0)
        if i in (4, 5, 6):
            row_arrive(1, i)
        sib_arrive(i + 8 if i else 7)

    @pl.loop(0, 8)
    def _(i):
        for v in range(8):
            pl.when(i == v)(functools.partial(before_full, v))
        last = jnp.where(i == 0, 6, jnp.where(i == 1, 7, 7 + i))
        score(jnp.where(i == 0, 7, 8 + i), (0, 1, 2, 3), True, last)
        pl.when(i == 1)(functools.partial(settled, 7))
        pl.when(i == 4)(functools.partial(settled, 11))

    soften(15)
    settled(15)

    def step_of(n, j):
        return next(s for s in range(3) if n >> PIECES[j][2][s] & 1)

    def sum_copy(n, j):
        at = pl.ds(*PIECES[j][:2])
        s = step_of(n, j)
        d = PIECES[j][2][s]
        group = 3 if n in (1, 2, 4) else 0 if n == 7 else 1 + s
        box = (inbox1, inbox2, inbox3)[s]
        dst = box.at[0 if s == 2 else PLACE[n ^ 1 << d], at]
        return remote(
            outbox.at[PLACE[n], at], dst, sum_send, sum_recv.at[group], cent_peer(1 << d)
        )

    def gathered(n, j):
        off, size, _ = PIECES[j]
        value = sums[PLACE[n], off : off + size, :]
        for s in range(step_of(n, j) if n else 3):
            box = (inbox1, inbox2, inbox3)[s]
            at = 0 if s == 2 else PLACE[n]
            value = value + box[at, off : off + size, :].astype(jnp.float32)
        return value

    def send_sums(n, step):
        for j in range(N_PIECES):
            if step_of(n, j) == step:
                if step:
                    off, size, _ = PIECES[j]
                    outbox[PLACE[n], off : off + size, :] = gathered(n, j).astype(jnp.bfloat16)
                sum_copy(n, j).start()

    def after(p):
        n = ORDER[p]
        if n:
            send_sums(n, 0)
            count_copy(p).start()
        if p == 4:
            took(sum_recv.at[0], inbox1.at[0])
            for m in (6, 5, 3):
                send_sums(m, 1)
        if p == 1:
            took(sum_recv.at[1], inbox1.at[pl.ds(0, 2)])
            for m in (4, 2, 1):
                send_sums(m, 1)

    @pl.loop(2, 8)
    def _(i):
        weigh(7 - i, 0)

    agree(1)

    @pl.loop(0, 8)
    def _(i):
        weigh(7 - i, 1)
        for p in range(8):
            pl.when(i == 7 - p)(functools.partial(after, p))

    took(sum_recv.at[2], inbox2.at[0])
    for n in (4, 2, 1):
        send_sums(n, 2)

    took(row_send, rows.at[pl.ds(0, 14 * PART)])
    took(sib_send, rows.at[pl.ds(0, 16 * PART)])
    took(cent_send, cents.at[pl.ds(0, 7 * CENTS)])
    for r in range(2):
        took(stat_send, lse_in.at[r, pl.ds(1, EARLY - 1)])
        took(part_send, part_in.at[r, pl.ds(1, 15)])
        took(fin_send, fin_in.at[r, pl.ds(1, 15)])
    took(count_send, count_in.at[pl.ds(1, 7)])
    took(count_recv, count_in.at[pl.ds(1, 7)])
    count = functools.reduce(jnp.add, [count_mine[0]] + [count_in[n] for n in range(1, 8)])
    count_out[...] = count.reshape(CENTS)
    below = jnp.broadcast_to(count, (CENTS, 128)).T + PRIOR
    took(sum_recv.at[3], inbox1.at[pl.ds(0, 3)])
    for j in range(N_PIECES):
        off, size, _ = PIECES[j]
        top = gathered(0, j) + PRIOR * book_in[off : off + size, :]
        for q in range(WIDTH // 128):
            cols = slice(q * 128, (q + 1) * 128)
            new_out[off : off + size, cols] = top[:, cols] / below[off : off + size, :]
    took(sum_send, outbox.at[pl.ds(1, 7)])


def hand_over(*results):
    def body(*refs):
        for i in range(3):
            refs[3 + i][...] = refs[i][...]

    return pl.pallas_call(
        body,
        out_shape=[jax.ShapeDtypeStruct(r.shape, r.dtype) for r in results],
        in_specs=[pl.BlockSpec(memory_space=pltpu.VMEM)] * 3,
        out_specs=[pl.BlockSpec(memory_space=pltpu.VMEM)] * 3,
    )(*results)


def local(embeddings, codebook):
    f32, bf16 = jnp.float32, jnp.bfloat16
    vmem, dma = pltpu.VMEM, pltpu.SemaphoreType.DMA
    new, count, norm = pl.pallas_call(
        kernel,
        out_shape=(
            jax.ShapeDtypeStruct((CENTS, WIDTH), f32),
            jax.ShapeDtypeStruct((CENTS,), f32),
            jax.ShapeDtypeStruct((ROWS,), f32),
        ),
        in_specs=[pl.BlockSpec(memory_space=pl.ANY)] * 2,
        out_specs=[pl.BlockSpec(memory_space=pltpu.VMEM)] * 3,
        scratch_shapes=[
            vmem((16 * UNIT, WIDTH), bf16),
            vmem((8 * CENTS, WIDTH), bf16),
            vmem((8 * CENTS, 16 * UNIT), f32),
            vmem((8 * CENTS, 128), f32),
            vmem((16, 8, UNIT), f32),
            vmem((8, CENTS, WIDTH), f32),
            vmem((8, CENTS, 128), f32),
            vmem((1, 16 * UNIT), f32),
            vmem((16, 2, 1, PART), f32),
            vmem((2, 16, 1, PART), f32),
            vmem((2, 16, 1, PART), f32),
            vmem((2, 1, PART), f32),
            vmem((2, 16, 1, PART), f32),
            vmem((2, 16, 16 - EARLY, 1, PART), f32),
            vmem((8, 1, CENTS), f32),
            vmem((8, 1, CENTS), f32),
            vmem((8, CENTS, WIDTH), bf16),
            vmem((8, CENTS, WIDTH), bf16),
            vmem((8, CENTS, WIDTH), bf16),
            vmem((1, CENTS, WIDTH), bf16),
            vmem((CENTS, WIDTH), f32),
            dma((3,)),
            dma(()), dma((2, 7)),
            dma(()), dma((2, 8)),
            dma(()), dma((7,)),
            dma(()), dma((2,)),
            dma(()), dma((2,)),
            dma(()), dma((2,)),
            dma(()), dma(()),
            dma(()), dma((4,)),
        ],
        compiler_params=pltpu.CompilerParams(
            collective_id=0, has_side_effects=True, vmem_limit_bytes=58 * 2**20
        ),
        cost_estimate=pl.CostEstimate(
            flops=4 * 4096 * 1024 * 1024, bytes_accessed=2**21, transcendentals=2**23
        ),
    )(embeddings, codebook)
    return hand_over(new, count, norm)


def solution(mesh):
    return jax.shard_map(
        local,
        mesh=mesh,
        in_specs=(P(("dp", "cent"), None), P(("cent", "dp"), None)),
        out_specs=(P(("cent", "dp"), None), P(("cent", "dp")), P(("dp", "cent"))),
        check_vma=False,
    )
```

```python
import functools
import math

import jax
import jax.numpy as jnp
from jax import lax
from jax.experimental import pallas as pl
from jax.experimental.pallas import tpu as pltpu
from jax.sharding import PartitionSpec as P

TEMPER = 0.8
PRIOR = 1.0
ALPHA = math.log2(math.e) / TEMPER
LN2 = math.log(2.0)
MESH = pl.DeviceIdType.MESH

ROWS, CENTS, WIDTH = 256, 128, 1024
PART, UNIT = 128, 256
PIECES = (
    (0, 16, (2, 1, 0)),
    (16, 32, (1, 2, 0)),
    (48, 16, (2, 0, 1)),
    (64, 32, (0, 2, 1)),
    (96, 16, (1, 0, 2)),
    (112, 16, (0, 1, 2)),
)
N_PIECES = len(PIECES)
ORDER = (0, 1, 2, 4, 3, 5, 6, 7)
PLACE = {mask: i for i, mask in enumerate(ORDER)}
EARLY = 8
NT = (((1,), (1,)), ((), ()))
NN = (((1,), (0,)), ((), ()))


def waves():
    wave = [[] for _ in range(7)]
    for j, (_, _, (a, b, c)) in enumerate(PIECES):
        sent = ((a, 0), (b, 0), (c, 0), (b, 1 << a), (c, 1 << a), (c, 1 << b), (c, 1 << a | 1 << b))
        for w, (d, m) in enumerate(sent):
            wave[w].append((d, j, m))
    return wave


def wave_of(j, mask):
    a, b, c = (1 << d for d in PIECES[j][2])
    return (a, b, c, a | b, a | c, b | c, 7).index(mask)


def mask_of(j, w):
    return next(mask for mask in range(1, 8) if wave_of(j, mask) == w)


def mosaic(rows):
    lane = lax.broadcasted_iota(jnp.int32, (1, PART), 1)
    whole = rows[-1]
    for (off, _, _), (end, _, _), row in list(zip(PIECES, PIECES[1:], rows))[::-1]:
        if row is not whole:
            whole = jnp.where((lane >= off) & (lane < end), row, whole)
    return whole


def combine(terms):
    top = functools.reduce(jnp.maximum, terms)
    total = functools.reduce(jnp.add, [jnp.exp2(t - top) for t in terms])
    return top + jnp.log2(total)


def kernel(
    emb, book, new_out, count_out, norm_out,
    rows, cents, scores, half_sq, peak, sums, tally, lse_all,
    lse_unit, lse_mine, lse_in, part_mine, part_in, fin_in, count_mine, count_in,
    outbox, inbox1, inbox2, inbox3,
    book_in, own_sem, row_send, row_recv, sib_send, sib_recv, cent_send, cent_recv,
    stat_send, stat_recv, part_send, part_recv, fin_send, fin_recv,
    count_send, count_recv, sum_send, sum_recv,
):
    dp, cent = lax.axis_index("dp"), lax.axis_index("cent")
    place = (cent // 4, cent % 4, dp // 2)
    core = dp % 2

    def device(p, c):
        return (p[2] * 2 + c, p[0] * 4 + p[1])

    def row_peer(mask, other=0):
        p = [v + 1 - 2 * (v % 2) if mask >> d & 1 else v for d, v in enumerate(place)]
        return device(p, 1 - core if other else core)

    def cent_peer(mask):
        return device([3 - v if mask >> d & 1 else v for d, v in enumerate(place)], core)

    def slot_peer(a):
        return row_peer(ORDER[a // 2], a % 2)

    def remote(src, dst, send, recv, to):
        return pltpu.make_async_remote_copy(
            src_ref=src, dst_ref=dst, send_sem=send, recv_sem=recv,
            device_id=to, device_id_type=MESH,
        )

    barrier = pltpu.get_barrier_semaphore()
    peers = [row_peer(0, 1)] + [row_peer(b) for b in (1, 2, 4)] + [cent_peer(b) for b in (1, 2, 4)]
    for peer in peers:
        pl.semaphore_signal(barrier, inc=1, device_id=peer, device_id_type=MESH)
    own = [
        pltpu.make_async_copy(
            emb.at[pl.ds(r * PART, PART)], rows.at[pl.ds(r * 8 * UNIT, PART)], own_sem.at[r]
        )
        for r in range(2)
    ]
    own.append(pltpu.make_async_copy(book, book_in, own_sem.at[2]))
    own[2].start()
    own[0].start()
    own[1].start()
    pl.semaphore_wait(barrier, len(peers))

    def row_at(r, n, j):
        return pl.ds((r * 8 + 1 + wave_of(j, n)) * UNIT + PIECES[j][0], PIECES[j][1])

    def cent_at(n, j):
        return pl.ds(PLACE[n] * CENTS + PIECES[j][0], PIECES[j][1])

    def row_copy(r, w, d, j, m):
        off, size, _ = PIECES[j]
        src = rows.at[row_at(r, m, j)] if m else emb.at[pl.ds(r * PART + off, size)]
        dst = rows.at[row_at(r, m | 1 << d, j)]
        return remote(src, dst, row_send, row_recv.at[r, w], row_peer(1 << d))

    def cent_copy(w, d, j, m):
        n = m | 1 << d
        src, dst = cents.at[cent_at(m, j)], cents.at[cent_at(n, j)]
        return remote(src, dst, cent_send, cent_recv.at[w], cent_peer(1 << d))

    def sib_copy(r, i):
        at = (r * 8 + i) * UNIT
        src = rows.at[pl.ds(at, PART)] if i else emb.at[pl.ds(r * PART, PART)]
        dst = rows.at[pl.ds(at + PART, PART)]
        return remote(src, dst, sib_send, sib_recv.at[r, i], row_peer(0, 1))

    wave = waves()

    def took(sem, *refs):
        for ref in refs:
            pltpu.make_async_copy(ref, ref, sem).wait()

    def row_start(r, w):
        for msg in wave[w]:
            row_copy(r, w, *msg).start()

    def cent_start(w):
        for msg in wave[w]:
            cent_copy(w, *msg).start()

    def row_arrive(r, w):
        took(row_recv.at[r, w], rows.at[pl.ds(0, PART)])
        sib_copy(r, 1 + w).start()

    def cent_arrive(w):
        took(cent_recv.at[w], cents.at[pl.ds(0, CENTS)])

    def sib_arrive(u):
        took(sib_recv.at[u // 8, u % 8], rows.at[pl.ds(0, PART)])

    def squares(half):
        @pl.loop(0, 4)
        def _(i):
            at = pl.ds(pl.multiple_of(half * 512 + i * CENTS, CENTS), CENTS)
            c = cents[at, :].astype(jnp.float32)
            total = jnp.sum(c * c, axis=1, keepdims=True) * (0.5 * ALPHA)
            half_sq[at, :] = jnp.broadcast_to(total, (CENTS, 128))

    def columns(u):
        return pl.ds(pl.multiple_of(u * UNIT, UNIT), UNIT)

    def score(u, blocks, fresh, last=None):
        cols = columns(u)
        top = jnp.full((8, UNIT), -jnp.inf, jnp.float32) if fresh else peak[u]
        if last is not None:
            summed = columns(last)
            high = jnp.max(peak[last], axis=0, keepdims=True)
            total = jnp.zeros((8, UNIT), jnp.float32)
        for i in blocks:
            at = slice(i * 256, (i + 1) * 256)
            product = lax.dot_general(
                cents[at, :], rows[cols, :], NT, preferred_element_type=jnp.float32
            )
            if last is not None:
                step = 1024 // len(blocks)
                first = (i - blocks[0]) * step
                e = jnp.exp2(scores[first : first + step, summed] - high)
                total = total + jnp.sum(e.reshape(step // 8, 8, UNIT), axis=0)
            h = half_sq[at, :]
            t = product * ALPHA - jnp.concatenate([h] * (UNIT // 128), axis=1)
            scores[at, cols] = t
            top = jnp.maximum(top, jnp.max(t.reshape(32, 8, UNIT), axis=0))
        peak[u] = top
        if last is not None:
            settle(last, high, total)

    def settle(u, high, total):
        lse = high + jnp.log2(jnp.sum(total, axis=0, keepdims=True))
        lse_unit[u, 0] = lse[:, :PART]
        lse_unit[u, 1] = lse[:, PART:]

    def soften(u):
        high = jnp.max(peak[u], axis=0, keepdims=True)
        total = jnp.zeros((8, UNIT), jnp.float32)
        for i in range(4):
            e = jnp.exp2(scores[i * 256 : (i + 1) * 256, columns(u)] - high)
            total = total + jnp.sum(e.reshape(32, 8, UNIT), axis=0)
        settle(u, high, total)

    def mirror(s, a):
        return 2 * PLACE[ORDER[s // 2] ^ ORDER[a // 2]] + (s % 2 ^ a % 2)

    def stat_copy(r, a):
        return remote(
            lse_mine.at[r, a], lse_in.at[r, a], stat_send, stat_recv.at[r], slot_peer(a)
        )

    def part_copy(r, a):
        return remote(
            part_mine.at[r], part_in.at[r, a], part_send, part_recv.at[r], slot_peer(a)
        )

    def fin_copy(r, a):
        return remote(
            lse_mine.at[r, pl.ds(EARLY, 16 - EARLY)], fin_in.at[r, a],
            fin_send, fin_recv.at[r], slot_peer(a),
        )

    def count_copy(n):
        return remote(
            count_mine.at[n], count_in.at[n], count_send, count_recv, cent_peer(ORDER[n])
        )

    def settled(u):
        r, i = u // 8, u % 8
        if i in (3, 7):
            for a in range(0, EARLY) if i == 3 else range(EARLY, 16):
                n, k = ORDER[a // 2], a % 2
                units = [r * 8 + (1 + wave_of(j, n) if n else 0) for j in range(N_PIECES)]
                known = {v: lse_unit[v, k] for v in set(units)}
                lse_mine[r, a] = mosaic([known[v] for v in units])
        if i == 3:
            for a in range(1, EARLY):
                stat_copy(r, a).start()
        if i == 7:
            for a in range(1, 16):
                fin_copy(r, a).start()
            took(stat_recv.at[r], lse_in.at[r, pl.ds(1, EARLY - 1)])
            part_mine[r] = combine([lse_mine[r, 0]] + [lse_in[r, a] for a in range(1, EARLY)])
            for a in range(1, 16):
                part_copy(r, a).start()

    def agree(r):
        took(part_recv.at[r], part_in.at[r, pl.ds(1, 15)])
        took(fin_recv.at[r], fin_in.at[r, pl.ds(1, 15)])
        agreed = []
        for s in range(16):
            terms = [part_mine[r] if s == 0 else part_in[r, s]]
            for q in range(EARLY, 16):
                a = mirror(s, q)
                terms.append(lse_mine[r, q] if a == 0 else fin_in[r, a, q - EARLY])
            agreed.append(combine(terms))
        norm_out[r * PART : (r + 1) * PART] = (agreed[0] * LN2).reshape(PART)
        for i in range(8):
            masks = [mask_of(j, i - 1) if i else 0 for j in range(N_PIECES)]
            for k in range(2):
                at = (r * 8 + i) * UNIT + k * PART
                lse_all[:, at : at + PART] = mosaic([agreed[2 * PLACE[n] + k] for n in masks])

    def weigh(p, r):
        at = pl.ds(pl.multiple_of(p * CENTS, CENTS), CENTS)
        count = tally[p] if r else jnp.zeros((CENTS, 128), jnp.float32)
        total = sums[p] if r else jnp.zeros((CENTS, WIDTH), jnp.float32)
        for i in range(4):
            cols = slice((r * 4 + i) * 2 * UNIT, (r * 4 + i + 1) * 2 * UNIT)
            resp = jnp.exp2(scores[at, cols] - lse_all[:, cols]).astype(jnp.bfloat16)
            wide = resp.astype(jnp.float32)
            for q in range(2 * UNIT // 128):
                count = count + wide[:, q * 128 : (q + 1) * 128]
            total = total + lax.dot_general(
                resp, rows[cols, :], NN, preferred_element_type=jnp.float32
            )
        sums[p] = total
        if r:
            outbox[p] = total.astype(jnp.bfloat16)
            count_mine[p] = jnp.sum(count.T, axis=0, keepdims=True)
        else:
            tally[p] = count

    for w in range(3):
        row_start(0, w)
    own[2].wait()
    cents[0:CENTS, :] = book_in[...].astype(jnp.bfloat16)
    for w in range(3):
        cent_start(w)
    sib_copy(0, 0).start()
    sib_copy(1, 0).start()
    own[0].wait()
    own[1].wait()
    cent_arrive(0)
    cent_start(3)
    cent_start(4)
    row_arrive(0, 0)
    row_start(0, 3)
    row_start(0, 4)
    cent_arrive(1)
    cent_start(5)
    row_arrive(0, 1)
    row_start(0, 5)
    cent_arrive(2)
    squares(0)
    row_arrive(0, 2)

    first = (0, 8, 1, 2, 3, 4, 5, 6)

    def first_unit(i):
        return jnp.where(i == 0, 0, jnp.where(i == 1, 8, i - 1))

    def before_first(i):
        if i == 4:
            cent_arrive(3)
            cent_start(6)
            row_arrive(0, 3)
            row_start(0, 6)
            row_start(1, 0)
        if i == 5:
            row_arrive(0, 4)
            cent_arrive(4)
        if i == 6:
            row_arrive(0, 5)
            row_start(1, 1)
            row_start(1, 2)
            cent_arrive(5)
        if i == 7:
            row_arrive(0, 6)
        sib_arrive(first[i])

    @pl.loop(0, 8)
    def _(i):
        for v in range(8):
            pl.when(i == v)(functools.partial(before_first, v))
        score(first_unit(i), (0, 1), True)

    cent_arrive(6)
    squares(1)
    score(0, (2, 3), False)

    @pl.loop(1, 8)
    def _(i):
        @pl.when(i == 3)
        def _():
            row_arrive(1, 0)
            row_start(1, 3)
            row_start(1, 4)

        score(first_unit(i), (2, 3), False, first_unit(i - 1))
        pl.when(i == 5)(functools.partial(settled, 3))

    def before_full(i):
        if i == 1:
            row_arrive(1, 1)
            row_start(1, 5)
        if i == 2:
            row_arrive(1, 2)
        if i == 3:
            row_arrive(1, 3)
            row_start(1, 6)
        if i == 5:
            agree(0)
        if i in (5, 6):
            weigh(12 - i, 0)
        if i in (4, 5, 6):
            row_arrive(1, i)
        sib_arrive(i + 8 if i else 7)

    @pl.loop(0, 8)
    def _(i):
        for v in range(8):
            pl.when(i == v)(functools.partial(before_full, v))
        last = jnp.where(i == 0, 6, jnp.where(i == 1, 7, 7 + i))
        score(jnp.where(i == 0, 7, 8 + i), (0, 1, 2, 3), True, last)
        pl.when(i == 1)(functools.partial(settled, 7))
        pl.when(i == 4)(functools.partial(settled, 11))

    soften(15)
    settled(15)

    def step_of(n, j):
        return next(s for s in range(3) if n >> PIECES[j][2][s] & 1)

    def sum_copy(n, j):
        at = pl.ds(*PIECES[j][:2])
        s = step_of(n, j)
        d = PIECES[j][2][s]
        group = 3 if n in (1, 2, 4) else 0 if n == 7 else 1 + s
        box = (inbox1, inbox2, inbox3)[s]
        dst = box.at[0 if s == 2 else PLACE[n ^ 1 << d], at]
        return remote(
            outbox.at[PLACE[n], at], dst, sum_send, sum_recv.at[group], cent_peer(1 << d)
        )

    def gathered(n, j):
        off, size, _ = PIECES[j]
        value = sums[PLACE[n], off : off + size, :]
        for s in range(step_of(n, j) if n else 3):
            box = (inbox1, inbox2, inbox3)[s]
            at = 0 if s == 2 else PLACE[n]
            value = value + box[at, off : off + size, :].astype(jnp.float32)
        return value

    def send_sums(n, step):
        for j in range(N_PIECES):
            if step_of(n, j) == step:
                if step:
                    off, size, _ = PIECES[j]
                    outbox[PLACE[n], off : off + size, :] = gathered(n, j).astype(jnp.bfloat16)
                sum_copy(n, j).start()

    def after(p):
        n = ORDER[p]
        if n:
            send_sums(n, 0)
            count_copy(p).start()
        if p == 4:
            took(sum_recv.at[0], inbox1.at[0])
            for m in (6, 5, 3):
                send_sums(m, 1)
        if p == 1:
            took(sum_recv.at[1], inbox1.at[pl.ds(0, 2)])
            for m in (4, 2, 1):
                send_sums(m, 1)

    @pl.loop(2, 8)
    def _(i):
        weigh(7 - i, 0)

    agree(1)

    @pl.loop(0, 8)
    def _(i):
        weigh(7 - i, 1)
        for p in range(8):
            pl.when(i == 7 - p)(functools.partial(after, p))

    took(sum_recv.at[2], inbox2.at[0])
    for n in (4, 2, 1):
        send_sums(n, 2)

    took(row_send, rows.at[pl.ds(0, 14 * PART)])
    took(sib_send, rows.at[pl.ds(0, 16 * PART)])
    took(cent_send, cents.at[pl.ds(0, 7 * CENTS)])
    for r in range(2):
        took(stat_send, lse_in.at[r, pl.ds(1, EARLY - 1)])
        took(part_send, part_in.at[r, pl.ds(1, 15)])
        took(fin_send, fin_in.at[r, pl.ds(1, 15)])
    took(count_send, count_in.at[pl.ds(1, 7)])
    took(count_recv, count_in.at[pl.ds(1, 7)])
    count = functools.reduce(jnp.add, [count_mine[0]] + [count_in[n] for n in range(1, 8)])
    count_out[...] = count.reshape(CENTS)
    below = jnp.broadcast_to(count, (CENTS, 128)).T + PRIOR
    took(sum_recv.at[3], inbox1.at[pl.ds(0, 3)])
    for j in range(N_PIECES):
        off, size, _ = PIECES[j]
        top = gathered(0, j) + PRIOR * book_in[off : off + size, :]
        for q in range(WIDTH // 128):
            cols = slice(q * 128, (q + 1) * 128)
            new_out[off : off + size, cols] = top[:, cols] / below[off : off + size, :]
    took(sum_send, outbox.at[pl.ds(1, 7)])


def local(embeddings, codebook):
    f32, bf16 = jnp.float32, jnp.bfloat16
    vmem, dma = pltpu.VMEM, pltpu.SemaphoreType.DMA
    new, count, norm = pl.pallas_call(
        kernel,
        out_shape=(
            vmem((CENTS, WIDTH), f32),
            vmem((CENTS,), f32),
            vmem((ROWS,), f32),
        ),
        in_specs=[pl.BlockSpec(memory_space=pl.ANY)] * 2,
        out_specs=[pl.BlockSpec(memory_space=pltpu.VMEM)] * 3,
        scratch_shapes=[
            vmem((16 * UNIT, WIDTH), bf16),
            vmem((8 * CENTS, WIDTH), bf16),
            vmem((8 * CENTS, 16 * UNIT), f32),
            vmem((8 * CENTS, 128), f32),
            vmem((16, 8, UNIT), f32),
            vmem((8, CENTS, WIDTH), f32),
            vmem((8, CENTS, 128), f32),
            vmem((1, 16 * UNIT), f32),
            vmem((16, 2, 1, PART), f32),
            vmem((2, 16, 1, PART), f32),
            vmem((2, 16, 1, PART), f32),
            vmem((2, 1, PART), f32),
            vmem((2, 16, 1, PART), f32),
            vmem((2, 16, 16 - EARLY, 1, PART), f32),
            vmem((8, 1, CENTS), f32),
            vmem((8, 1, CENTS), f32),
            vmem((8, CENTS, WIDTH), bf16),
            vmem((8, CENTS, WIDTH), bf16),
            vmem((8, CENTS, WIDTH), bf16),
            vmem((1, CENTS, WIDTH), bf16),
            vmem((CENTS, WIDTH), f32),
            dma((3,)),
            dma(()), dma((2, 7)),
            dma(()), dma((2, 8)),
            dma(()), dma((7,)),
            dma(()), dma((2,)),
            dma(()), dma((2,)),
            dma(()), dma((2,)),
            dma(()), dma(()),
            dma(()), dma((4,)),
        ],
        compiler_params=pltpu.CompilerParams(
            collective_id=0, has_side_effects=True, vmem_limit_bytes=58 * 2**20
        ),
        cost_estimate=pl.CostEstimate(
            flops=4 * 4096 * 1024 * 1024, bytes_accessed=2**21, transcendentals=2**23
        ),
    )(embeddings, codebook)
    return new, count, norm


def solution(mesh):
    return jax.shard_map(
        local,
        mesh=mesh,
        in_specs=(P(("dp", "cent"), None), P(("cent", "dp"), None)),
        out_specs=(P(("cent", "dp"), None), P(("cent", "dp")), P(("dp", "cent"))),
        check_vma=False,
    )
```

```python
import functools
import math

import jax
import jax.numpy as jnp
from jax import lax
from jax.experimental import pallas as pl
from jax.experimental.pallas import tpu as pltpu
from jax.sharding import PartitionSpec as P

TEMPER = 0.8
PRIOR = 1.0
ALPHA = math.log2(math.e) / TEMPER
LN2 = math.log(2.0)
MESH = pl.DeviceIdType.MESH

ROWS, CENTS, WIDTH = 256, 128, 1024
PART, UNIT = 128, 256
PIECES = (
    (0, 16, (2, 1, 0)),
    (16, 32, (1, 2, 0)),
    (48, 16, (2, 0, 1)),
    (64, 32, (0, 2, 1)),
    (96, 16, (1, 0, 2)),
    (112, 16, (0, 1, 2)),
)
N_PIECES = len(PIECES)
ORDER = (0, 1, 2, 4, 3, 5, 6, 7)
PLACE = {mask: i for i, mask in enumerate(ORDER)}
EARLY = 8
NT = (((1,), (1,)), ((), ()))
NN = (((1,), (0,)), ((), ()))


def waves():
    wave = [[] for _ in range(7)]
    for j, (_, _, (a, b, c)) in enumerate(PIECES):
        sent = ((a, 0), (b, 0), (c, 0), (b, 1 << a), (c, 1 << a), (c, 1 << b), (c, 1 << a | 1 << b))
        for w, (d, m) in enumerate(sent):
            wave[w].append((d, j, m))
    return wave


def wave_of(j, mask):
    a, b, c = (1 << d for d in PIECES[j][2])
    return (a, b, c, a | b, a | c, b | c, 7).index(mask)


def mask_of(j, w):
    return next(mask for mask in range(1, 8) if wave_of(j, mask) == w)


def mosaic(rows):
    lane = lax.broadcasted_iota(jnp.int32, (1, PART), 1)
    whole = rows[-1]
    for (off, _, _), (end, _, _), row in list(zip(PIECES, PIECES[1:], rows))[::-1]:
        if row is not whole:
            whole = jnp.where((lane >= off) & (lane < end), row, whole)
    return whole


def combine(terms):
    top = functools.reduce(jnp.maximum, terms)
    total = functools.reduce(jnp.add, [jnp.exp2(t - top) for t in terms])
    return top + jnp.log2(total)


def kernel(
    emb, book, new_out, count_out, norm_out,
    rows, cents, scores, half_sq, peak, sums, tally, lse_all,
    lse_unit, lse_mine, lse_in, part_mine, part_in, fin_in, count_mine, count_in,
    outbox, inbox1, inbox2, inbox3,
    book_in, own_sem, row_send, row_recv, sib_send, sib_recv, cent_send, cent_recv,
    stat_send, stat_recv, part_send, part_recv, fin_send, fin_recv,
    count_send, count_recv, sum_send, sum_recv,
):
    dp, cent = lax.axis_index("dp"), lax.axis_index("cent")
    place = (cent // 4, cent % 4, dp // 2)
    core = dp % 2

    def device(p, c):
        return (p[2] * 2 + c, p[0] * 4 + p[1])

    def row_peer(mask, other=0):
        p = [v + 1 - 2 * (v % 2) if mask >> d & 1 else v for d, v in enumerate(place)]
        return device(p, 1 - core if other else core)

    def cent_peer(mask):
        return device([3 - v if mask >> d & 1 else v for d, v in enumerate(place)], core)

    def slot_peer(a):
        return row_peer(ORDER[a // 2], a % 2)

    def remote(src, dst, send, recv, to):
        return pltpu.make_async_remote_copy(
            src_ref=src, dst_ref=dst, send_sem=send, recv_sem=recv,
            device_id=to, device_id_type=MESH,
        )

    barrier = pltpu.get_barrier_semaphore()
    peers = [row_peer(0, 1)] + [row_peer(b) for b in (1, 2, 4)] + [cent_peer(b) for b in (1, 2, 4)]
    for peer in peers:
        pl.semaphore_signal(barrier, inc=1, device_id=peer, device_id_type=MESH)
    own = [
        pltpu.make_async_copy(
            emb.at[pl.ds(r * PART, PART)], rows.at[pl.ds(r * 8 * UNIT, PART)], own_sem.at[r]
        )
        for r in range(2)
    ]
    own.append(pltpu.make_async_copy(book, book_in, own_sem.at[2]))
    own[2].start()
    own[0].start()
    own[1].start()
    pl.semaphore_wait(barrier, len(peers))

    def row_at(r, n, j):
        return pl.ds((r * 8 + 1 + wave_of(j, n)) * UNIT + PIECES[j][0], PIECES[j][1])

    def cent_at(n, j):
        return pl.ds(PLACE[n] * CENTS + PIECES[j][0], PIECES[j][1])

    def row_copy(r, w, d, j, m):
        off, size, _ = PIECES[j]
        src = rows.at[row_at(r, m, j)] if m else emb.at[pl.ds(r * PART + off, size)]
        dst = rows.at[row_at(r, m | 1 << d, j)]
        return remote(src, dst, row_send, row_recv.at[r, w], row_peer(1 << d))

    def cent_copy(w, d, j, m):
        n = m | 1 << d
        src, dst = cents.at[cent_at(m, j)], cents.at[cent_at(n, j)]
        return remote(src, dst, cent_send, cent_recv.at[w], cent_peer(1 << d))

    def sib_copy(r, i):
        at = (r * 8 + i) * UNIT
        src = rows.at[pl.ds(at, PART)] if i else emb.at[pl.ds(r * PART, PART)]
        dst = rows.at[pl.ds(at + PART, PART)]
        return remote(src, dst, sib_send, sib_recv.at[r, i], row_peer(0, 1))

    wave = waves()

    def took(sem, *refs):
        for ref in refs:
            pltpu.make_async_copy(ref, ref, sem).wait()

    def row_start(r, w):
        for msg in wave[w]:
            row_copy(r, w, *msg).start()

    def cent_start(w):
        for msg in wave[w]:
            cent_copy(w, *msg).start()

    def row_arrive(r, w):
        took(row_recv.at[r, w], rows.at[pl.ds(0, PART)])
        sib_copy(r, 1 + w).start()

    def cent_arrive(w):
        took(cent_recv.at[w], cents.at[pl.ds(0, CENTS)])

    def sib_arrive(u):
        took(sib_recv.at[u // 8, u % 8], rows.at[pl.ds(0, PART)])

    def squares(half):
        @pl.loop(0, 4)
        def _(i):
            at = pl.ds(pl.multiple_of(half * 512 + i * CENTS, CENTS), CENTS)
            c = cents[at, :].astype(jnp.float32)
            total = jnp.sum(c * c, axis=1, keepdims=True) * (0.5 * ALPHA)
            half_sq[at, :] = jnp.broadcast_to(total, (CENTS, 128))

    def columns(u):
        return pl.ds(pl.multiple_of(u * UNIT, UNIT), UNIT)

    def score(u, blocks, fresh, last=None):
        cols = columns(u)
        top = jnp.full((8, UNIT), -jnp.inf, jnp.float32) if fresh else peak[u]
        if last is not None:
            summed = columns(last)
            high = jnp.max(peak[last], axis=0, keepdims=True)
            total = jnp.zeros((8, UNIT), jnp.float32)
        for i in blocks:
            at = slice(i * 256, (i + 1) * 256)
            product = lax.dot_general(
                cents[at, :], rows[cols, :], NT, preferred_element_type=jnp.float32
            )
            if last is not None:
                step = 1024 // len(blocks)
                first = (i - blocks[0]) * step
                e = jnp.exp2(scores[first : first + step, summed] - high)
                total = total + jnp.sum(e.reshape(step // 8, 8, UNIT), axis=0)
            h = half_sq[at, :]
            t = product * ALPHA - jnp.concatenate([h] * (UNIT // 128), axis=1)
            scores[at, cols] = t
            top = jnp.maximum(top, jnp.max(t.reshape(32, 8, UNIT), axis=0))
        peak[u] = top
        if last is not None:
            settle(last, high, total)

    def settle(u, high, total):
        lse = high + jnp.log2(jnp.sum(total, axis=0, keepdims=True))
        lse_unit[u, 0] = lse[:, :PART]
        lse_unit[u, 1] = lse[:, PART:]

    def soften(u):
        high = jnp.max(peak[u], axis=0, keepdims=True)
        total = jnp.zeros((8, UNIT), jnp.float32)
        for i in range(4):
            e = jnp.exp2(scores[i * 256 : (i + 1) * 256, columns(u)] - high)
            total = total + jnp.sum(e.reshape(32, 8, UNIT), axis=0)
        settle(u, high, total)

    def mirror(s, a):
        return 2 * PLACE[ORDER[s // 2] ^ ORDER[a // 2]] + (s % 2 ^ a % 2)

    def stat_copy(r, a):
        return remote(
            lse_mine.at[r, a], lse_in.at[r, a], stat_send, stat_recv.at[r], slot_peer(a)
        )

    def part_copy(r, a):
        return remote(
            part_mine.at[r], part_in.at[r, a], part_send, part_recv.at[r], slot_peer(a)
        )

    def fin_copy(r, a):
        return remote(
            lse_mine.at[r, pl.ds(EARLY, 16 - EARLY)], fin_in.at[r, a],
            fin_send, fin_recv.at[r], slot_peer(a),
        )

    def count_copy(n):
        return remote(
            count_mine.at[n], count_in.at[n], count_send, count_recv, cent_peer(ORDER[n])
        )

    def settled(u):
        r, i = u // 8, u % 8
        if i in (3, 7):
            for a in range(0, EARLY) if i == 3 else range(EARLY, 16):
                n, k = ORDER[a // 2], a % 2
                units = [r * 8 + (1 + wave_of(j, n) if n else 0) for j in range(N_PIECES)]
                known = {v: lse_unit[v, k] for v in set(units)}
                lse_mine[r, a] = mosaic([known[v] for v in units])
        if i == 3:
            for a in range(1, EARLY):
                stat_copy(r, a).start()
        if i == 7:
            for a in range(1, 16):
                fin_copy(r, a).start()
            took(stat_recv.at[r], lse_in.at[r, pl.ds(1, EARLY - 1)])
            part_mine[r] = combine([lse_mine[r, 0]] + [lse_in[r, a] for a in range(1, EARLY)])
            for a in range(1, 16):
                part_copy(r, a).start()

    def agree(r):
        took(part_recv.at[r], part_in.at[r, pl.ds(1, 15)])
        took(fin_recv.at[r], fin_in.at[r, pl.ds(1, 15)])
        agreed = []
        for s in range(16):
            terms = [part_mine[r] if s == 0 else part_in[r, s]]
            for q in range(EARLY, 16):
                a = mirror(s, q)
                terms.append(lse_mine[r, q] if a == 0 else fin_in[r, a, q - EARLY])
            agreed.append(combine(terms))
        norm_out[r * PART : (r + 1) * PART] = (agreed[0] * LN2).reshape(PART)
        for i in range(8):
            masks = [mask_of(j, i - 1) if i else 0 for j in range(N_PIECES)]
            for k in range(2):
                at = (r * 8 + i) * UNIT + k * PART
                lse_all[:, at : at + PART] = mosaic([agreed[2 * PLACE[n] + k] for n in masks])

    def weigh(p, r):
        at = pl.ds(pl.multiple_of(p * CENTS, CENTS), CENTS)
        count = tally[p] if r else jnp.zeros((CENTS, 128), jnp.float32)
        total = sums[p] if r else jnp.zeros((CENTS, WIDTH), jnp.float32)
        for i in range(4):
            cols = slice((r * 4 + i) * 2 * UNIT, (r * 4 + i + 1) * 2 * UNIT)
            resp = jnp.exp2(scores[at, cols] - lse_all[:, cols]).astype(jnp.bfloat16)
            wide = resp.astype(jnp.float32)
            for q in range(2 * UNIT // 128):
                count = count + wide[:, q * 128 : (q + 1) * 128]
            total = total + lax.dot_general(
                resp, rows[cols, :], NN, preferred_element_type=jnp.float32
            )
        sums[p] = total
        if r:
            outbox[p] = total.astype(jnp.bfloat16)
            count_mine[p] = jnp.sum(count.T, axis=0, keepdims=True)
        else:
            tally[p] = count

    for w in range(3):
        row_start(0, w)
    own[2].wait()
    cents[0:CENTS, :] = book_in[...].astype(jnp.bfloat16)
    for w in range(3):
        cent_start(w)
    sib_copy(0, 0).start()
    sib_copy(1, 0).start()
    own[0].wait()
    own[1].wait()
    cent_arrive(0)
    cent_start(3)
    cent_start(4)
    row_arrive(0, 0)
    row_start(0, 3)
    row_start(0, 4)
    cent_arrive(1)
    cent_start(5)
    row_arrive(0, 1)
    row_start(0, 5)
    cent_arrive(2)
    squares(0)
    row_arrive(0, 2)

    first = (0, 8, 1, 2, 3, 4, 5, 6)

    def first_unit(i):
        return jnp.where(i == 0, 0, jnp.where(i == 1, 8, i - 1))

    def before_first(i):
        if i == 4:
            cent_arrive(3)
            cent_start(6)
            row_arrive(0, 3)
            row_start(0, 6)
            row_start(1, 0)
        if i == 5:
            row_arrive(0, 4)
            cent_arrive(4)
        if i == 6:
            row_arrive(0, 5)
            row_start(1, 1)
            row_start(1, 2)
            cent_arrive(5)
        if i == 7:
            row_arrive(0, 6)
        sib_arrive(first[i])

    @pl.loop(0, 8)
    def _(i):
        for v in range(8):
            pl.when(i == v)(functools.partial(before_first, v))
        score(first_unit(i), (0, 1), True)

    cent_arrive(6)
    squares(1)
    score(0, (2, 3), False)

    @pl.loop(1, 8)
    def _(i):
        @pl.when(i == 3)
        def _():
            row_arrive(1, 0)
            row_start(1, 3)
            row_start(1, 4)

        score(first_unit(i), (2, 3), False, first_unit(i - 1))
        pl.when(i == 5)(functools.partial(settled, 3))

    def before_full(i):
        if i == 1:
            row_arrive(1, 1)
            row_start(1, 5)
        if i == 2:
            row_arrive(1, 2)
        if i == 3:
            row_arrive(1, 3)
            row_start(1, 6)
        if i == 5:
            agree(0)
        if i in (5, 6):
            weigh(12 - i, 0)
        if i in (4, 5, 6):
            row_arrive(1, i)
        sib_arrive(i + 8 if i else 7)

    @pl.loop(0, 8)
    def _(i):
        for v in range(8):
            pl.when(i == v)(functools.partial(before_full, v))
        last = jnp.where(i == 0, 6, jnp.where(i == 1, 7, 7 + i))
        score(jnp.where(i == 0, 7, 8 + i), (0, 1, 2, 3), True, last)
        pl.when(i == 1)(functools.partial(settled, 7))
        pl.when(i == 4)(functools.partial(settled, 11))

    soften(15)
    settled(15)

    def step_of(n, j):
        return next(s for s in range(3) if n >> PIECES[j][2][s] & 1)

    def sum_copy(n, j):
        at = pl.ds(*PIECES[j][:2])
        s = step_of(n, j)
        d = PIECES[j][2][s]
        group = 0 if n == 7 else 1 + s if n in (3, 5, 6) else 3 + s // 2
        box = (inbox1, inbox2, inbox3)[s]
        dst = box.at[0 if s == 2 else PLACE[n ^ 1 << d], at]
        return remote(
            outbox.at[PLACE[n], at], dst, sum_send, sum_recv.at[group], cent_peer(1 << d)
        )

    def gathered(n, j):
        at = PLACE[n], slice(PIECES[j][0], PIECES[j][0] + PIECES[j][1])
        value = sums[at]
        for box in (inbox1, inbox2)[: step_of(n, j)]:
            value = value + box[at].astype(jnp.float32)
        return value

    def send_sums(n, step):
        for j in range(N_PIECES):
            if step_of(n, j) == step:
                if step:
                    off, size, _ = PIECES[j]
                    outbox[PLACE[n], off : off + size, :] = gathered(n, j).astype(jnp.bfloat16)
                sum_copy(n, j).start()

    def after(p):
        n = ORDER[p]
        if n:
            send_sums(n, 0)
            count_copy(p).start()
        if p == 4:
            took(sum_recv.at[0], inbox1.at[0])
            for m in (6, 5, 3):
                send_sums(m, 1)
        if p == 1:
            took(sum_recv.at[1], inbox1.at[pl.ds(0, 2)])
            for m in (4, 2, 1):
                send_sums(m, 1)

    @pl.loop(2, 6)
    def _(i):
        weigh(7 - i, 0)

    agree(1)

    @pl.loop(0, 8)
    def _(i):
        pl.when(i > 5)(lambda: weigh(7 - i, 0))
        weigh(7 - i, 1)
        for p in range(8):
            pl.when(i == 7 - p)(functools.partial(after, p))

    took(sum_recv.at[2], inbox2.at[0])
    for n in (4, 2, 1):
        send_sums(n, 2)

    took(row_send, rows.at[pl.ds(0, 14 * PART)])
    took(sib_send, rows.at[pl.ds(0, 16 * PART)])
    took(cent_send, cents.at[pl.ds(0, 7 * CENTS)])
    for r in range(2):
        took(stat_send, lse_in.at[r, pl.ds(1, EARLY - 1)])
        took(part_send, part_in.at[r, pl.ds(1, 15)])
        took(fin_send, fin_in.at[r, pl.ds(1, 15)])
    took(count_send, count_in.at[pl.ds(1, 7)])
    took(count_recv, count_in.at[pl.ds(1, 7)])
    count = functools.reduce(jnp.add, [count_mine[0]] + [count_in[n] for n in range(1, 8)])
    count_out[...] = count.reshape(CENTS)
    below = jnp.broadcast_to(count, (CENTS, 128)).T + PRIOR
    took(sum_recv.at[3], inbox1.at[pl.ds(0, 2)])
    share = 1.0 / below
    for q in range(WIDTH // 128):
        cols = slice(q * 128, (q + 1) * 128)
        near = sums[0, :, cols] + PRIOR * book_in[:, cols]
        for box in (inbox1, inbox2):
            near = near + box[0, :, cols].astype(jnp.float32)
        sums[0, :, cols] = near
    took(sum_recv.at[4], inbox3.at[0])
    for q in range(WIDTH // 128):
        cols = slice(q * 128, (q + 1) * 128)
        new_out[:, cols] = (sums[0, :, cols] + inbox3[0, :, cols].astype(jnp.float32)) * share
    took(sum_send, outbox.at[pl.ds(1, 7)])


def local(embeddings, codebook):
    f32, bf16 = jnp.float32, jnp.bfloat16
    vmem, dma = pltpu.VMEM, pltpu.SemaphoreType.DMA
    new, count, norm = pl.pallas_call(
        kernel,
        out_shape=(
            vmem((CENTS, WIDTH), f32),
            vmem((CENTS,), f32),
            vmem((ROWS,), f32),
        ),
        in_specs=[pl.BlockSpec(memory_space=pl.ANY)] * 2,
        out_specs=[pl.BlockSpec(memory_space=pltpu.VMEM)] * 3,
        scratch_shapes=[
            vmem((16 * UNIT, WIDTH), bf16),
            vmem((8 * CENTS, WIDTH), bf16),
            vmem((8 * CENTS, 16 * UNIT), f32),
            vmem((8 * CENTS, 128), f32),
            vmem((16, 8, UNIT), f32),
            vmem((8, CENTS, WIDTH), f32),
            vmem((8, CENTS, 128), f32),
            vmem((1, 16 * UNIT), f32),
            vmem((16, 2, 1, PART), f32),
            vmem((2, 16, 1, PART), f32),
            vmem((2, 16, 1, PART), f32),
            vmem((2, 1, PART), f32),
            vmem((2, 16, 1, PART), f32),
            vmem((2, 16, 16 - EARLY, 1, PART), f32),
            vmem((8, 1, CENTS), f32),
            vmem((8, 1, CENTS), f32),
            vmem((8, CENTS, WIDTH), bf16),
            vmem((8, CENTS, WIDTH), bf16),
            vmem((8, CENTS, WIDTH), bf16),
            vmem((1, CENTS, WIDTH), bf16),
            vmem((CENTS, WIDTH), f32),
            dma((3,)),
            dma(()), dma((2, 7)),
            dma(()), dma((2, 8)),
            dma(()), dma((7,)),
            dma(()), dma((2,)),
            dma(()), dma((2,)),
            dma(()), dma((2,)),
            dma(()), dma(()),
            dma(()), dma((5,)),
        ],
        compiler_params=pltpu.CompilerParams(
            collective_id=0, has_side_effects=True, vmem_limit_bytes=58 * 2**20
        ),
        cost_estimate=pl.CostEstimate(
            flops=4 * 4096 * 1024 * 1024, bytes_accessed=2**21, transcendentals=2**23
        ),
    )(embeddings, codebook)
    return new, count, norm


def solution(mesh):
    return jax.shard_map(
        local,
        mesh=mesh,
        in_specs=(P(("dp", "cent"), None), P(("cent", "dp"), None)),
        out_specs=(P(("cent", "dp"), None), P(("cent", "dp")), P(("dp", "cent"))),
        check_vma=False,
    )
```

```python
import functools
import math

import jax
import jax.numpy as jnp
from jax import lax
from jax.experimental import pallas as pl
from jax.experimental.pallas import tpu as pltpu
from jax.sharding import PartitionSpec as P

TEMPER = 0.8
PRIOR = 1.0
ALPHA = math.log2(math.e) / TEMPER
LN2 = math.log(2.0)
MESH = pl.DeviceIdType.MESH

ROWS, CENTS, WIDTH = 256, 128, 1024
PART, UNIT = 128, 256
PIECES = (
    (0, 16, (2, 1, 0)),
    (16, 32, (1, 2, 0)),
    (48, 16, (2, 0, 1)),
    (64, 32, (0, 2, 1)),
    (96, 16, (1, 0, 2)),
    (112, 16, (0, 1, 2)),
)
N_PIECES = len(PIECES)
ORDER = (0, 1, 2, 4, 3, 5, 6, 7)
PLACE = {mask: i for i, mask in enumerate(ORDER)}
EARLY = 8
NT = (((1,), (1,)), ((), ()))
NN = (((1,), (0,)), ((), ()))


def waves():
    wave = [[] for _ in range(7)]
    for j, (_, _, (a, b, c)) in enumerate(PIECES):
        sent = ((a, 0), (b, 0), (c, 0), (b, 1 << a), (c, 1 << a), (c, 1 << b), (c, 1 << a | 1 << b))
        for w, (d, m) in enumerate(sent):
            wave[w].append((d, j, m))
    return wave


def wave_of(j, mask):
    a, b, c = (1 << d for d in PIECES[j][2])
    return (a, b, c, a | b, a | c, b | c, 7).index(mask)


def mask_of(j, w):
    return next(mask for mask in range(1, 8) if wave_of(j, mask) == w)


def mosaic(rows):
    lane = lax.broadcasted_iota(jnp.int32, (1, PART), 1)
    whole = rows[-1]
    for (off, _, _), (end, _, _), row in list(zip(PIECES, PIECES[1:], rows))[::-1]:
        if row is not whole:
            whole = jnp.where((lane >= off) & (lane < end), row, whole)
    return whole


def combine(terms):
    top = functools.reduce(jnp.maximum, terms)
    total = functools.reduce(jnp.add, [jnp.exp2(t - top) for t in terms])
    return top + jnp.log2(total)


def kernel(
    emb, book, new_out, count_out, norm_out,
    rows, cents, scores, half_sq, peak, sums, tally, lse_all,
    lse_unit, lse_mine, lse_in, part_mine, part_in, fin_in, count_mine, count_in,
    outbox, inbox1, inbox2, inbox3,
    book_in, own_sem, row_send, row_recv, sib_send, sib_recv, cent_send, cent_recv,
    stat_send, stat_recv, part_send, part_recv, fin_send, fin_recv,
    count_send, count_recv, sum_send, sum_recv,
):
    dp, cent = lax.axis_index("dp"), lax.axis_index("cent")
    place = (cent // 4, cent % 4, dp // 2)
    core = dp % 2

    def device(p, c):
        return (p[2] * 2 + c, p[0] * 4 + p[1])

    def row_peer(mask, other=0):
        p = [v + 1 - 2 * (v % 2) if mask >> d & 1 else v for d, v in enumerate(place)]
        return device(p, 1 - core if other else core)

    def cent_peer(mask):
        return device([3 - v if mask >> d & 1 else v for d, v in enumerate(place)], core)

    def slot_peer(a):
        return row_peer(ORDER[a // 2], a % 2)

    def remote(src, dst, send, recv, to):
        return pltpu.make_async_remote_copy(
            src_ref=src, dst_ref=dst, send_sem=send, recv_sem=recv,
            device_id=to, device_id_type=MESH,
        )

    barrier = pltpu.get_barrier_semaphore()
    peers = [row_peer(0, 1)] + [row_peer(b) for b in (1, 2, 4)] + [cent_peer(b) for b in (1, 2, 4)]
    for peer in peers:
        pl.semaphore_signal(barrier, inc=1, device_id=peer, device_id_type=MESH)
    own = [
        pltpu.make_async_copy(
            emb.at[pl.ds(r * PART, PART)], rows.at[pl.ds(r * 8 * UNIT, PART)], own_sem.at[r]
        )
        for r in range(2)
    ]
    own.append(pltpu.make_async_copy(book, book_in, own_sem.at[2]))
    own[2].start()
    own[0].start()
    own[1].start()
    pl.semaphore_wait(barrier, len(peers))

    def row_at(r, n, j):
        return pl.ds((r * 8 + 1 + wave_of(j, n)) * UNIT + PIECES[j][0], PIECES[j][1])

    def cent_at(n, j):
        return pl.ds(PLACE[n] * CENTS + PIECES[j][0], PIECES[j][1])

    def row_copy(r, w, d, j, m):
        off, size, _ = PIECES[j]
        src = rows.at[row_at(r, m, j)] if m else emb.at[pl.ds(r * PART + off, size)]
        dst = rows.at[row_at(r, m | 1 << d, j)]
        return remote(src, dst, row_send, row_recv.at[r, w], row_peer(1 << d))

    def cent_copy(w, d, j, m):
        n = m | 1 << d
        src, dst = cents.at[cent_at(m, j)], cents.at[cent_at(n, j)]
        return remote(src, dst, cent_send, cent_recv.at[w], cent_peer(1 << d))

    def sib_copy(r, i):
        at = (r * 8 + i) * UNIT
        src = rows.at[pl.ds(at, PART)] if i else emb.at[pl.ds(r * PART, PART)]
        dst = rows.at[pl.ds(at + PART, PART)]
        return remote(src, dst, sib_send, sib_recv.at[r, i], row_peer(0, 1))

    wave = waves()

    def took(sem, *refs):
        for ref in refs:
            pltpu.make_async_copy(ref, ref, sem).wait()

    def row_start(r, w):
        for msg in wave[w]:
            row_copy(r, w, *msg).start()

    def cent_start(w):
        for msg in wave[w]:
            cent_copy(w, *msg).start()

    def row_arrive(r, w):
        took(row_recv.at[r, w], rows.at[pl.ds(0, PART)])
        sib_copy(r, 1 + w).start()

    def cent_arrive(w):
        took(cent_recv.at[w], cents.at[pl.ds(0, CENTS)])

    def sib_arrive(u):
        took(sib_recv.at[u // 8, u % 8], rows.at[pl.ds(0, PART)])

    def squares(half):
        @pl.loop(0, 4)
        def _(i):
            at = pl.ds(pl.multiple_of(half * 512 + i * CENTS, CENTS), CENTS)
            c = cents[at, :].astype(jnp.float32)
            total = jnp.sum(c * c, axis=1, keepdims=True) * (0.5 * ALPHA)
            half_sq[at, :] = jnp.broadcast_to(total, (CENTS, 128))

    def columns(u):
        return pl.ds(pl.multiple_of(u * UNIT, UNIT), UNIT)

    def score(u, blocks, fresh, last=None):
        cols = columns(u)
        top = jnp.full((8, UNIT), -jnp.inf, jnp.float32) if fresh else peak[u]
        if last is not None:
            summed = columns(last)
            high = jnp.max(peak[last], axis=0, keepdims=True)
            total = jnp.zeros((8, UNIT), jnp.float32)
        for i in blocks:
            at = slice(i * 256, (i + 1) * 256)
            product = lax.dot_general(
                cents[at, :], rows[cols, :], NT, preferred_element_type=jnp.float32
            )
            if last is not None:
                step = 1024 // len(blocks)
                first = (i - blocks[0]) * step
                e = jnp.exp2(scores[first : first + step, summed] - high)
                total = total + jnp.sum(e.reshape(step // 8, 8, UNIT), axis=0)
            h = half_sq[at, :]
            t = product * ALPHA - jnp.concatenate([h] * (UNIT // 128), axis=1)
            scores[at, cols] = t
            top = jnp.maximum(top, jnp.max(t.reshape(32, 8, UNIT), axis=0))
        peak[u] = top
        if last is not None:
            settle(last, high, total)

    def settle(u, high, total):
        lse = high + jnp.log2(jnp.sum(total, axis=0, keepdims=True))
        lse_unit[u, 0] = lse[:, :PART]
        lse_unit[u, 1] = lse[:, PART:]

    def soften(u):
        high = jnp.max(peak[u], axis=0, keepdims=True)
        total = jnp.zeros((8, UNIT), jnp.float32)
        for i in range(4):
            e = jnp.exp2(scores[i * 256 : (i + 1) * 256, columns(u)] - high)
            total = total + jnp.sum(e.reshape(32, 8, UNIT), axis=0)
        settle(u, high, total)

    def mirror(s, a):
        return 2 * PLACE[ORDER[s // 2] ^ ORDER[a // 2]] + (s % 2 ^ a % 2)

    def stat_copy(r, a):
        return remote(
            lse_mine.at[r, a], lse_in.at[r, a], stat_send, stat_recv.at[r], slot_peer(a)
        )

    def part_copy(r, a):
        return remote(
            part_mine.at[r], part_in.at[r, a], part_send, part_recv.at[r], slot_peer(a)
        )

    def fin_copy(r, a):
        return remote(
            lse_mine.at[r, pl.ds(EARLY, 16 - EARLY)], fin_in.at[r, a],
            fin_send, fin_recv.at[r], slot_peer(a),
        )

    def count_copy(n):
        return remote(
            count_mine.at[n], count_in.at[n], count_send, count_recv, cent_peer(ORDER[n])
        )

    def settled(u):
        r, i = u // 8, u % 8
        if i in (3, 7):
            for a in range(0, EARLY) if i == 3 else range(EARLY, 16):
                n, k = ORDER[a // 2], a % 2
                units = [r * 8 + (1 + wave_of(j, n) if n else 0) for j in range(N_PIECES)]
                known = {v: lse_unit[v, k] for v in set(units)}
                lse_mine[r, a] = mosaic([known[v] for v in units])
        if i == 3:
            for a in range(1, EARLY):
                stat_copy(r, a).start()
        if i == 7:
            for a in range(1, 16):
                fin_copy(r, a).start()
            took(stat_recv.at[r], lse_in.at[r, pl.ds(1, EARLY - 1)])
            part_mine[r] = combine([lse_mine[r, 0]] + [lse_in[r, a] for a in range(1, EARLY)])
            for a in range(1, 16):
                part_copy(r, a).start()

    def agree(r):
        took(part_recv.at[r], part_in.at[r, pl.ds(1, 15)])
        took(fin_recv.at[r], fin_in.at[r, pl.ds(1, 15)])
        agreed = []
        for s in range(16):
            terms = [part_mine[r] if s == 0 else part_in[r, s]]
            for q in range(EARLY, 16):
                a = mirror(s, q)
                terms.append(lse_mine[r, q] if a == 0 else fin_in[r, a, q - EARLY])
            agreed.append(combine(terms))
        norm_out[r * PART : (r + 1) * PART] = (agreed[0] * LN2).reshape(PART)
        for i in range(8):
            masks = [mask_of(j, i - 1) if i else 0 for j in range(N_PIECES)]
            for k in range(2):
                at = (r * 8 + i) * UNIT + k * PART
                lse_all[:, at : at + PART] = mosaic([agreed[2 * PLACE[n] + k] for n in masks])

    def weigh(p, r):
        at = pl.ds(pl.multiple_of(p * CENTS, CENTS), CENTS)
        count = tally[p] if r else jnp.zeros((CENTS, 128), jnp.float32)
        total = sums[p] if r else jnp.zeros((CENTS, WIDTH), jnp.float32)
        for i in range(4):
            cols = slice((r * 4 + i) * 2 * UNIT, (r * 4 + i + 1) * 2 * UNIT)
            resp = jnp.exp2(scores[at, cols] - lse_all[:, cols]).astype(jnp.bfloat16)
            wide = resp.astype(jnp.float32)
            for q in range(2 * UNIT // 128):
                count = count + wide[:, q * 128 : (q + 1) * 128]
            total = total + lax.dot_general(
                resp, rows[cols, :], NN, preferred_element_type=jnp.float32
            )
        sums[p] = total
        if r:
            outbox[p] = total.astype(jnp.bfloat16)
            count_mine[p] = jnp.sum(count.T, axis=0, keepdims=True)
        else:
            tally[p] = count

    for w in range(3):
        row_start(0, w)
    own[2].wait()
    cents[0:CENTS, :] = book_in[...].astype(jnp.bfloat16)
    for w in range(3):
        cent_start(w)
    sib_copy(0, 0).start()
    sib_copy(1, 0).start()
    own[0].wait()
    own[1].wait()
    cent_arrive(0)
    cent_start(3)
    cent_start(4)
    row_arrive(0, 0)
    row_start(0, 3)
    row_start(0, 4)
    cent_arrive(1)
    cent_start(5)
    row_arrive(0, 1)
    row_start(0, 5)
    cent_arrive(2)
    squares(0)
    row_arrive(0, 2)

    first = (0, 8, 1, 2, 3, 4, 5, 6)

    def first_unit(i):
        return jnp.where(i == 0, 0, jnp.where(i == 1, 8, i - 1))

    def before_first(i):
        if i == 4:
            cent_arrive(3)
            cent_start(6)
            row_arrive(0, 3)
            row_start(0, 6)
            row_start(1, 0)
        if i == 5:
            row_arrive(0, 4)
            cent_arrive(4)
        if i == 6:
            row_arrive(0, 5)
            row_start(1, 1)
            row_start(1, 2)
            cent_arrive(5)
        if i == 7:
            row_arrive(0, 6)
        sib_arrive(first[i])

    @pl.loop(0, 8)
    def _(i):
        for v in range(8):
            pl.when(i == v)(functools.partial(before_first, v))
        score(first_unit(i), (0, 1), True)

    cent_arrive(6)
    squares(1)
    score(0, (2, 3), False)

    @pl.loop(1, 8)
    def _(i):
        @pl.when(i == 3)
        def _():
            row_arrive(1, 0)
            row_start(1, 3)
            row_start(1, 4)

        score(first_unit(i), (2, 3), False, first_unit(i - 1))
        pl.when(i == 5)(functools.partial(settled, 3))

    def before_full(i):
        if i == 1:
            row_arrive(1, 1)
            row_start(1, 5)
        if i == 2:
            row_arrive(1, 2)
        if i == 3:
            row_arrive(1, 3)
            row_start(1, 6)
        if i == 6:
            agree(0)
            weigh(7, 0)
        if i in (4, 5, 6):
            row_arrive(1, i)
        sib_arrive(i + 8 if i else 7)

    @pl.loop(0, 8)
    def _(i):
        for v in range(8):
            pl.when(i == v)(functools.partial(before_full, v))
        last = jnp.where(i == 0, 6, jnp.where(i == 1, 7, 7 + i))
        score(jnp.where(i == 0, 7, 8 + i), (0, 1, 2, 3), True, last)
        pl.when(i == 1)(functools.partial(settled, 7))
        pl.when(i == 4)(functools.partial(settled, 11))

    soften(15)
    settled(15)

    def step_of(n, j):
        return next(s for s in range(3) if n >> PIECES[j][2][s] & 1)

    def sum_copy(n, j):
        at = pl.ds(*PIECES[j][:2])
        s = step_of(n, j)
        d = PIECES[j][2][s]
        group = 0 if n == 7 else 1 + s if n in (3, 5, 6) else 3 + s // 2
        box = (inbox1, inbox2, inbox3)[s]
        dst = box.at[0 if s == 2 else PLACE[n ^ 1 << d], at]
        return remote(
            outbox.at[PLACE[n], at], dst, sum_send, sum_recv.at[group], cent_peer(1 << d)
        )

    def gathered(n, j):
        at = PLACE[n], slice(PIECES[j][0], PIECES[j][0] + PIECES[j][1])
        value = sums[at]
        for box in (inbox1, inbox2)[: step_of(n, j)]:
            value = value + box[at].astype(jnp.float32)
        return value

    def send_sums(n, step):
        for j in range(N_PIECES):
            if step_of(n, j) == step:
                if step:
                    off, size, _ = PIECES[j]
                    outbox[PLACE[n], off : off + size, :] = gathered(n, j).astype(jnp.bfloat16)
                sum_copy(n, j).start()

    def after(p):
        n = ORDER[p]
        if n:
            send_sums(n, 0)
            count_copy(p).start()
        if p == 4:
            took(sum_recv.at[0], inbox1.at[0])
            for m in (6, 5, 3):
                send_sums(m, 1)
        if p == 1:
            took(sum_recv.at[1], inbox1.at[pl.ds(0, 2)])
            for m in (4, 2, 1):
                send_sums(m, 1)

    @pl.loop(1, 5)
    def _(i):
        weigh(7 - i, 0)

    agree(1)

    @pl.loop(0, 8)
    def _(i):
        pl.when(i > 4)(lambda: weigh(7 - i, 0))
        weigh(7 - i, 1)
        for p in range(8):
            pl.when(i == 7 - p)(functools.partial(after, p))

    took(sum_recv.at[2], inbox2.at[0])
    for n in (4, 2, 1):
        send_sums(n, 2)

    took(row_send, rows.at[pl.ds(0, 14 * PART)])
    took(sib_send, rows.at[pl.ds(0, 16 * PART)])
    took(cent_send, cents.at[pl.ds(0, 7 * CENTS)])
    for r in range(2):
        took(stat_send, lse_in.at[r, pl.ds(1, EARLY - 1)])
        took(part_send, part_in.at[r, pl.ds(1, 15)])
        took(fin_send, fin_in.at[r, pl.ds(1, 15)])
    took(count_send, count_in.at[pl.ds(1, 7)])
    took(count_recv, count_in.at[pl.ds(1, 7)])
    count = functools.reduce(jnp.add, [count_mine[0]] + [count_in[n] for n in range(1, 8)])
    count_out[...] = count.reshape(CENTS)
    below = jnp.broadcast_to(count, (CENTS, 128)).T + PRIOR
    took(sum_recv.at[3], inbox1.at[pl.ds(0, 2)])
    share = 1.0 / below
    for q in range(WIDTH // 128):
        cols = slice(q * 128, (q + 1) * 128)
        near = sums[0, :, cols] + PRIOR * book_in[:, cols]
        for box in (inbox1, inbox2):
            near = near + box[0, :, cols].astype(jnp.float32)
        sums[0, :, cols] = near
    took(sum_recv.at[4], inbox3.at[0])
    for q in range(WIDTH // 128):
        cols = slice(q * 128, (q + 1) * 128)
        new_out[:, cols] = (sums[0, :, cols] + inbox3[0, :, cols].astype(jnp.float32)) * share
    took(sum_send, outbox.at[pl.ds(1, 7)])


def local(embeddings, codebook):
    f32, bf16 = jnp.float32, jnp.bfloat16
    vmem, dma = pltpu.VMEM, pltpu.SemaphoreType.DMA
    new, count, norm = pl.pallas_call(
        kernel,
        out_shape=(
            vmem((CENTS, WIDTH), f32),
            vmem((CENTS,), f32),
            vmem((ROWS,), f32),
        ),
        in_specs=[pl.BlockSpec(memory_space=pl.ANY)] * 2,
        out_specs=[pl.BlockSpec(memory_space=pltpu.VMEM)] * 3,
        scratch_shapes=[
            vmem((16 * UNIT, WIDTH), bf16),
            vmem((8 * CENTS, WIDTH), bf16),
            vmem((8 * CENTS, 16 * UNIT), f32),
            vmem((8 * CENTS, 128), f32),
            vmem((16, 8, UNIT), f32),
            vmem((8, CENTS, WIDTH), f32),
            vmem((8, CENTS, 128), f32),
            vmem((1, 16 * UNIT), f32),
            vmem((16, 2, 1, PART), f32),
            vmem((2, 16, 1, PART), f32),
            vmem((2, 16, 1, PART), f32),
            vmem((2, 1, PART), f32),
            vmem((2, 16, 1, PART), f32),
            vmem((2, 16, 16 - EARLY, 1, PART), f32),
            vmem((8, 1, CENTS), f32),
            vmem((8, 1, CENTS), f32),
            vmem((8, CENTS, WIDTH), bf16),
            vmem((8, CENTS, WIDTH), bf16),
            vmem((8, CENTS, WIDTH), bf16),
            vmem((1, CENTS, WIDTH), bf16),
            vmem((CENTS, WIDTH), f32),
            dma((3,)),
            dma(()), dma((2, 7)),
            dma(()), dma((2, 8)),
            dma(()), dma((7,)),
            dma(()), dma((2,)),
            dma(()), dma((2,)),
            dma(()), dma((2,)),
            dma(()), dma(()),
            dma(()), dma((5,)),
        ],
        compiler_params=pltpu.CompilerParams(
            collective_id=0, has_side_effects=True, vmem_limit_bytes=58 * 2**20
        ),
        cost_estimate=pl.CostEstimate(
            flops=4 * 4096 * 1024 * 1024, bytes_accessed=2**21, transcendentals=2**23
        ),
    )(embeddings, codebook)
    return new, count, norm


def solution(mesh):
    return jax.shard_map(
        local,
        mesh=mesh,
        in_specs=(P(("dp", "cent"), None), P(("cent", "dp"), None)),
        out_specs=(P(("cent", "dp"), None), P(("cent", "dp")), P(("dp", "cent"))),
        check_vma=False,
    )
```

```python
import functools
import math

import jax
import jax.numpy as jnp
from jax import lax
from jax.experimental import pallas as pl
from jax.experimental.pallas import tpu as pltpu
from jax.sharding import PartitionSpec as P

TEMPER = 0.8
PRIOR = 1.0
ALPHA = math.log2(math.e) / TEMPER
LN2 = math.log(2.0)
MESH = pl.DeviceIdType.MESH

ROWS, CENTS, WIDTH = 256, 128, 1024
PART, UNIT = 128, 256
PIECES = (
    (0, 16, (2, 1, 0)),
    (16, 32, (1, 2, 0)),
    (48, 16, (2, 0, 1)),
    (64, 32, (0, 2, 1)),
    (96, 16, (1, 0, 2)),
    (112, 16, (0, 1, 2)),
)
N_PIECES = len(PIECES)
ORDER = (0, 1, 2, 4, 3, 5, 6, 7)
PLACE = {mask: i for i, mask in enumerate(ORDER)}
EARLY = 8
NT = (((1,), (1,)), ((), ()))
NN = (((1,), (0,)), ((), ()))


def waves():
    wave = [[] for _ in range(7)]
    for j, (_, _, (a, b, c)) in enumerate(PIECES):
        sent = ((a, 0), (b, 0), (c, 0), (b, 1 << a), (c, 1 << a), (c, 1 << b), (c, 1 << a | 1 << b))
        for w, (d, m) in enumerate(sent):
            wave[w].append((d, j, m))
    return wave


def wave_of(j, mask):
    a, b, c = (1 << d for d in PIECES[j][2])
    return (a, b, c, a | b, a | c, b | c, 7).index(mask)


def mask_of(j, w):
    return next(mask for mask in range(1, 8) if wave_of(j, mask) == w)


def mosaic(rows):
    lane = lax.broadcasted_iota(jnp.int32, (1, PART), 1)
    whole = rows[-1]
    for (off, _, _), (end, _, _), row in list(zip(PIECES, PIECES[1:], rows))[::-1]:
        if row is not whole:
            whole = jnp.where((lane >= off) & (lane < end), row, whole)
    return whole


def combine(terms):
    top = functools.reduce(jnp.maximum, terms)
    total = functools.reduce(jnp.add, [jnp.exp2(t - top) for t in terms])
    return top + jnp.log2(total)


def kernel(
    emb, book, new_out, count_out, norm_out,
    rows, cents, scores, half_sq, peak, sums, tally, lse_all,
    lse_unit, lse_mine, lse_in, part_mine, part_in, fin_in, count_mine, count_in,
    outbox, inbox1, inbox2, inbox3,
    book_in, own_sem, row_send, row_recv, sib_send, sib_recv, cent_send, cent_recv,
    stat_send, stat_recv, part_send, part_recv, fin_send, fin_recv,
    count_send, count_recv, sum_send, sum_recv,
):
    dp, cent = lax.axis_index("dp"), lax.axis_index("cent")
    place = (cent // 4, cent % 4, dp // 2)
    core = dp % 2

    def device(p, c):
        return (p[2] * 2 + c, p[0] * 4 + p[1])

    def row_peer(mask, other=0):
        p = [v + 1 - 2 * (v % 2) if mask >> d & 1 else v for d, v in enumerate(place)]
        return device(p, 1 - core if other else core)

    def cent_peer(mask):
        return device([3 - v if mask >> d & 1 else v for d, v in enumerate(place)], core)

    def slot_peer(a):
        return row_peer(ORDER[a // 2], a % 2)

    def remote(src, dst, send, recv, to):
        return pltpu.make_async_remote_copy(
            src_ref=src, dst_ref=dst, send_sem=send, recv_sem=recv,
            device_id=to, device_id_type=MESH,
        )

    barrier = pltpu.get_barrier_semaphore()
    peers = [row_peer(0, 1)] + [row_peer(b) for b in (1, 2, 4)] + [cent_peer(b) for b in (1, 2, 4)]
    for peer in peers:
        pl.semaphore_signal(barrier, inc=1, device_id=peer, device_id_type=MESH)
    own = [
        pltpu.make_async_copy(
            emb.at[pl.ds(r * PART, PART)], rows.at[pl.ds(r * 8 * UNIT, PART)], own_sem.at[r]
        )
        for r in range(2)
    ]
    own.append(pltpu.make_async_copy(book, book_in, own_sem.at[2]))
    own[2].start()
    own[0].start()
    own[1].start()
    pl.semaphore_wait(barrier, len(peers))

    def row_at(r, n, j):
        return pl.ds((r * 8 + 1 + wave_of(j, n)) * UNIT + PIECES[j][0], PIECES[j][1])

    def cent_at(n, j):
        return pl.ds(PLACE[n] * CENTS + PIECES[j][0], PIECES[j][1])

    def row_copy(r, w, d, j, m):
        off, size, _ = PIECES[j]
        src = rows.at[row_at(r, m, j)] if m else emb.at[pl.ds(r * PART + off, size)]
        dst = rows.at[row_at(r, m | 1 << d, j)]
        return remote(src, dst, row_send, row_recv.at[r, w], row_peer(1 << d))

    def cent_copy(w, d, j, m):
        n = m | 1 << d
        src, dst = cents.at[cent_at(m, j)], cents.at[cent_at(n, j)]
        return remote(src, dst, cent_send, cent_recv.at[w], cent_peer(1 << d))

    def sib_copy(r, i):
        at = (r * 8 + i) * UNIT
        src = rows.at[pl.ds(at, PART)] if i else emb.at[pl.ds(r * PART, PART)]
        dst = rows.at[pl.ds(at + PART, PART)]
        return remote(src, dst, sib_send, sib_recv.at[r, i], row_peer(0, 1))

    wave = waves()

    def took(sem, *refs):
        for ref in refs:
            pltpu.make_async_copy(ref, ref, sem).wait()

    def row_start(r, w):
        for msg in wave[w]:
            row_copy(r, w, *msg).start()

    def cent_start(w):
        for msg in wave[w]:
            cent_copy(w, *msg).start()

    def row_arrive(r, w):
        took(row_recv.at[r, w], rows.at[pl.ds(0, PART)])
        sib_copy(r, 1 + w).start()

    def cent_arrive(w):
        took(cent_recv.at[w], cents.at[pl.ds(0, CENTS)])

    def sib_arrive(u):
        took(sib_recv.at[u // 8, u % 8], rows.at[pl.ds(0, PART)])

    def squares(lo, hi):
        @pl.loop(lo, hi)
        def _(i):
            at = pl.ds(pl.multiple_of(i * CENTS, CENTS), CENTS)
            c = cents[at, :].astype(jnp.float32)
            total = jnp.sum(c * c, axis=1, keepdims=True) * (0.5 * ALPHA)
            half_sq[at, :] = jnp.broadcast_to(total, (CENTS, 128))

    def columns(u):
        return pl.ds(pl.multiple_of(u * UNIT, UNIT), UNIT)

    def score(u, blocks, fresh, last=None):
        cols = columns(u)
        top = jnp.full((8, UNIT), -jnp.inf, jnp.float32) if fresh else peak[u]
        if last is not None:
            summed = columns(last)
            high = jnp.max(peak[last], axis=0, keepdims=True)
            total = jnp.zeros((8, UNIT), jnp.float32)
        for i in blocks:
            at = slice(i * 256, (i + 1) * 256)
            product = lax.dot_general(
                cents[at, :], rows[cols, :], NT, preferred_element_type=jnp.float32
            )
            if last is not None:
                step = 1024 // len(blocks)
                first = (i - blocks[0]) * step
                e = jnp.exp2(scores[first : first + step, summed] - high)
                total = total + jnp.sum(e.reshape(step // 8, 8, UNIT), axis=0)
            h = half_sq[at, :]
            t = product * ALPHA - jnp.concatenate([h] * (UNIT // 128), axis=1)
            scores[at, cols] = t
            top = jnp.maximum(top, jnp.max(t.reshape(32, 8, UNIT), axis=0))
        peak[u] = top
        if last is not None:
            settle(last, high, total)

    def settle(u, high, total):
        lse = high + jnp.log2(jnp.sum(total, axis=0, keepdims=True))
        lse_unit[u, 0] = lse[:, :PART]
        lse_unit[u, 1] = lse[:, PART:]

    def soften(u):
        high = jnp.max(peak[u], axis=0, keepdims=True)
        total = jnp.zeros((8, UNIT), jnp.float32)
        for i in range(4):
            e = jnp.exp2(scores[i * 256 : (i + 1) * 256, columns(u)] - high)
            total = total + jnp.sum(e.reshape(32, 8, UNIT), axis=0)
        settle(u, high, total)

    def mirror(s, a):
        return 2 * PLACE[ORDER[s // 2] ^ ORDER[a // 2]] + (s % 2 ^ a % 2)

    def stat_copy(r, a):
        return remote(
            lse_mine.at[r, a], lse_in.at[r, a], stat_send, stat_recv.at[r], slot_peer(a)
        )

    def part_copy(r, a):
        return remote(
            part_mine.at[r], part_in.at[r, a], part_send, part_recv.at[r], slot_peer(a)
        )

    def fin_copy(r, a):
        return remote(
            lse_mine.at[r, pl.ds(EARLY, 16 - EARLY)], fin_in.at[r, a],
            fin_send, fin_recv.at[r], slot_peer(a),
        )

    def count_copy(n):
        return remote(
            count_mine.at[n], count_in.at[n], count_send, count_recv, cent_peer(ORDER[n])
        )

    def settled(u):
        r, i = u // 8, u % 8
        if i in (3, 7):
            for a in range(0, EARLY) if i == 3 else range(EARLY, 16):
                n, k = ORDER[a // 2], a % 2
                units = [r * 8 + (1 + wave_of(j, n) if n else 0) for j in range(N_PIECES)]
                known = {v: lse_unit[v, k] for v in set(units)}
                lse_mine[r, a] = mosaic([known[v] for v in units])
        if i == 3:
            for a in range(1, EARLY):
                stat_copy(r, a).start()
        if i == 7:
            for a in range(1, 16):
                fin_copy(r, a).start()
            took(stat_recv.at[r], lse_in.at[r, pl.ds(1, EARLY - 1)])
            part_mine[r] = combine([lse_mine[r, 0]] + [lse_in[r, a] for a in range(1, EARLY)])
            for a in range(1, 16):
                part_copy(r, a).start()

    def agree(r):
        took(part_recv.at[r], part_in.at[r, pl.ds(1, 15)])
        took(fin_recv.at[r], fin_in.at[r, pl.ds(1, 15)])
        agreed = []
        for s in range(16):
            terms = [part_mine[r] if s == 0 else part_in[r, s]]
            for q in range(EARLY, 16):
                a = mirror(s, q)
                terms.append(lse_mine[r, q] if a == 0 else fin_in[r, a, q - EARLY])
            agreed.append(combine(terms))
        norm_out[r * PART : (r + 1) * PART] = (agreed[0] * LN2).reshape(PART)
        for i in range(8):
            masks = [mask_of(j, i - 1) if i else 0 for j in range(N_PIECES)]
            for k in range(2):
                at = (r * 8 + i) * UNIT + k * PART
                lse_all[:, at : at + PART] = mosaic([agreed[2 * PLACE[n] + k] for n in masks])

    def weigh(p, r):
        at = pl.ds(pl.multiple_of(p * CENTS, CENTS), CENTS)
        count = tally[p] if r else jnp.zeros((CENTS, 128), jnp.float32)
        total = sums[p] if r else jnp.zeros((CENTS, WIDTH), jnp.float32)
        for i in range(4):
            cols = slice((r * 4 + i) * 2 * UNIT, (r * 4 + i + 1) * 2 * UNIT)
            resp = jnp.exp2(scores[at, cols] - lse_all[:, cols]).astype(jnp.bfloat16)
            wide = resp.astype(jnp.float32)
            for q in range(2 * UNIT // 128):
                count = count + wide[:, q * 128 : (q + 1) * 128]
            total = total + lax.dot_general(
                resp, rows[cols, :], NN, preferred_element_type=jnp.float32
            )
        sums[p] = total
        if r:
            outbox[p] = total.astype(jnp.bfloat16)
            count_mine[p] = jnp.sum(count.T, axis=0, keepdims=True)
        else:
            tally[p] = count

    for w in range(3):
        row_start(0, w)
    own[2].wait()
    cents[0:CENTS, :] = book_in[...].astype(jnp.bfloat16)
    for w in range(3):
        cent_start(w)
    sib_copy(0, 0).start()
    sib_copy(1, 0).start()
    own[0].wait()
    own[1].wait()
    squares(0, 1)
    cent_arrive(0)
    cent_start(3)
    cent_start(4)
    row_arrive(0, 0)
    row_start(0, 3)
    row_start(0, 4)
    cent_arrive(1)
    cent_start(5)
    row_arrive(0, 1)
    row_start(0, 5)
    cent_arrive(2)
    squares(1, 4)
    row_arrive(0, 2)

    first = (0, 8, 1, 2, 3, 4, 5, 6)

    def first_unit(i):
        return jnp.where(i == 0, 0, jnp.where(i == 1, 8, i - 1))

    def before_first(i):
        if i == 4:
            cent_arrive(3)
            cent_start(6)
            row_arrive(0, 3)
            row_start(0, 6)
            row_start(1, 0)
        if i == 5:
            row_arrive(0, 4)
            cent_arrive(4)
        if i == 6:
            row_arrive(0, 5)
            row_start(1, 1)
            row_start(1, 2)
            cent_arrive(5)
        if i == 7:
            squares(4, 7)
            row_arrive(0, 6)
        sib_arrive(first[i])

    @pl.loop(0, 8)
    def _(i):
        for v in range(8):
            pl.when(i == v)(functools.partial(before_first, v))
        score(first_unit(i), (0, 1), True)

    cent_arrive(6)
    squares(7, 8)
    score(0, (2, 3), False)

    @pl.loop(1, 8)
    def _(i):
        @pl.when(i == 3)
        def _():
            row_arrive(1, 0)
            row_start(1, 3)
            row_start(1, 4)

        score(first_unit(i), (2, 3), False, first_unit(i - 1))
        pl.when(i == 5)(functools.partial(settled, 3))

    def before_full(i):
        if i == 1:
            row_arrive(1, 1)
            row_start(1, 5)
        if i == 2:
            row_arrive(1, 2)
        if i == 3:
            row_arrive(1, 3)
            row_start(1, 6)
        if i == 6:
            agree(0)
            weigh(7, 0)
        if i in (4, 5, 6):
            row_arrive(1, i)
        sib_arrive(i + 8 if i else 7)

    @pl.loop(0, 8)
    def _(i):
        for v in range(8):
            pl.when(i == v)(functools.partial(before_full, v))
        last = jnp.where(i == 0, 6, jnp.where(i == 1, 7, 7 + i))
        score(jnp.where(i == 0, 7, 8 + i), (0, 1, 2, 3), True, last)
        pl.when(i == 1)(functools.partial(settled, 7))
        pl.when(i == 4)(functools.partial(settled, 11))

    soften(15)
    settled(15)

    def step_of(n, j):
        return next(s for s in range(3) if n >> PIECES[j][2][s] & 1)

    def sum_copy(n, j):
        at = pl.ds(*PIECES[j][:2])
        s = step_of(n, j)
        d = PIECES[j][2][s]
        group = 0 if n == 7 else 1 + s if n in (3, 5, 6) else 3 + s // 2
        box = (inbox1, inbox2, inbox3)[s]
        dst = box.at[0 if s == 2 else PLACE[n ^ 1 << d], at]
        return remote(
            outbox.at[PLACE[n], at], dst, sum_send, sum_recv.at[group], cent_peer(1 << d)
        )

    def gathered(n, j):
        at = PLACE[n], slice(PIECES[j][0], PIECES[j][0] + PIECES[j][1])
        value = sums[at]
        for box in (inbox1, inbox2)[: step_of(n, j)]:
            value = value + box[at].astype(jnp.float32)
        return value

    def send_sums(n, step):
        for j in range(N_PIECES):
            if step_of(n, j) == step:
                if step:
                    off, size, _ = PIECES[j]
                    outbox[PLACE[n], off : off + size, :] = gathered(n, j).astype(jnp.bfloat16)
                sum_copy(n, j).start()

    def after(p):
        n = ORDER[p]
        if n:
            send_sums(n, 0)
            count_copy(p).start()
        if p == 4:
            took(sum_recv.at[0], inbox1.at[0])
            for m in (6, 5, 3):
                send_sums(m, 1)
        if p == 1:
            took(sum_recv.at[1], inbox1.at[pl.ds(0, 2)])
            for m in (4, 2, 1):
                send_sums(m, 1)

    @pl.loop(1, 5)
    def _(i):
        weigh(7 - i, 0)

    agree(1)

    @pl.loop(0, 8)
    def _(i):
        pl.when(i > 4)(lambda: weigh(7 - i, 0))
        weigh(7 - i, 1)
        for p in range(8):
            pl.when(i == 7 - p)(functools.partial(after, p))

    took(sum_recv.at[2], inbox2.at[0])
    for n in (4, 2, 1):
        send_sums(n, 2)

    took(row_send, rows.at[pl.ds(0, 14 * PART)])
    took(sib_send, rows.at[pl.ds(0, 16 * PART)])
    took(cent_send, cents.at[pl.ds(0, 7 * CENTS)])
    for r in range(2):
        took(stat_send, lse_in.at[r, pl.ds(1, EARLY - 1)])
        took(part_send, part_in.at[r, pl.ds(1, 15)])
        took(fin_send, fin_in.at[r, pl.ds(1, 15)])
    took(count_send, count_in.at[pl.ds(1, 7)])
    took(count_recv, count_in.at[pl.ds(1, 7)])
    count = functools.reduce(jnp.add, [count_mine[0]] + [count_in[n] for n in range(1, 8)])
    count_out[...] = count.reshape(CENTS)
    below = jnp.broadcast_to(count, (CENTS, 128)).T + PRIOR
    took(sum_recv.at[3], inbox1.at[pl.ds(0, 2)])
    share = 1.0 / below
    for q in range(WIDTH // 128):
        cols = slice(q * 128, (q + 1) * 128)
        near = sums[0, :, cols] + PRIOR * book_in[:, cols]
        for box in (inbox1, inbox2):
            near = near + box[0, :, cols].astype(jnp.float32)
        sums[0, :, cols] = near
    took(sum_recv.at[4], inbox3.at[0])
    for q in range(WIDTH // 128):
        cols = slice(q * 128, (q + 1) * 128)
        new_out[:, cols] = (sums[0, :, cols] + inbox3[0, :, cols].astype(jnp.float32)) * share
    took(sum_send, outbox.at[pl.ds(1, 7)])


def local(embeddings, codebook):
    f32, bf16 = jnp.float32, jnp.bfloat16
    vmem, dma = pltpu.VMEM, pltpu.SemaphoreType.DMA
    new, count, norm = pl.pallas_call(
        kernel,
        out_shape=(
            vmem((CENTS, WIDTH), f32),
            vmem((CENTS,), f32),
            vmem((ROWS,), f32),
        ),
        in_specs=[pl.BlockSpec(memory_space=pl.ANY)] * 2,
        out_specs=[pl.BlockSpec(memory_space=pltpu.VMEM)] * 3,
        scratch_shapes=[
            vmem((16 * UNIT, WIDTH), bf16),
            vmem((8 * CENTS, WIDTH), bf16),
            vmem((8 * CENTS, 16 * UNIT), f32),
            vmem((8 * CENTS, 128), f32),
            vmem((16, 8, UNIT), f32),
            vmem((8, CENTS, WIDTH), f32),
            vmem((8, CENTS, 128), f32),
            vmem((1, 16 * UNIT), f32),
            vmem((16, 2, 1, PART), f32),
            vmem((2, 16, 1, PART), f32),
            vmem((2, 16, 1, PART), f32),
            vmem((2, 1, PART), f32),
            vmem((2, 16, 1, PART), f32),
            vmem((2, 16, 16 - EARLY, 1, PART), f32),
            vmem((8, 1, CENTS), f32),
            vmem((8, 1, CENTS), f32),
            vmem((8, CENTS, WIDTH), bf16),
            vmem((8, CENTS, WIDTH), bf16),
            vmem((8, CENTS, WIDTH), bf16),
            vmem((1, CENTS, WIDTH), bf16),
            vmem((CENTS, WIDTH), f32),
            dma((3,)),
            dma(()), dma((2, 7)),
            dma(()), dma((2, 8)),
            dma(()), dma((7,)),
            dma(()), dma((2,)),
            dma(()), dma((2,)),
            dma(()), dma((2,)),
            dma(()), dma(()),
            dma(()), dma((5,)),
        ],
        compiler_params=pltpu.CompilerParams(
            collective_id=0, has_side_effects=True, vmem_limit_bytes=58 * 2**20
        ),
        cost_estimate=pl.CostEstimate(
            flops=4 * 4096 * 1024 * 1024, bytes_accessed=2**21, transcendentals=2**23
        ),
    )(embeddings, codebook)
    return new, count, norm


def solution(mesh):
    return jax.shard_map(
        local,
        mesh=mesh,
        in_specs=(P(("dp", "cent"), None), P(("cent", "dp"), None)),
        out_specs=(P(("cent", "dp"), None), P(("cent", "dp")), P(("dp", "cent"))),
        check_vma=False,
    )
```
